32 devices in a mesh: dp: 8 (over z, y), seq: 4 (over x, core).
Axes of the slice: x: 2, y: 2, z: 4, core: 2. Of those that a mesh axis runs over, the one named last changes fastest.
Arguments:
- inputs: bfloat16 [16, 2048, 512], P('dp', 'seq'), may hold values from -6 to 6
- segment_ids: int32 [16, 2048], P('dp'), may hold values from 0 to 3, never falling along the last dimension, each value on 1 to 1024 neighbouring positions
- out_grad: bfloat16 [16, 2048, 512], P('dp', 'seq'), may hold values from -6 to 6
- w_qkv: float32 [3, 512, 512], P(None, 'dp'), may hold values from -0.25 to 0.25
- w_out: float32 [512, 512], P('dp'), may hold values from -1.5 to 1.5
- w_up: float32 [512, 2048], P('dp'), may hold values from -0.25 to 0.25
- w_down: float32 [2048, 512], P('dp'), may hold values from -0.125 to 0.125
- norm_params: float32 [4, 512], P(None, 'dp'), may hold values from -0.4 to 2.34, as said below
- qkv_first: float32 [3, 512, 512], P(None, 'dp'), may hold values from -0.00036621094 to 0.00036621094
- qkv_second: float32 [3, 512, 512], P(None, 'dp'), may hold values from 1.588423e-10 to 2.5414768e-09
- out_first: float32 [512, 512], P('dp'), may hold values from -0.00036621094 to 0.00036621094
- out_second: float32 [512, 512], P('dp'), may hold values from 9.530539e-12 to 1.588423e-10
- up_first: float32 [512, 2048], P('dp'), may hold values from -0.00036621094 to 0.00036621094
- up_second: float32 [512, 2048], P('dp'), may hold values from 1.588423e-10 to 2.5414768e-09
- down_first: float32 [2048, 512], P('dp'), may hold values from -0.00036621094 to 0.00036621094
- down_second: float32 [2048, 512], P('dp'), may hold values from 1.588423e-10 to 2.5414768e-09
- norm_first: float32 [4, 512], P(None, 'dp'), may hold values from -0.00036621094 to 0.00036621094
- norm_second: float32 [4, 512], P(None, 'dp'), may hold values from 1.588423e-10 to 2.5414768e-09
Outputs:
- outputs: bfloat16 [16, 2048, 512], P('dp', 'seq')
- input_grad: float32 [16, 2048, 512], P('dp', 'seq')
- grad_norm: float32 [], replicated
- qkv_weight: float32 [3, 512, 512], P(None, 'dp')
- out_weight: float32 [512, 512], P('dp')
- up_weight: float32 [512, 2048], P('dp')
- down_weight: float32 [2048, 512], P('dp')
- norm_grad: float32 [4, 512], P(None, 'dp')
- qkv_mean: float32 [3, 512, 512], P(None, 'dp')
- out_mean: float32 [512, 512], P('dp')
- up_mean: float32 [512, 2048], P('dp')
- down_mean: float32 [2048, 512], P('dp')
- norm_mean: float32 [4, 512], P(None, 'dp')
- qkv_square: float32 [3, 512, 512], P(None, 'dp')
- out_square: float32 [512, 512], P('dp')
- up_square: float32 [512, 2048], P('dp')
- down_square: float32 [2048, 512], P('dp')
- norm_square: float32 [4, 512], P(None, 'dp')
The draws below stay inside these ranges and needn't reach their ends.
Inputs may be any that keep to these rules, and one draw needn't show every extreme that they name: `segment_ids`: ids never fall along a row; each document has at most 1024 tokens. `norm_params`: rows 0 and 2 hold the two norms' gains, rows 1 and 3 their biases.
All inputs are finite; a program needn't handle non-finite values.
Results may differ from the reference program's by a relative error of at most 0.012.
The reference program's roundings to bfloat16 on the way count: a program that leaves them out, or rounds other values in their place, can miss the bound.
Values may be sent and summed in bfloat16 or wider, within the bound.
A program may use at most 320 MiB of HBM per device.

```python
import math
import jax
import jax.numpy as jnp
import numpy as np
from jax import lax

D = 512
HEADS = 8
DH = 64
FF = 2048
SEQ_LEN = 2048
LEVELS = 7
ROWS = 16
NPARAM = 3147776


def draw_norm_params(key, part):
    first_key, second_key = jax.random.split(jax.random.fold_in(key, 7))
    ramp = 0.6 + 1.2 * jnp.arange(D, dtype=jnp.float32) / (D - 1)
    factor = jax.random.uniform(first_key, (2, D), jnp.float32, 0.85, 1.15)
    shift = jax.random.uniform(second_key, (2, D), jnp.float32, -0.3, 0.3)
    gains = ramp[None, :] * factor
    return jnp.stack([gains[0], shift[0], gains[1], shift[1]]).astype(jnp.float32)


def levels(own_key, shape, cuts, smallest, high):
    def one(dim, shards_of):
        steps = jax.random.uniform(jax.random.fold_in(jax.random.fold_in(own_key, 6), dim), (shards_of,), jnp.float32, smallest / len(cuts), high / len(cuts))
        return jnp.repeat(jnp.exp(steps), shape[dim] // shards_of).reshape((-1,) + (1,) * (len(shape) - dim - 1))

    level = one(*cuts[0])
    for cut in cuts[1:]:
        level = level * one(*cut)
    return level


def split_up(count, total, reach, lean):
    weights = [(1 << 20) // math.isqrt(rank ** lean) + 1 for rank in range(2, count + 1)]
    surplus, given = total - reach - (count - 1), [1] * (count - 1)
    while surplus > 0:
        free = [i for i in range(count - 1) if given[i] < reach]
        pool, left = sum([weights[i] for i in free]), surplus
        for i in free:
            addition = min(reach - given[i], max(1, left * weights[i] // pool), surplus)
            given[i] = given[i] + addition
            surplus = surplus - addition
    return np.array([reach] + given)


def uneven(stream_key, amount, total, most, slope):
    if amount == 2:
        one = jax.random.randint(stream_key, (), max(1, total - most), min(most, total - 1) + 1)
        return jnp.stack([one, total - one])
    tallies = jnp.asarray(split_up(amount, total, most, slope), jnp.int32)
    twos = (amount - 1) // 2
    source_of, sink = tallies[1:1 + 2 * twos:2], tallies[2:2 + 2 * twos:2]
    margin = jnp.minimum(source_of - 1, most - sink)
    moved = jax.random.randint(jax.random.fold_in(stream_key, 1), (twos,), 0, 1 << 20) % (margin + 1)
    tallies = tallies.at[1:1 + 2 * twos:2].set(source_of - moved).at[2:2 + 2 * twos:2].set(sink + moved)
    return tallies[jax.random.permutation(jax.random.fold_in(stream_key, 2), amount)]


def centred(own_key, extent, deviation, limit, pieces=(), held_as=jnp.bfloat16):
    entries = deviation * jax.random.normal(own_key, extent, jnp.float32)
    if pieces:
        entries = entries * levels(own_key, extent, pieces, -0.22, 0.18)
    return jnp.clip(entries, -limit, limit).astype(held_as)


def setup_inputs(seed: int = 0) -> dict:
    streams_of = jax.random.split(jax.random.key(seed), 19)
    return {
        "inputs": centred(streams_of[0], (ROWS, SEQ_LEN, D), 1.0, 6.0, ((0, 8), (1, 4))),
        "segment_ids": jax.vmap(lambda own: jnp.searchsorted(jnp.cumsum(uneven(own, 4, SEQ_LEN, SEQ_LEN // 2, 0)), jnp.arange(SEQ_LEN), side="right"))(jax.random.split(streams_of[1], ROWS)).reshape((ROWS, SEQ_LEN)).astype(jnp.int32),
        "out_grad": centred(streams_of[2], (ROWS, SEQ_LEN, D), 1.0, 6.0, ((0, 8), (1, 4))),
        "w_qkv": centred(streams_of[3], (3, D, D), D ** -0.5, 0.25, ((1, 8),), jnp.float32),
        "w_out": centred(streams_of[4], (D, D), (D // 32) ** -0.5, 1.5, ((0, 8),), jnp.float32),
        "w_up": centred(streams_of[5], (D, FF), D ** -0.5, 0.25, ((0, 8),), jnp.float32),
        "w_down": centred(streams_of[6], (FF, D), FF ** -0.5, 0.125, ((0, 8),), jnp.float32),
        "norm_params": draw_norm_params(jax.random.fold_in(streams_of[18], 71), 0),
        "qkv_first": centred(streams_of[8], (3, D, D), (81 * NPARAM) ** -0.5, 0.00036621094, ((1, 8),), jnp.float32),
        "qkv_second": jnp.clip(jnp.exp(math.log(2.541476806783294e-09) - 2.7725887 * jax.random.uniform(streams_of[9], (3, D, D), jnp.float32) ** levels(streams_of[9], (3, D, D), ((1, 8),), -0.2, 0.2)), 1.5884230042395586e-10, 2.541476806783294e-09),
        "out_first": centred(streams_of[10], (D, D), (81 * NPARAM) ** -0.5, 0.00036621094, ((0, 8),), jnp.float32),
        "out_second": jnp.clip(jnp.exp(math.log(1.5884230042395586e-10) - 2.81341065 * jax.random.uniform(streams_of[11], (D, D), jnp.float32) ** levels(streams_of[11], (D, D), ((0, 8),), -0.2, 0.2)), 9.530538684632273e-12, 1.5884230042395586e-10),
        "up_first": centred(streams_of[12], (D, FF), (81 * NPARAM) ** -0.5, 0.00036621094, ((0, 8),), jnp.float32),
        "up_second": jnp.clip(jnp.exp(math.log(2.541476806783294e-09) - 2.7725887 * jax.random.uniform(streams_of[13], (D, FF), jnp.float32) ** levels(streams_of[13], (D, FF), ((0, 8),), -0.2, 0.2)), 1.5884230042395586e-10, 2.541476806783294e-09),
        "down_first": centred(streams_of[14], (FF, D), (81 * NPARAM) ** -0.5, 0.00036621094, ((0, 8),), jnp.float32),
        "down_second": jnp.clip(jnp.exp(math.log(2.541476806783294e-09) - 2.7725887 * jax.random.uniform(streams_of[15], (FF, D), jnp.float32) ** levels(streams_of[15], (FF, D), ((0, 8),), -0.2, 0.2)), 1.5884230042395586e-10, 2.541476806783294e-09),
        "norm_first": centred(streams_of[16], (4, D), (81 * NPARAM) ** -0.5, 0.00036621094, ((1, 8),), jnp.float32),
        "norm_second": jnp.clip(jnp.exp(math.log(2.541476806783294e-09) - 2.7725887 * jax.random.uniform(streams_of[17], (4, D), jnp.float32) ** levels(streams_of[17], (4, D), ((1, 8),), -0.2, 0.2)), 1.5884230042395586e-10, 2.541476806783294e-09),
    }


@jax.custom_vjp
def low(v):
    return lax.optimization_barrier(v.astype(jnp.bfloat16)).astype(jnp.float32)

@jax.custom_vjp
def low_back(v):
    return v

def low_keep(v):
    return (low(v), None)

def low_pass(kept, grad):
    return (grad,)

def back_keep(v):
    return (v, None)

def back_low(kept, grad):
    return (low(grad),)
low.defvjp(low_keep, low_pass)
low_back.defvjp(back_keep, back_low)
masked_score = -1e+30
highest = lax.Precision.HIGHEST
beta_one = 0.9
beta_two = 0.999
bias_first = 1.0 - 0.9 ** 10
bias_second = 1.0 - 0.999 ** 10
learn_rate = 0.1
weight_decay = 0.1
epsilon = 1e-08
clip_norm = 1.0

def layer_norm(values, gain, shift):
    center = lax.optimization_barrier(jnp.mean(values, axis=-1, keepdims=True))
    centered = values - center
    spread = lax.optimization_barrier(jnp.mean(centered * centered, axis=-1, keepdims=True))
    return centered * lax.rsqrt(spread + 1e-05) * gain + shift

def gelu_tanh(values):
    return 0.5 * values * (1.0 + jnp.tanh(0.7978845608 * (values + 0.044715 * values * values * values)))

def windows(coarse, offset, blocks):
    window = lax.dynamic_slice_in_dim(coarse, jnp.asarray(offset).astype(jnp.int32), (blocks + 2) * 16, coarse.ndim - 2)
    window = window.reshape(window.shape[:-2] + (blocks + 2, 16, window.shape[-1]))
    return jnp.concatenate([window[..., 0:blocks, :, :], window[..., 1:blocks + 1, :, :], window[..., 2:blocks + 2, :, :]], axis=-2)

def segment_ends(segments, group_size):
    seg_first = jnp.pad(segments[:, ::group_size], ((0, 0), (16, 16)), constant_values=-1)
    seg_last = jnp.pad(segments[:, group_size - 1::group_size], ((0, 0), (16, 16)), constant_values=-1)
    return (seg_first, seg_last)

def level_mask(seg_first, seg_last, level_index, query_pos, key_index, query_seg):
    key_first = jnp.take(seg_first, key_index + 16, axis=1)
    key_last = jnp.take(seg_last, key_index + 16, axis=1)
    allowed = (key_first[:, :, None, :] == query_seg[..., None]) & (key_last[:, :, None, :] == query_seg[..., None])
    if level_index > 0:
        parent = query_pos // (8 * 2 ** level_index)
        inner = (key_index[:, None, :] >= ((parent - 1) * 8)[..., None]) & (key_index[:, None, :] < ((parent + 2) * 8)[..., None])
        allowed = allowed & jnp.logical_not(inner)[None]
    return allowed

def moment_update(clipped, first, second):
    mean_new = beta_one * first + (1.0 - beta_one) * clipped
    square_new = beta_two * second + (1.0 - beta_two) * clipped * clipped
    return (mean_new, square_new)

def adam_update(weight, grad, first, second, factor):
    mean_new, square_new = moment_update(grad * factor, first, second)
    update = mean_new / bias_first / (jnp.sqrt(square_new / bias_second) + epsilon) + weight_decay * weight
    return (weight - learn_rate * update, mean_new, square_new)

def row_forward(tokens, segments, qkv_low, out_low, up_low, down_low, norm_low):
    normed = low(layer_norm(tokens, norm_low[0], norm_low[1]))
    projected = low(low_back(jnp.einsum('rtd,cde->crte', normed, qkv_low, precision=highest)))
    queries = projected[0].reshape(1, SEQ_LEN, HEADS, DH)
    score_scale = DH ** (-0.5)
    score_list = []
    value_list = []
    shapes = []
    for level_index in range(LEVELS):
        group_size = 2 ** level_index
        block_span = 16 * group_size
        blocks = SEQ_LEN // block_span
        if level_index == 0:
            keys_coarse = projected[1]
            values_coarse = projected[2]
        else:
            keys_coarse = low(lax.optimization_barrier(jnp.mean(projected[1].reshape(1, SEQ_LEN // group_size, group_size, D), axis=2)))
            values_coarse = low(lax.optimization_barrier(jnp.mean(projected[2].reshape(1, SEQ_LEN // group_size, group_size, D), axis=2)))
        padding = ((0, 0), (16, 16), (0, 0))
        key_window = windows(jnp.pad(keys_coarse, padding), 0, blocks).reshape(1, blocks, 48, HEADS, DH)
        value_window = windows(jnp.pad(values_coarse, padding), 0, blocks).reshape(1, blocks, 48, HEADS, DH)
        grouped = queries.reshape(1, blocks, block_span, HEADS, DH)
        raw = jnp.einsum('rbqhd,rbkhd->rbqhk', grouped, key_window, precision=highest)
        raw = low_back(raw * score_scale + level_index * math.log(2.0))
        query_pos = jnp.arange(SEQ_LEN, dtype=jnp.int32).reshape(blocks, block_span)
        key_index = (jnp.arange(blocks, dtype=jnp.int32)[:, None] - 1) * 16 + jnp.arange(48, dtype=jnp.int32)[None, :]
        seg_first, seg_last = segment_ends(segments, group_size)
        allowed = level_mask(seg_first, seg_last, level_index, query_pos, key_index, segments.reshape(1, blocks, block_span))
        scores = jnp.where(allowed[:, :, :, None, :], raw, masked_score)
        score_list.append(scores.reshape(1, SEQ_LEN, HEADS, 48))
        value_list.append(value_window)
        shapes.append((blocks, block_span))
    scores = jnp.concatenate(score_list, axis=-1)
    highest_score = lax.optimization_barrier(jnp.max(scores, axis=-1, keepdims=True))
    log_total = highest_score + jnp.log(lax.optimization_barrier(jnp.sum(jnp.exp(scores - highest_score), axis=-1, keepdims=True)))
    attention_weights = low(jnp.exp(scores - log_total))
    mixed = jnp.zeros((1, SEQ_LEN, HEADS, DH), jnp.float32)
    for level_index in range(LEVELS):
        blocks, block_span = shapes[level_index]
        piece = attention_weights[..., 48 * level_index:48 * (level_index + 1)].reshape(1, blocks, block_span, HEADS, 48)
        mixed = mixed + jnp.einsum('rbqhk,rbkhd->rbqhd', piece, value_list[level_index], precision=highest).reshape(1, SEQ_LEN, HEADS, DH)
    mixed = low(low_back(mixed.reshape(1, SEQ_LEN, D)))
    residual = tokens + low_back(jnp.einsum('rtd,de->rte', mixed, out_low, precision=highest))
    second = low(layer_norm(residual, norm_low[2], norm_low[3]))
    hidden_pre = low_back(jnp.einsum('rtd,df->rtf', second, up_low, precision=highest))
    hidden = low(gelu_tanh(hidden_pre))
    return residual + jnp.einsum('rtf,fd->rtd', hidden, down_low, precision=highest)

def reference(inputs, segment_ids, out_grad, w_qkv, w_out, w_up, w_down, norm_params, qkv_first, qkv_second, out_first, out_second, up_first, up_second, down_first, down_second, norm_first, norm_second):

    def forward(params, tokens):
        lowered = [low(item) for item in params]

        def one_row(carry, row_pair):
            row_tokens, row_segments = row_pair
            result = row_forward(row_tokens[None], row_segments[None], lowered[0], lowered[1], lowered[2], lowered[3], lowered[4])
            return (carry, result[0])
        _, result = lax.scan(jax.checkpoint(one_row), jnp.zeros((), jnp.float32), (tokens, segment_ids))
        return result
    params = (w_qkv, w_out, w_up, w_down, norm_params)
    produced, pullback = jax.vjp(forward, params, inputs.astype(jnp.float32))
    grads, input_grad = pullback(out_grad.astype(jnp.float32))
    squares = [jnp.sum(item * item) for item in grads]
    grad_norm = jnp.sqrt(squares[0] + squares[1] + squares[2] + squares[3] + squares[4])
    factor = jnp.minimum(1.0, clip_norm / grad_norm)
    firsts = (qkv_first, out_first, up_first, down_first)
    seconds = (qkv_second, out_second, up_second, down_second)
    updated = [adam_update(params[which], grads[which], firsts[which], seconds[which], factor) for which in range(4)]
    norm_grad = grads[4] * factor
    norm_mean, norm_square = moment_update(norm_grad, norm_first, norm_second)
    return (produced.astype(jnp.bfloat16), input_grad, grad_norm, updated[0][0], updated[1][0], updated[2][0], updated[3][0], norm_grad, updated[0][1], updated[1][1], updated[2][1], updated[3][1], norm_mean, updated[0][2], updated[1][2], updated[2][2], updated[3][2], norm_square)
```

```python
import functools
import math

import jax
import jax.numpy as jnp
from jax import lax
from jax.experimental import pallas as pl
from jax.experimental.pallas import tpu as pltpu
from jax.sharding import PartitionSpec as P

D = 512
HEADS = 8
DH = 64
FF = 2048
LEVELS = 7
DOCS = 4
QB = 128
NKEY = 512
PAIRS = HEADS // 2

masked_score = -1e30
beta_one = 0.9
beta_two = 0.999
bias_first = 1.0 - 0.9**10
bias_second = 1.0 - 0.999**10
learn_rate = 0.1
weight_decay = 0.1
epsilon = 1e-08
clip_norm = 1.0

BF = jnp.bfloat16
F32 = jnp.float32
MESH = pl.DeviceIdType.MESH
VM = pl.BlockSpec(memory_space=pltpu.VMEM)

NN = ((1,), (0,))
NT = ((1,), (1,))
TN = ((0,), (0,))


def mm(left, right, dims):
    return lax.dot_general(left, right, (dims, ((), ())), preferred_element_type=F32)


def params(cid=None):
    if cid is None:
        return pltpu.CompilerParams(vmem_limit_bytes=60 * 2**20)
    return pltpu.CompilerParams(
        vmem_limit_bytes=60 * 2**20, collective_id=cid, has_side_effects=True
    )


def sds(shape, dtype):
    return jax.ShapeDtypeStruct(shape, dtype)


def level_offset(local, level):
    return local - (local >> (level - 1))


def edge_levels(local):
    return [lv for lv in range(LEVELS) if (local >> lv) >= 16]


def far_levels(local):
    return [lv for lv in range(LEVELS) if (local >> lv) < 16]


def ext_rows(local, seq_len, level):
    return ((local >> level) if (local >> level) >= 16 else (seq_len >> level)) + 32


def key_rows(level):
    return max(QB >> level, 16) + 32


def key_start(level):
    return sum(key_rows(lv) for lv in range(level))


def window_start(level, block, offset, local):
    span = 16 << level
    if (local >> level) >= 16:
        if span <= QB:
            return block * (QB >> level)
        return (block * QB) // span * 16
    return (offset + block * QB) // span * 16


def averaging(local):
    row = lax.broadcasted_iota(jnp.int32, (local, local), 0)
    col = lax.broadcasted_iota(jnp.int32, (local, local), 1)
    total = jnp.zeros((local, local), F32)
    for lv in range(1, LEVELS):
        at = lax.shift_right_logical(col, lv) + level_offset(local, lv)
        total = jnp.where(at == row, 2.0**-lv, total)
    return total.astype(BF)


def norm_parts(values):
    center = jnp.mean(values, axis=-1, keepdims=True)
    centered = values - center
    spread = jnp.mean(centered * centered, axis=-1, keepdims=True)
    inverse = lax.rsqrt(spread + 1e-05)
    return centered * inverse, inverse


def norm_back(grad_in, normed, inverse, gain):
    scaled = grad_in * gain
    return inverse * (
        scaled
        - jnp.mean(scaled, axis=-1, keepdims=True)
        - normed * jnp.mean(scaled * normed, axis=-1, keepdims=True)
    )


def document_bounds(seg_row, seq_len):
    return [
        jnp.sum(jnp.where(seg_row < doc, 1.0, 0.0), axis=1, keepdims=True)
        for doc in range(1, DOCS)
    ]


def fill_bias(starts, first_query, seq_len, bias_ref):
    qpos = first_query + lax.broadcasted_iota(jnp.int32, (1, QB), 1)
    qf = qpos.astype(F32)
    low = jnp.zeros((1, QB), F32)
    high = jnp.full((1, QB), float(seq_len), F32)
    for start in starts:
        low = jnp.where(qf >= start, jnp.maximum(low, start), low)
        high = jnp.where(qf < start, jnp.minimum(high, start), high)
    for lv in range(LEVELS):
        span = 16 << lv
        rows = key_rows(lv)
        if span <= QB:
            key_first = first_query // (1 << lv) - 16
        else:
            key_first = first_query // span * 16 - 16
        index = key_first + lax.broadcasted_iota(jnp.int32, (rows, QB), 0)
        begin = (index * (1 << lv)).astype(F32)
        end = begin + float((1 << lv) - 1)
        block = lax.div(qpos, span)
        lo = jnp.maximum(low, ((block - 1) * span).astype(F32))
        hi = jnp.minimum(high, ((block + 2) * span).astype(F32))
        allowed = (begin >= lo) & (end < hi)
        if lv > 0:
            half = span // 2
            parent = lax.div(qpos, half)
            inner_lo = ((parent - 1) * half).astype(F32)
            inner_hi = ((parent + 2) * half).astype(F32)
            allowed = allowed & ((begin < inner_lo) | (begin >= inner_hi))
        bias_ref[key_start(lv) : key_start(lv) + rows, :] = jnp.where(
            allowed, lv * math.log(2.0), masked_score
        )


def build_ext(row, local, kv_ref, coarse_ref, edge_ref, far_ref, ext):
    count = far_ref.shape[1]
    for lv in range(LEVELS):
        rows = local >> lv
        if rows >= 16:
            ext[lv][0:16, :] = edge_ref[row, 0, 16 * lv : 16 * lv + 16, :]
            if lv == 0:
                ext[lv][16 : 16 + rows, :] = kv_ref[row]
            else:
                at = level_offset(local, lv)
                ext[lv][16 : 16 + rows, :] = coarse_ref[row, at : at + rows, :]
            ext[lv][16 + rows : 32 + rows, :] = edge_ref[row, 1, 16 * lv : 16 * lv + 16, :]
        else:
            at = level_offset(local, lv) - (local - 16)
            blank = jnp.zeros((16, 2 * D), F32)
            pieces = [blank]
            for owner in range(count):
                pieces.append(far_ref[row, owner].astype(F32)[at : at + rows, :])
            pieces.append(blank)
            ext[lv][...] = jnp.concatenate(pieces, axis=0).astype(BF)


def gather_keys(ext, block, offset, local, keys_ref):
    for lv in range(LEVELS):
        start = pl.multiple_of(window_start(lv, block, offset, local), 16)
        at = key_start(lv)
        keys_ref[at : at + key_rows(lv), :] = ext[lv][pl.ds(start, key_rows(lv)), :]


def lane_halves(values):
    lane = lax.broadcasted_iota(jnp.int32, values.shape, 1)
    zero = jnp.zeros_like(values)
    return jnp.concatenate(
        [jnp.where(lane < DH, values, zero), jnp.where(lane >= DH, values, zero)], axis=0
    )


def own_halves(pair_t):
    n = pair_t.shape[1] // 2
    sub = lax.broadcasted_iota(jnp.int32, (2 * DH, n), 0)
    return jnp.where(sub < DH, pair_t[:, :n], pair_t[:, n:])


def project_kernel(x_ref, w_ref, norm_ref, normed_ref, q_ref, kv_ref, coarse_ref, edge_ref, far_ref):
    rows, local = x_ref.shape[0], x_ref.shape[1]
    mean_of = averaging(local)
    tile = min(local, 256)
    gain, shift = norm_ref[0:1, :], norm_ref[1:2, :]
    for row in range(rows):

        def step(i, carry):
            part = pl.ds(pl.multiple_of(i * tile, tile), tile)
            hat, _ = norm_parts(x_ref[row, part, :].astype(F32))
            low = (hat * gain + shift).astype(BF)
            normed_ref[row, part, :] = low
            q_ref[row, part, :] = mm(low, w_ref[0], NN).astype(BF)
            kv_ref[row, part, 0:D] = mm(low, w_ref[1], NN).astype(BF)
            kv_ref[row, part, D : 2 * D] = mm(low, w_ref[2], NN).astype(BF)
            return carry

        lax.fori_loop(0, local // tile, step, 0)
        coarse_ref[row] = mm(mean_of, kv_ref[row], NN).astype(BF)
        for lv in edge_levels(local):
            n = local >> lv
            to = slice(16 * lv, 16 * lv + 16)
            if lv == 0:
                edge_ref[row, 0, to, :] = kv_ref[row, 0:16, :]
                edge_ref[row, 1, to, :] = kv_ref[row, n - 16 : n, :]
            else:
                at = level_offset(local, lv)
                edge_ref[row, 0, to, :] = coarse_ref[row, at : at + 16, :]
                edge_ref[row, 1, to, :] = coarse_ref[row, at + n - 16 : at + n, :]
        far_ref[row] = coarse_ref[row, local - 16 : local, :]


def attend_kernel(
    q_ref, kv_ref, coarse_ref, edge_ref, far_ref, seg_ref, mixed_ref, total_ref, keys, bias, *ext
):
    rows, local = q_ref.shape[0], q_ref.shape[1]
    seq_len = seg_ref.shape[1]
    offset = lax.axis_index("seq") * local
    for row in range(rows):
        build_ext(row, local, kv_ref, coarse_ref, edge_ref, far_ref, ext)
        starts = document_bounds(seg_ref[row : row + 1, :], seq_len)

        def step(block, carry):
            gather_keys(ext, block, offset, local, keys)
            fill_bias(starts, offset + block * QB, seq_len, bias)
            part = pl.ds(pl.multiple_of(block * QB, QB), QB)
            both = jnp.concatenate([bias[...], bias[...]], axis=1)
            for pair in range(PAIRS):
                lanes = slice(128 * pair, 128 * pair + 128)
                queries = lane_halves(q_ref[row, part, lanes] * BF(DH**-0.5))
                scores = mm(keys[:, lanes], queries, NT) + both
                peak = jnp.max(scores, axis=0, keepdims=True)
                weights = jnp.exp(scores - peak)
                denominator = jnp.sum(weights, axis=0, keepdims=True)
                total_ref[row, block, pair : pair + 1, :] = peak + jnp.log(denominator)
                values = keys[:, D + 128 * pair : D + 128 * pair + 128]
                mixed_t = mm(values, weights.astype(BF), TN) / denominator
                mixed_ref[row, part, lanes] = own_halves(mixed_t).T.astype(BF)
            return carry

        lax.fori_loop(0, local // QB, step, 0)


def feed_kernel(
    x_ref,
    mixed_ref,
    og_ref,
    wout_ref,
    wup_ref,
    wdown_ref,
    norm_ref,
    out_ref,
    gres_ref,
    gmix_ref,
    gout_ref,
    gup_ref,
    gdown_ref,
    grow_ref,
    resid_s,
    second_s,
    second_t,
    og_t,
    acc_s,
    gsec_s,
    hid_s,
    gpre_s,
    low_s,
):
    tokens = x_ref.shape[0]
    tile = 256
    tiles = tokens // tile
    width = 512
    gain, shift = norm_ref[2:3, :], norm_ref[3:4, :]

    def rows_of(i):
        return pl.ds(pl.multiple_of(i * tile, tile), tile)

    def first(i, carry):
        part = rows_of(i)
        resid = x_ref[part, :].astype(F32) + mm(mixed_ref[part, :], wout_ref[...], NN)
        resid_s[part, :] = resid
        acc_s[part, :] = resid
        hat, _ = norm_parts(resid)
        second = (hat * gain + shift).astype(BF)
        second_s[part, :] = second
        second_t[:, part] = second.T
        og_t[:, part] = og_ref[part, :].T
        gsec_s[part, :] = jnp.zeros((tile, D), F32)
        return carry

    lax.fori_loop(0, tiles, first, 0)

    def chunk(f, carry):
        cols = pl.ds(pl.multiple_of(f * width, width), width)

        def inner(i, inner_carry):
            part = rows_of(i)
            pre = mm(second_s[part, :], wup_ref[:, cols], NN)
            square = pre * pre
            tangent = jnp.tanh(0.7978845608 * (pre + 0.044715 * pre * square))
            half = 0.5 + 0.5 * tangent
            hidden = (pre * half).astype(BF)
            slope = half + 0.5 * pre * (1.0 - tangent * tangent) * (
                0.7978845608 + 0.7978845608 * 3.0 * 0.044715 * square
            )
            grad_pre = (mm(og_ref[part, :], wdown_ref[cols, :], NT) * slope).astype(BF)
            hid_s[part, :] = hidden
            gpre_s[part, :] = grad_pre
            acc_s[part, :] += mm(hidden, wdown_ref[cols, :], NN)
            gsec_s[part, :] += mm(grad_pre, wup_ref[:, cols], NT)
            return inner_carry

        lax.fori_loop(0, tiles, inner, 0)
        gdown_ref[:, cols] = mm(og_t[...], hid_s[...], NN).astype(BF)
        gup_ref[:, cols] = mm(second_t[...], gpre_s[...], NN).astype(BF)
        return carry

    lax.fori_loop(0, FF // width, chunk, 0)
    grow_ref[...] = jnp.zeros_like(grow_ref)

    def last(i, carry):
        part = rows_of(i)
        out_ref[part, :] = acc_s[part, :].astype(BF)
        hat, inverse = norm_parts(resid_s[part, :])
        grad = gsec_s[part, :]
        gres = og_ref[part, :].astype(F32) + norm_back(grad, hat, inverse, gain)
        gres_ref[part, :] = gres
        low = gres.astype(BF)
        low_s[part, :] = low
        gmix_ref[part, :] = mm(low, wout_ref[...], NT).astype(BF)
        grow_ref[2:3, :] += jnp.sum(grad * hat, axis=0, keepdims=True)
        grow_ref[3:4, :] += jnp.sum(grad, axis=0, keepdims=True)
        return carry

    lax.fori_loop(0, tiles, last, 0)
    gout_ref[...] = mm(mixed_ref[...], low_s[...], TN).astype(BF)


def attend_back_kernel(
    q_ref,
    kv_ref,
    coarse_ref,
    edge_ref,
    far_ref,
    seg_ref,
    total_ref,
    gmix_ref,
    gq_ref,
    gkv_ref,
    gcoarse_ref,
    gedge_ref,
    gfar_ref,
    keys,
    bias,
    gkeys,
    *ext_both,
):
    ext, gext = ext_both[:LEVELS], ext_both[LEVELS:]
    rows, local = q_ref.shape[0], q_ref.shape[1]
    seq_len = seg_ref.shape[1]
    count = far_ref.shape[1]
    offset = lax.axis_index("seq") * local
    for row in range(rows):
        build_ext(row, local, kv_ref, coarse_ref, edge_ref, far_ref, ext)
        starts = document_bounds(seg_ref[row : row + 1, :], seq_len)
        for item in gext:
            item[...] = jnp.zeros_like(item)

        def step(block, carry):
            gather_keys(ext, block, offset, local, keys)
            fill_bias(starts, offset + block * QB, seq_len, bias)
            part = pl.ds(pl.multiple_of(block * QB, QB), QB)
            both = jnp.concatenate([bias[...], bias[...]], axis=1)
            for pair in range(PAIRS):
                lanes = slice(128 * pair, 128 * pair + 128)
                vlanes = slice(D + 128 * pair, D + 128 * pair + 128)
                queries = lane_halves(q_ref[row, part, lanes] * BF(DH**-0.5))
                grads = lane_halves(gmix_ref[row, part, lanes])
                scores = mm(keys[:, lanes], queries, NT) + both
                soft = jnp.exp(scores - total_ref[row, block, pair : pair + 1, :])
                gsoft = mm(keys[:, vlanes], grads, NT)
                row_total = jnp.sum(soft * gsoft, axis=0, keepdims=True)
                gscore = (soft * (gsoft - row_total)).astype(BF)
                gkeys[:, lanes] = mm(gscore, queries, NN)
                gkeys[:, vlanes] = mm(soft.astype(BF), grads, NN)
                gq_t = own_halves(mm(keys[:, lanes], gscore, TN)) * DH**-0.5
                gq_ref[row, part, lanes] = gq_t.T.astype(BF)
            for lv in range(LEVELS):
                start = pl.multiple_of(window_start(lv, block, offset, local), 16)
                at = key_start(lv)
                gext[lv][pl.ds(start, key_rows(lv)), :] += gkeys[at : at + key_rows(lv), :]
            return carry

        lax.fori_loop(0, local // QB, step, 0)
        gkv_ref[row] = gext[0][16 : 16 + local, :]
        for lv in edge_levels(local):
            n = local >> lv
            if lv > 0:
                at = level_offset(local, lv)
                gcoarse_ref[row, at : at + n, :] = gext[lv][16 : 16 + n, :]
            gedge_ref[row, 0, 16 * lv : 16 * lv + 16, :] = gext[lv][0:16, :].astype(BF)
            gedge_ref[row, 1, 16 * lv : 16 * lv + 16, :] = gext[lv][16 + n : 32 + n, :].astype(BF)
        for owner in range(count):
            pieces = []
            used = 0
            for lv in far_levels(local):
                n = local >> lv
                pieces.append(gext[lv][16 + owner * n : 16 + owner * n + n, :])
                used += n
            pieces.append(jnp.zeros((16 - used, 2 * D), F32))
            gfar_ref[row, owner] = jnp.concatenate(pieces, axis=0).astype(BF)


def project_back_kernel(
    x_ref,
    normed_ref,
    w_ref,
    norm_ref,
    gres_ref,
    gq_ref,
    gkv_ref,
    gcoarse_ref,
    edge_ref,
    far_ref,
    grow_in_ref,
    ginput_ref,
    gqkv_ref,
    grow_ref,
    coarse_s,
    pair_s,
    normed_t,
):
    rows, local = x_ref.shape[0], x_ref.shape[1]
    count = far_ref.shape[1]
    spread_of = averaging(local)
    gain = norm_ref[0:1, :]
    tile = min(local, 256)
    grow_ref[...] = grow_in_ref[...]
    for row in range(rows):
        for lv in edge_levels(local):
            n = local >> lv
            near = edge_ref[row, 0, 16 * lv : 16 * lv + 16, :].astype(F32)
            after = edge_ref[row, 1, 16 * lv : 16 * lv + 16, :].astype(F32)
            if lv == 0:
                gkv_ref[row, 0:16, :] += near
                gkv_ref[row, n - 16 : n, :] += after
            else:
                at = level_offset(local, lv)
                gcoarse_ref[row, at : at + 16, :] += near
                gcoarse_ref[row, at + n - 16 : at + n, :] += after
        total = far_ref[row, 0].astype(F32)
        for owner in range(1, count):
            total += far_ref[row, owner].astype(F32)
        gcoarse_ref[row, local - 16 : local, :] = total
        coarse_s[...] = gcoarse_ref[row].astype(BF)
        for part in range(local // tile):
            span = slice(part * tile, part * tile + tile)
            where = slice(row * local + part * tile, row * local + part * tile + tile)
            pair = (gkv_ref[row, span, :] + mm(spread_of[:, span], coarse_s[...], TN)).astype(BF)
            pair_s[where, :] = pair
            normed_t[:, where] = normed_ref[row, span, :].T
            gnormed = (
                mm(gq_ref[row, span, :], w_ref[0], NT)
                + mm(pair[:, 0:D], w_ref[1], NT)
                + mm(pair[:, D : 2 * D], w_ref[2], NT)
            )
            hat, inverse = norm_parts(x_ref[row, span, :].astype(F32))
            ginput_ref[row, span, :] = gres_ref[row, span, :] + norm_back(
                gnormed, hat, inverse, gain
            )
            grow_ref[0:1, :] += jnp.sum(gnormed * hat, axis=0, keepdims=True)
            grow_ref[1:2, :] += jnp.sum(gnormed, axis=0, keepdims=True)
    flat_q = gq_ref[...].reshape(rows * local, D)
    gqkv_ref[:, 0:D] = mm(normed_t[...], flat_q, NN).astype(BF)
    gqkv_ref[:, D : 2 * D] = mm(normed_t[...], pair_s[:, 0:D], NN).astype(BF)
    gqkv_ref[:, 2 * D : 3 * D] = mm(normed_t[...], pair_s[:, D : 2 * D], NN).astype(BF)


def adam_kernel(n_dp, *refs):
    (gup, gmix, gdown, grow, square) = refs[0:5]
    weights, firsts, seconds = refs[5:9], refs[9:14], refs[14:19]
    outs = refs[19:]
    new_w, norm_grad, new_m, new_s, grad_norm = (
        outs[0:4],
        outs[4],
        outs[5:10],
        outs[10:15],
        outs[15],
    )
    root = jnp.sqrt(square[0:1, 0:1])
    grad_norm[...] = root
    factor = jnp.minimum(1.0, clip_norm / root)

    def moments(clipped, first, second):
        return (
            beta_one * first + (1.0 - beta_one) * clipped,
            beta_two * second + (1.0 - beta_two) * clipped * clipped,
        )

    def update(weight, grad, first, second):
        mean, sq = moments(grad * factor, first, second)
        change = mean / bias_first / (jnp.sqrt(sq / bias_second) + epsilon) + weight_decay * weight
        return weight - learn_rate * change, mean, sq

    for c in range(3):
        w, m, s = update(
            weights[0][c], gmix[:, c * D : c * D + D].astype(F32), firsts[0][c], seconds[0][c]
        )
        new_w[0][c], new_m[0][c], new_s[0][c] = w, m, s
    for at, grad in ((1, gmix[:, 3 * D : 4 * D]), (2, gup[...]), (3, gdown[...])):
        grad = grad.astype(F32)
        if at == 3:
            grad = grad.T
        w, m, s = update(weights[at][...], grad, firsts[at][...], seconds[at][...])
        new_w[at][...], new_m[at][...], new_s[at][...] = w, m, s
    width = D // n_dp
    own = lax.axis_index("dp") * width
    rolled = pltpu.roll(grow[...], D - own, 1)[0:4, 0:width]
    clipped = rolled * factor
    norm_grad[...] = clipped
    m, s = moments(clipped, firsts[4][...], seconds[4][...])
    new_m[4][...], new_s[4][...] = m, s


class Copies:
    def __init__(self, send, recv):
        self.send, self.recv = send, recv
        self.started = []

    def push(self, src, dst, send_at, recv_at, device):
        copy = pltpu.make_async_remote_copy(
            src_ref=src,
            dst_ref=dst,
            send_sem=self.send.at[send_at],
            recv_sem=self.recv.at[recv_at],
            device_id=device,
            device_id_type=MESH,
        )
        copy.start()
        self.started.append(copy)

    def arrived(self, dst, recv_at, device):
        pltpu.make_async_remote_copy(
            src_ref=dst,
            dst_ref=dst,
            send_sem=self.send.at[0],
            recv_sem=self.recv.at[recv_at],
            device_id=device,
            device_id_type=MESH,
        ).wait_recv()

    def finish(self):
        for copy in self.started:
            copy.wait_send()
        self.started = []


def greet(peers):
    barrier = pltpu.get_barrier_semaphore()
    for peer in peers:
        pl.semaphore_signal(barrier, inc=1, device_id=peer, device_id_type=MESH)
    pl.semaphore_wait(barrier, len(peers))


def weight_kernel(
    n_dp, wqkv, wout, wup, wdown, norm, fqkv, fout, fup, fdown, fnorm, slots, send, recv
):
    d, s = lax.axis_index("dp"), lax.axis_index("seq")
    core = lax.rem(s, 2)
    z, y = lax.div(d, 2), lax.rem(d, 2)
    depth = n_dp // 2
    flip = d + 1 - 2 * y
    mate = s + 1 - 2 * core
    others = [lax.rem(d + k, n_dp) for k in range(1, n_dp)]
    greet([(o, s) for o in others] + [(d, mate)])

    fulls = [fqkv, fout, fup, fdown]
    counts = [D // n_dp, D // n_dp, D // n_dp, FF // n_dp]

    def half(p, shard, which):
        n = counts[p] // 2
        start = pl.multiple_of(shard * counts[p] + which * n, n)
        if p == 0:
            return fulls[p].at[:, pl.ds(start, n), :]
        return fulls[p].at[pl.ds(start, n), :]

    for p, w in enumerate((wqkv, wout, wup, wdown)):
        start = pl.multiple_of(d * counts[p], counts[p])
        if p == 0:
            fulls[p][:, pl.ds(start, counts[p]), :] = w[...].astype(BF)
        else:
            fulls[p][pl.ds(start, counts[p]), :] = w[...].astype(BF)
    slots[d] = norm[...].astype(BF).astype(F32)

    base_y, base_c, base_n = 4 * depth, 8 * depth, 8 * depth + 4 * n_dp
    copies = Copies(send, recv)
    for k, o in enumerate(others):
        copies.push(slots.at[d], slots.at[d], base_n + 1 + k, base_n + d, (o, s))
    for p in range(4):
        for k in range(1, depth):
            other = lax.rem(z + k, depth) * 2 + y
            mine = half(p, d, core)
            copies.push(mine, mine, p * depth + k, p * depth + z, (other, s))
        mine = half(p, d, core)
        copies.push(mine, mine, base_y + p * depth, base_y + p * depth + z, (flip, s))
    for p in range(4):
        for k in range(1, depth):
            zz = lax.rem(z + k, depth)
            shard = zz * 2 + y
            here = half(p, shard, core)
            copies.arrived(here, p * depth + zz, (shard, s))
            copies.push(here, here, base_y + p * depth + k, base_y + p * depth + zz, (flip, s))
            copies.push(here, here, base_c + p * n_dp + k, base_c + p * n_dp + shard, (d, mate))
    for p in range(4):
        for k in range(depth):
            zz = lax.rem(z + k, depth)
            shard = zz * 2 + 1 - y
            here = half(p, shard, core)
            copies.arrived(here, base_y + p * depth + zz, (flip, s))
            copies.push(
                here, here, base_c + p * n_dp + depth + k, base_c + p * n_dp + shard, (d, mate)
            )
    for o in others:
        copies.arrived(slots.at[o], base_n + o, (o, s))
    width = D // n_dp
    total = jnp.zeros((8, D), F32)
    for shard in range(n_dp):
        i = lax.broadcasted_iota(jnp.int32, (128, D), 0)
        j = lax.broadcasted_iota(jnp.int32, (128, D), 1)
        pick = jnp.where((j == i + shard * width) & (i < width), 1.0, 0.0).astype(BF)
        total += mm(slots[shard].astype(BF), pick, NN)
    fnorm[...] = total
    for p in range(4):
        for k in range(1, n_dp):
            shard = lax.rem(d + k, n_dp)
            copies.arrived(half(p, shard, 1 - core), base_c + p * n_dp + shard, (d, mate))
    copies.finish()


def edge_kernel(n_seq, personal, edge_in, far_in, edge_out, far_out, send, recv):
    d, s = lax.axis_index("dp"), lax.axis_index("seq")
    rows = edge_in.shape[0]
    others = [lax.rem(s + k, n_seq) for k in range(1, n_seq)]
    greet([(d, o) for o in others])

    def edge_copy(row, way, device):
        at = row * 2 + way
        return pltpu.make_async_remote_copy(
            src_ref=edge_in.at[row, way],
            dst_ref=edge_out.at[row, 1 - way],
            send_sem=send.at[at],
            recv_sem=recv.at[row * 2 + 1 - way],
            device_id=(d, device),
            device_id_type=MESH,
        )

    def far_copy(row, k, other):
        src = far_in.at[row, other] if personal else far_in.at[row]
        return pltpu.make_async_remote_copy(
            src_ref=src,
            dst_ref=far_out.at[row, s],
            send_sem=send.at[2 * rows + row * n_seq + k],
            recv_sem=recv.at[2 * rows + row * n_seq + s],
            device_id=(d, other),
            device_id_type=MESH,
        )

    for row in range(rows):

        @pl.when(s > 0)
        def _():
            edge_copy(row, 0, s - 1).start()

        @pl.when(s < n_seq - 1)
        def _():
            edge_copy(row, 1, s + 1).start()

        for k, other in enumerate(others):
            far_copy(row, k, other).start()
        far_out[row, s] = far_in[row, s] if personal else far_in[row]

    for row in range(rows):

        @pl.when(s > 0)
        def _():
            edge_copy(row, 1, s - 1).wait_recv()

        @pl.when(s == 0)
        def _():
            edge_out[row, 0] = jnp.zeros(edge_out.shape[2:], BF)

        @pl.when(s < n_seq - 1)
        def _():
            edge_copy(row, 0, s + 1).wait_recv()

        @pl.when(s == n_seq - 1)
        def _():
            edge_out[row, 1] = jnp.zeros(edge_out.shape[2:], BF)

        for k, other in enumerate(others):
            pltpu.make_async_remote_copy(
                src_ref=far_out.at[row, other],
                dst_ref=far_out.at[row, other],
                send_sem=send.at[0],
                recv_sem=recv.at[2 * rows + row * n_seq + other],
                device_id=(d, other),
                device_id_type=MESH,
            ).wait_recv()

        @pl.when(s > 0)
        def _():
            edge_copy(row, 0, s - 1).wait_send()

        @pl.when(s < n_seq - 1)
        def _():
            edge_copy(row, 1, s + 1).wait_send()

        for k, other in enumerate(others):
            far_copy(row, k, other).wait_send()


def grad_parts(n_dp, n_seq):
    mixed = [(1, 0, 3 * D), (1, 3 * D, 4 * D)]
    if (3 * D // n_seq) % 128 or (D // n_seq) % 128:
        mixed = [(1, 0, 4 * D)]
    parts = [(0, 0, FF, True), (2, 0, FF, False)]
    parts += [(src, lo, hi, True) for src, lo, hi in mixed]
    return parts


def block_shape(part, n_dp, n_seq):
    _, lo, hi, by_rows = part
    if by_rows:
        return (D // n_dp, (hi - lo) // n_seq)
    return (D // n_seq, (hi - lo) // n_dp)


def reduce_kernel(n_dp, n_seq, gup, gmix, gdown, grow, oup, omix, odown, orow, osq, *scratch):
    parts = grad_parts(n_dp, n_seq)
    n = len(parts)
    sources, finals = (gup, gmix, gdown), (oup, omix, odown)
    first_in, held, mid_in, late_in, last_in = (scratch[i * n : i * n + n] for i in range(5))
    rows_seq, rows_dp, sq_seq, sq_dp, send, recv = scratch[5 * n :]
    d, s = lax.axis_index("dp"), lax.axis_index("seq")
    core, hi = lax.rem(s, 2), lax.div(s, 2)
    z, y = lax.div(d, 2), lax.rem(d, 2)
    high, depth = n_seq // 2, n_dp // 2
    mate, flip = s + 1 - 2 * core, d + 1 - 2 * y
    seq_others = [lax.rem(s + k, n_seq) for k in range(1, n_seq)]
    dp_others = [lax.rem(d + k, n_dp) for k in range(1, n_dp)]
    greet([(d, o) for o in seq_others] + [(o, s) for o in dp_others])

    copies = Copies(send, recv)
    stride = 1 + high + 1 + depth + n_seq
    rows_base = n * stride

    def half_of(part, which):
        src, lo, up, by_rows = part
        ref = sources[src]
        if by_rows:
            w = (up - lo) // 2
            return ref.at[:, pl.ds(pl.multiple_of(lo + which * w, 128), w)]
        w = D // 2
        return ref.at[pl.ds(pl.multiple_of(which * w, w), w), lo:up]

    for p, part in enumerate(parts):
        copies.push(half_of(part, 1 - core), first_in[p], p * stride, p * stride, (d, mate))
    for k, o in enumerate(seq_others):
        copies.push(grow, rows_seq.at[s], rows_base + 1 + k, rows_base + s, (d, o))
    rows_seq[s] = grow[...]

    for p, part in enumerate(parts):
        copies.arrived(first_in[p], p * stride, (d, mate))
        src, lo, up, by_rows = part
        a, b = block_shape(part, n_dp, n_seq)
        for h in range(high):
            for shard in range(n_dp):
                if by_rows:
                    r = slice(shard * a, shard * a + a)
                    own = pl.ds(pl.multiple_of(lo + (core * high + h) * b, 128), b)
                    mine = sources[src][r, own]
                    theirs = first_in[p][r, h * b : h * b + b]
                else:
                    r = pl.ds(pl.multiple_of((core * high + h) * a, a), a)
                    mine = sources[src][r, lo + shard * b : lo + shard * b + b]
                    theirs = first_in[p][h * a : h * a + a, shard * b : shard * b + b]
                held[p][h, shard // 2, shard % 2] = (mine.astype(F32) + theirs.astype(F32)).astype(
                    BF
                )
        if p % 2 == 0:
            send_high(copies, p * stride + 1, held[p], None, mid_in[p], d, hi, core, high)
        else:
            copies.push(
                held[p].at[:, :, 1 - y], late_in[p], p * stride + 1 + high, p * stride + 1 + high,
                (flip, s),
            )
    for k, o in enumerate(seq_others):
        copies.arrived(rows_seq.at[o], rows_base + o, (d, o))
    total = rows_seq[0]
    for o in range(1, n_seq):
        total += rows_seq[o]
    rows_dp[d] = total
    dp_base = rows_base + n_seq
    for k, o in enumerate(dp_others):
        copies.push(rows_dp.at[d], rows_dp.at[d], dp_base + 1 + k, dp_base + d, (o, s))

    for p, part in enumerate(parts):
        if p % 2 == 0:
            take_high(copies, p * stride + 1, mid_in[p], d, hi, core, high)
            for zz in range(depth):
                for yy in range(2):
                    value = held[p][hi, zz, yy].astype(F32)
                    for k in range(1, high):
                        value += mid_in[p][lax.rem(hi + k, high), zz, yy].astype(F32)
                    held[p][hi, zz, yy] = value.astype(BF)
            copies.push(
                held[p].at[hi, :, 1 - y], late_in[p], p * stride + 1 + high, p * stride + 1 + high,
                (flip, s),
            )
        else:
            copies.arrived(late_in[p], p * stride + 1 + high, (flip, s))
            for h in range(high):
                for zz in range(depth):
                    value = held[p][h, zz, y].astype(F32) + late_in[p][h, zz].astype(F32)
                    held[p][h, zz, y] = value.astype(BF)
            send_high(copies, p * stride + 1, held[p], y, mid_in[p], d, hi, core, high)
    for p, part in enumerate(parts):
        if p % 2 == 0:
            copies.arrived(late_in[p], p * stride + 1 + high, (flip, s))
            for zz in range(depth):
                value = held[p][hi, zz, y].astype(F32) + late_in[p][zz].astype(F32)
                held[p][hi, zz, y] = value.astype(BF)
        else:
            take_high(copies, p * stride + 1, mid_in[p], d, hi, core, high)
            for zz in range(depth):
                value = held[p][hi, zz, y].astype(F32)
                for k in range(1, high):
                    value += mid_in[p][lax.rem(hi + k, high), zz].astype(F32)
                held[p][hi, zz, y] = value.astype(BF)
        for k in range(1, depth):
            zz = lax.rem(z + k, depth)
            at = p * stride + 2 + high
            copies.push(
                held[p].at[hi, zz, y], last_in[p].at[z], at + k, at + z, (zz * 2 + y, s)
            )
    square = jnp.zeros((1, 1), F32)
    for p, part in enumerate(parts):
        src, lo, up, by_rows = part
        a, b = block_shape(part, n_dp, n_seq)
        at = p * stride + 2 + high
        for k in range(1, depth):
            zz = lax.rem(z + k, depth)
            copies.arrived(last_in[p].at[zz], at + zz, (zz * 2 + y, s))
        value = held[p][hi, z, y].astype(F32)
        for k in range(1, depth):
            value += last_in[p][lax.rem(z + k, depth)].astype(F32)
        low = value.astype(BF)

        def final(owner_core, owner_high):
            which = owner_core * high + owner_high
            if by_rows:
                return finals[src].at[:, pl.ds(pl.multiple_of(lo + which * b, 128), b)]
            return finals[src].at[pl.ds(pl.multiple_of(which * a, a), a), :]

        final(core, hi)[...] = low
        value = low.astype(F32)
        square += jnp.sum(jnp.sum(value * value, axis=0, keepdims=True), axis=1, keepdims=True)
        at = p * stride + 2 + high + depth
        for k, o in enumerate(seq_others):
            copies.push(final(core, hi), final(core, hi), at + 1 + k, at + s, (d, o))
    sq_base = dp_base + n_dp
    sq_seq[s] = jnp.broadcast_to(square, (8, 128))
    for k, o in enumerate(seq_others):
        copies.push(sq_seq.at[s], sq_seq.at[s], sq_base + 1 + k, sq_base + s, (d, o))
    for k, o in enumerate(dp_others):
        copies.arrived(rows_dp.at[o], dp_base + o, (o, s))
    total = rows_dp[0]
    for o in range(1, n_dp):
        total += rows_dp[o]
    orow[...] = total
    for k, o in enumerate(seq_others):
        copies.arrived(sq_seq.at[o], sq_base + o, (d, o))
    square = sq_seq[0]
    for o in range(1, n_seq):
        square += sq_seq[o]
    sq_dp[d] = square
    sq_late = sq_base + n_seq
    for k, o in enumerate(dp_others):
        copies.push(sq_dp.at[d], sq_dp.at[d], sq_late + 1 + k, sq_late + d, (o, s))
    for p, part in enumerate(parts):
        src, lo, up, by_rows = part
        a, b = block_shape(part, n_dp, n_seq)
        at = p * stride + 2 + high + depth
        for k, o in enumerate(seq_others):
            which = lax.rem(o, 2) * high + lax.div(o, 2)
            if by_rows:
                here = finals[src].at[:, pl.ds(pl.multiple_of(lo + which * b, 128), b)]
            else:
                here = finals[src].at[pl.ds(pl.multiple_of(which * a, a), a), :]
            copies.arrived(here, at + o, (d, o))
    for k, o in enumerate(dp_others):
        copies.arrived(sq_dp.at[o], sq_late + o, (o, s))
    square = sq_dp[0]
    for o in range(1, n_dp):
        square += sq_dp[o]
    own = total[0:4, :]
    rows_square = jnp.sum(jnp.sum(own * own, axis=0, keepdims=True), axis=1, keepdims=True)
    osq[...] = square + rows_square
    copies.finish()


def send_high(copies, at, held, y, mid_in, d, hi, core, high):
    for k in range(1, high):
        h = lax.rem(hi + k, high)
        src = held.at[h] if y is None else held.at[h, :, y]
        copies.push(src, mid_in.at[hi], at + k, at + hi, (d, h * 2 + core))


def take_high(copies, at, mid_in, d, hi, core, high):
    for k in range(1, high):
        h = lax.rem(hi + k, high)
        copies.arrived(mid_in.at[h], at + h, (d, h * 2 + core))


def on_device(
    inputs,
    segment_ids,
    out_grad,
    w_qkv,
    w_out,
    w_up,
    w_down,
    norm_params,
    qkv_first,
    qkv_second,
    out_first,
    out_second,
    up_first,
    up_second,
    down_first,
    down_second,
    norm_first,
    norm_second,
):
    n_dp, n_seq = lax.axis_size("dp"), lax.axis_size("seq")
    rows, local = inputs.shape[0], inputs.shape[1]
    seq_len = segment_ids.shape[1]
    tokens = rows * local
    dma = pltpu.SemaphoreType.DMA

    norm_pad = jnp.pad(norm_params, ((0, 4), (0, 128 - norm_params.shape[1])))
    sems = 8 * (n_dp // 2) + 5 * n_dp
    fqkv, fout, fup, fdown, fnorm = pl.pallas_call(
        functools.partial(weight_kernel, n_dp),
        out_shape=[
            sds((3, D, D), BF),
            sds((D, D), BF),
            sds((D, FF), BF),
            sds((FF, D), BF),
            sds((8, D), F32),
        ],
        in_specs=[VM] * 5,
        out_specs=[VM] * 5,
        scratch_shapes=[pltpu.VMEM((n_dp, 8, 128), F32), dma((sems,)), dma((sems,))],
        compiler_params=params(0),
        name="gather_weights",
    )(w_qkv, w_out, w_up, w_down, norm_pad)

    edge = 16 * len(edge_levels(local))
    normed, q, kv, coarse, edge_own, far_own = pl.pallas_call(
        project_kernel,
        out_shape=[
            sds((rows, local, D), BF),
            sds((rows, local, D), BF),
            sds((rows, local, 2 * D), BF),
            sds((rows, local, 2 * D), BF),
            sds((rows, 2, edge, 2 * D), BF),
            sds((rows, 16, 2 * D), BF),
        ],
        in_specs=[VM] * 3,
        out_specs=[VM] * 6,
        compiler_params=params(),
        name="project",
    )(inputs, fqkv, fnorm)

    sems = rows * (2 + n_seq)

    def exchange(personal, cid, edge_part, far_part):
        return pl.pallas_call(
            functools.partial(edge_kernel, n_seq, personal),
            out_shape=[sds((rows, 2, edge, 2 * D), BF), sds((rows, n_seq, 16, 2 * D), BF)],
            in_specs=[VM] * 2,
            out_specs=[VM] * 2,
            scratch_shapes=[dma((sems,)), dma((sems,))],
            compiler_params=params(cid),
            name="exchange_back" if personal else "exchange",
        )(edge_part, far_part)

    edge_near, far_all = exchange(False, 1, edge_own, far_own)

    ext_shapes = [(ext_rows(local, seq_len, lv), 2 * D) for lv in range(LEVELS)]
    blocks = local // QB
    mixed, totals = pl.pallas_call(
        attend_kernel,
        out_shape=[sds((rows, local, D), BF), sds((rows, blocks, PAIRS, 2 * QB), F32)],
        in_specs=[VM] * 6,
        out_specs=[VM] * 2,
        scratch_shapes=[pltpu.VMEM((NKEY, 2 * D), BF), pltpu.VMEM((NKEY, QB), F32)]
        + [pltpu.VMEM(shape, BF) for shape in ext_shapes],
        compiler_params=params(),
        name="attend",
    )(q, kv, coarse, edge_near, far_all, segment_ids)

    outputs, gres, gmixed, gout, gup, gdown, grow = pl.pallas_call(
        feed_kernel,
        out_shape=[
            sds((tokens, D), BF),
            sds((tokens, D), F32),
            sds((tokens, D), BF),
            sds((D, D), BF),
            sds((D, FF), BF),
            sds((D, FF), BF),
            sds((8, D), F32),
        ],
        in_specs=[VM] * 7,
        out_specs=[VM] * 7,
        scratch_shapes=[
            pltpu.VMEM((tokens, D), F32),
            pltpu.VMEM((tokens, D), BF),
            pltpu.VMEM((D, tokens), BF),
            pltpu.VMEM((D, tokens), BF),
            pltpu.VMEM((tokens, D), F32),
            pltpu.VMEM((tokens, D), F32),
            pltpu.VMEM((tokens, 512), BF),
            pltpu.VMEM((tokens, 512), BF),
            pltpu.VMEM((tokens, D), BF),
        ],
        compiler_params=params(),
        name="feed",
    )(
        inputs.reshape(tokens, D),
        mixed.reshape(tokens, D),
        out_grad.reshape(tokens, D),
        fout,
        fup,
        fdown,
        fnorm,
    )

    gq, gkv, gcoarse, gedge, gfar = pl.pallas_call(
        attend_back_kernel,
        out_shape=[
            sds((rows, local, D), BF),
            sds((rows, local, 2 * D), F32),
            sds((rows, local, 2 * D), F32),
            sds((rows, 2, edge, 2 * D), BF),
            sds((rows, n_seq, 16, 2 * D), BF),
        ],
        in_specs=[VM] * 8,
        out_specs=[VM] * 5,
        scratch_shapes=[
            pltpu.VMEM((NKEY, 2 * D), BF),
            pltpu.VMEM((NKEY, QB), F32),
            pltpu.VMEM((NKEY, 2 * D), F32),
        ]
        + [pltpu.VMEM(shape, BF) for shape in ext_shapes]
        + [pltpu.VMEM(shape, F32) for shape in ext_shapes],
        compiler_params=params(),
        name="attend_back",
    )(q, kv, coarse, edge_near, far_all, segment_ids, totals, gmixed.reshape(rows, local, D))

    edge_back, far_back = exchange(True, 2, gedge, gfar)

    input_grad, gqkv, grow = pl.pallas_call(
        project_back_kernel,
        out_shape=[sds((rows, local, D), F32), sds((D, 3 * D), BF), sds((8, D), F32)],
        in_specs=[VM] * 11,
        out_specs=[VM] * 3,
        scratch_shapes=[
            pltpu.VMEM((local, 2 * D), BF),
            pltpu.VMEM((tokens, 2 * D), BF),
            pltpu.VMEM((D, tokens), BF),
        ],
        compiler_params=params(),
        name="project_back",
    )(
        inputs,
        normed,
        fqkv,
        fnorm,
        gres.reshape(rows, local, D),
        gq,
        gkv,
        gcoarse,
        edge_back,
        far_back,
        grow,
    )

    parts = grad_parts(n_dp, n_seq)
    high, depth = n_seq // 2, n_dp // 2
    scratch = [[], [], [], [], []]
    for p, part in enumerate(parts):
        _, lo, up, by_rows = part
        a, b = block_shape(part, n_dp, n_seq)
        half = (D, (up - lo) // 2) if by_rows else (D // 2, up - lo)
        scratch[0].append(pltpu.VMEM(half, BF))
        scratch[1].append(pltpu.VMEM((high, depth, 2, a, b), BF))
        scratch[2].append(pltpu.VMEM((high, depth, 2, a, b) if p % 2 == 0 else (high, depth, a, b), BF))
        scratch[3].append(pltpu.VMEM((depth, a, b) if p % 2 == 0 else (high, depth, a, b), BF))
        scratch[4].append(pltpu.VMEM((depth, a, b), BF))
    scratch = [item for group in scratch for item in group]
    stride = 1 + high + 1 + depth + n_seq
    sems = len(parts) * stride + 2 * (n_seq + n_dp)
    scratch += [
        pltpu.VMEM((n_seq, 8, D), F32),
        pltpu.VMEM((n_dp, 8, D), F32),
        pltpu.VMEM((n_seq, 8, 128), F32),
        pltpu.VMEM((n_dp, 8, 128), F32),
        dma((sems,)),
        dma((sems,)),
    ]
    sup, smix, sdown, srow, square = pl.pallas_call(
        functools.partial(reduce_kernel, n_dp, n_seq),
        out_shape=[
            sds((D // n_dp, FF), BF),
            sds((D // n_dp, 4 * D), BF),
            sds((D, FF // n_dp), BF),
            sds((8, D), F32),
            sds((8, 128), F32),
        ],
        in_specs=[VM] * 4,
        out_specs=[VM] * 5,
        scratch_shapes=scratch,
        compiler_params=params(3),
        name="reduce_grads",
    )(gup, jnp.concatenate([gqkv, gout], axis=1), gdown, grow)

    masters = [w_qkv, w_out, w_up, w_down]
    firsts = [qkv_first, out_first, up_first, down_first, norm_first]
    seconds = [qkv_second, out_second, up_second, down_second, norm_second]
    shapes = [sds(w.shape, F32) for w in masters]
    norm_shape = sds(norm_first.shape, F32)
    updated = pl.pallas_call(
        functools.partial(adam_kernel, n_dp),
        out_shape=shapes
        + [norm_shape]
        + shapes
        + [norm_shape]
        + shapes
        + [norm_shape, sds((1, 1), F32)],
        in_specs=[VM] * 19,
        out_specs=[VM] * 16,
        compiler_params=params(),
        name="adam",
    )(sup, smix, sdown, srow, square, *masters, *firsts, *seconds)
    return (
        outputs.reshape(rows, local, D),
        input_grad,
        updated[15].reshape(()),
        *updated[0:15],
    )


def solution(mesh):
    tokens = P("dp", "seq", None)
    rows, stack, lanes = P("dp", None), P(None, "dp", None), P(None, "dp")
    moments = (stack, stack, rows, rows, rows, rows, rows, rows, lanes, lanes)
    weights = (stack, rows, rows, rows)
    return jax.shard_map(
        on_device,
        mesh=mesh,
        in_specs=(tokens, rows, tokens, *weights, lanes, *moments),
        out_specs=(tokens, tokens, P(), *weights, lanes, *weights, lanes, *weights, lanes),
        check_vma=False,
    )
```

```python
import functools
import math

import jax
import jax.numpy as jnp
from jax import lax
from jax.experimental import pallas as pl
from jax.experimental.pallas import tpu as pltpu
from jax.sharding import PartitionSpec as P

D = 512
HEADS = 8
DH = 64
FF = 2048
LEVELS = 7
DOCS = 4
QB = 128
NKEY = 512
PAIRS = HEADS // 2

masked_score = -1e30
beta_one = 0.9
beta_two = 0.999
bias_first = 1.0 - 0.9**10
bias_second = 1.0 - 0.999**10
learn_rate = 0.1
weight_decay = 0.1
epsilon = 1e-08
clip_norm = 1.0

BF = jnp.bfloat16
F32 = jnp.float32
MESH = pl.DeviceIdType.MESH
VM = pl.BlockSpec(memory_space=pltpu.VMEM)

NN = ((1,), (0,))
NT = ((1,), (1,))
TN = ((0,), (0,))


def mm(left, right, dims):
    return lax.dot_general(left, right, (dims, ((), ())), preferred_element_type=F32)


def params(cid=None):
    if cid is None:
        return pltpu.CompilerParams(vmem_limit_bytes=60 * 2**20)
    return pltpu.CompilerParams(
        vmem_limit_bytes=60 * 2**20, collective_id=cid, has_side_effects=True
    )


def sds(shape, dtype):
    return jax.ShapeDtypeStruct(shape, dtype)


def level_offset(local, level):
    return local - (local >> (level - 1))


def edge_levels(local):
    return [lv for lv in range(LEVELS) if (local >> lv) >= 16]


def far_levels(local):
    return [lv for lv in range(LEVELS) if (local >> lv) < 16]


def ext_rows(local, seq_len, level):
    return ((local >> level) if (local >> level) >= 16 else (seq_len >> level)) + 32


def key_rows(level):
    return max(QB >> level, 16) + 32


def key_start(level):
    return sum(key_rows(lv) for lv in range(level))


def window_start(level, block, offset, local):
    span = 16 << level
    if (local >> level) >= 16:
        if span <= QB:
            return block * (QB >> level)
        return (block * QB) // span * 16
    return (offset + block * QB) // span * 16


def averaging(local):
    row = lax.broadcasted_iota(jnp.int32, (local, local), 0)
    col = lax.broadcasted_iota(jnp.int32, (local, local), 1)
    total = jnp.zeros((local, local), F32)
    for lv in range(1, LEVELS):
        at = lax.shift_right_logical(col, lv) + level_offset(local, lv)
        total = jnp.where(at == row, 2.0**-lv, total)
    return total.astype(BF)


def norm_parts(values):
    center = jnp.mean(values, axis=-1, keepdims=True)
    centered = values - center
    spread = jnp.mean(centered * centered, axis=-1, keepdims=True)
    inverse = lax.rsqrt(spread + 1e-05)
    return centered * inverse, inverse


def norm_back(grad_in, normed, inverse, gain):
    scaled = grad_in * gain
    return inverse * (
        scaled
        - jnp.mean(scaled, axis=-1, keepdims=True)
        - normed * jnp.mean(scaled * normed, axis=-1, keepdims=True)
    )


def document_bounds(seg_row, seq_len):
    return [
        jnp.sum(jnp.where(seg_row < doc, 1.0, 0.0), axis=1, keepdims=True)
        for doc in range(1, DOCS)
    ]


def fill_bias(starts, first_query, seq_len, bias_ref):
    qpos = first_query + lax.broadcasted_iota(jnp.int32, (1, QB), 1)
    qf = qpos.astype(F32)
    low = jnp.zeros((1, QB), F32)
    high = jnp.full((1, QB), float(seq_len), F32)
    for start in starts:
        low = jnp.where(qf >= start, jnp.maximum(low, start), low)
        high = jnp.where(qf < start, jnp.minimum(high, start), high)
    for lv in range(LEVELS):
        span = 16 << lv
        rows = key_rows(lv)
        if span <= QB:
            key_first = first_query // (1 << lv) - 16
        else:
            key_first = first_query // span * 16 - 16
        index = key_first + lax.broadcasted_iota(jnp.int32, (rows, QB), 0)
        begin = (index * (1 << lv)).astype(F32)
        end = begin + float((1 << lv) - 1)
        block = lax.div(qpos, span)
        lo = jnp.maximum(low, ((block - 1) * span).astype(F32))
        hi = jnp.minimum(high, ((block + 2) * span).astype(F32))
        allowed = (begin >= lo) & (end < hi)
        if lv > 0:
            half = span // 2
            parent = lax.div(qpos, half)
            inner_lo = ((parent - 1) * half).astype(F32)
            inner_hi = ((parent + 2) * half).astype(F32)
            allowed = allowed & ((begin < inner_lo) | (begin >= inner_hi))
        bias_ref[key_start(lv) : key_start(lv) + rows, :] = jnp.where(
            allowed, lv * math.log(2.0), masked_score
        )


def build_ext(row, local, kv_ref, coarse_ref, edge_ref, far_ref, ext):
    count = far_ref.shape[1]
    for lv in range(LEVELS):
        rows = local >> lv
        if rows >= 16:
            ext[lv][0:16, :] = edge_ref[row, 0, 16 * lv : 16 * lv + 16, :]
            if lv == 0:
                ext[lv][16 : 16 + rows, :] = kv_ref[row]
            else:
                at = level_offset(local, lv)
                ext[lv][16 : 16 + rows, :] = coarse_ref[row, at : at + rows, :]
            ext[lv][16 + rows : 32 + rows, :] = edge_ref[row, 1, 16 * lv : 16 * lv + 16, :]
        else:
            at = level_offset(local, lv) - (local - 16)
            blank = jnp.zeros((16, 2 * D), F32)
            pieces = [blank]
            for owner in range(count):
                pieces.append(far_ref[row, owner].astype(F32)[at : at + rows, :])
            pieces.append(blank)
            ext[lv][...] = jnp.concatenate(pieces, axis=0).astype(BF)


def gather_keys(ext, block, offset, local, keys_ref):
    for lv in range(LEVELS):
        start = pl.multiple_of(window_start(lv, block, offset, local), 16)
        at = key_start(lv)
        keys_ref[at : at + key_rows(lv), :] = ext[lv][pl.ds(start, key_rows(lv)), :]


def lane_halves(values):
    lane = lax.broadcasted_iota(jnp.int32, values.shape, 1)
    zero = jnp.zeros_like(values)
    return jnp.concatenate(
        [jnp.where(lane < DH, values, zero), jnp.where(lane >= DH, values, zero)], axis=0
    )


def own_halves(pair_t):
    n = pair_t.shape[1] // 2
    sub = lax.broadcasted_iota(jnp.int32, (2 * DH, n), 0)
    return jnp.where(sub < DH, pair_t[:, :n], pair_t[:, n:])


def feed_kernel(
    x_ref,
    mixed_ref,
    og_ref,
    wout_ref,
    wup_ref,
    wdown_ref,
    norm_ref,
    out_ref,
    gres_ref,
    gmix_ref,
    gout_ref,
    gup_ref,
    gdown_ref,
    grow_ref,
    resid_s,
    second_s,
    second_t,
    og_t,
    acc_s,
    gsec_s,
    hid_s,
    gpre_s,
    low_s,
):
    tokens = x_ref.shape[0]
    tile = 256
    tiles = tokens // tile
    width = 512
    gain, shift = norm_ref[2:3, :], norm_ref[3:4, :]

    def rows_of(i):
        return pl.ds(pl.multiple_of(i * tile, tile), tile)

    def first(i, carry):
        part = rows_of(i)
        resid = x_ref[part, :].astype(F32) + mm(mixed_ref[part, :], wout_ref[...], NN)
        resid_s[part, :] = resid
        acc_s[part, :] = resid
        hat, _ = norm_parts(resid)
        second = (hat * gain + shift).astype(BF)
        second_s[part, :] = second
        second_t[:, part] = second.T
        og_t[:, part] = og_ref[part, :].T
        gsec_s[part, :] = jnp.zeros((tile, D), F32)
        return carry

    lax.fori_loop(0, tiles, first, 0)

    def chunk(f, carry):
        cols = pl.ds(pl.multiple_of(f * width, width), width)

        def inner(i, inner_carry):
            part = rows_of(i)
            pre = mm(second_s[part, :], wup_ref[:, cols], NN)
            square = pre * pre
            tangent = jnp.tanh(0.7978845608 * (pre + 0.044715 * pre * square))
            half = 0.5 + 0.5 * tangent
            hidden = (pre * half).astype(BF)
            slope = half + 0.5 * pre * (1.0 - tangent * tangent) * (
                0.7978845608 + 0.7978845608 * 3.0 * 0.044715 * square
            )
            grad_pre = (mm(og_ref[part, :], wdown_ref[cols, :], NT) * slope).astype(BF)
            hid_s[part, :] = hidden
            gpre_s[part, :] = grad_pre
            acc_s[part, :] += mm(hidden, wdown_ref[cols, :], NN)
            gsec_s[part, :] += mm(grad_pre, wup_ref[:, cols], NT)
            return inner_carry

        lax.fori_loop(0, tiles, inner, 0)
        gdown_ref[:, cols] = mm(og_t[...], hid_s[...], NN).astype(BF)
        gup_ref[:, cols] = mm(second_t[...], gpre_s[...], NN).astype(BF)
        return carry

    lax.fori_loop(0, FF // width, chunk, 0)
    grow_ref[...] = jnp.zeros_like(grow_ref)

    def last(i, carry):
        part = rows_of(i)
        out_ref[part, :] = acc_s[part, :].astype(BF)
        hat, inverse = norm_parts(resid_s[part, :])
        grad = gsec_s[part, :]
        gres = og_ref[part, :].astype(F32) + norm_back(grad, hat, inverse, gain)
        gres_ref[part, :] = gres
        low = gres.astype(BF)
        low_s[part, :] = low
        gmix_ref[part, :] = mm(low, wout_ref[...], NT).astype(BF)
        grow_ref[2:3, :] += jnp.sum(grad * hat, axis=0, keepdims=True)
        grow_ref[3:4, :] += jnp.sum(grad, axis=0, keepdims=True)
        return carry

    lax.fori_loop(0, tiles, last, 0)
    gout_ref[...] = mm(mixed_ref[...], low_s[...], TN).astype(BF)


def adam_kernel(n_dp, *refs):
    gup, gmix, gdown, small = refs[0:4]
    weights, firsts, seconds = refs[4:8], refs[8:13], refs[13:18]
    outs = refs[18:]
    new_w, norm_grad, new_m, new_s, grad_norm = (
        outs[0:4],
        outs[4],
        outs[5:10],
        outs[10:15],
        outs[15],
    )
    own = small[0:4, :]
    square = jnp.sum(jnp.sum(own * own, axis=0, keepdims=True), axis=1, keepdims=True)
    root = jnp.sqrt(square + small[4:5, 0:1])
    grad_norm[...] = root
    factor = jnp.minimum(1.0, clip_norm / root)

    def moments(clipped, first, second):
        return (
            beta_one * first + (1.0 - beta_one) * clipped,
            beta_two * second + (1.0 - beta_two) * clipped * clipped,
        )

    def update(weight, grad, first, second):
        mean, sq = moments(grad * factor, first, second)
        change = mean / bias_first / (jnp.sqrt(sq / bias_second) + epsilon) + weight_decay * weight
        return weight - learn_rate * change, mean, sq

    for c in range(3):
        w, m, s = update(
            weights[0][c], gmix[:, c * D : c * D + D].astype(F32), firsts[0][c], seconds[0][c]
        )
        new_w[0][c], new_m[0][c], new_s[0][c] = w, m, s
    for at, grad in ((1, gmix[:, 3 * D : 4 * D]), (2, gup[...]), (3, gdown[...])):
        grad = grad.astype(F32)
        if at == 3:
            grad = grad.T
        w, m, s = update(weights[at][...], grad, firsts[at][...], seconds[at][...])
        new_w[at][...], new_m[at][...], new_s[at][...] = w, m, s
    width = D // n_dp
    lane = lax.axis_index("dp") * width
    rolled = pltpu.roll(small[...], D - lane, 1)[0:4, 0:width]
    clipped = rolled * factor
    norm_grad[...] = clipped
    m, s = moments(clipped, firsts[4][...], seconds[4][...])
    new_m[4][...], new_s[4][...] = m, s


class Copies:
    def __init__(self, send, recv):
        self.send, self.recv = send, recv
        self.started = []

    def push(self, src, dst, send_at, recv_at, device):
        copy = pltpu.make_async_remote_copy(
            src_ref=src,
            dst_ref=dst,
            send_sem=self.send.at[send_at],
            recv_sem=self.recv.at[recv_at],
            device_id=device,
            device_id_type=MESH,
        )
        copy.start()
        self.started.append(copy)

    def arrived(self, dst, recv_at, device):
        pltpu.make_async_remote_copy(
            src_ref=dst,
            dst_ref=dst,
            send_sem=self.send.at[0],
            recv_sem=self.recv.at[recv_at],
            device_id=device,
            device_id_type=MESH,
        ).wait_recv()

    def finish(self):
        for copy in self.started:
            copy.wait_send()
        self.started = []


def greet(peers):
    barrier = pltpu.get_barrier_semaphore()
    for peer in peers:
        pl.semaphore_signal(barrier, inc=1, device_id=peer, device_id_type=MESH)
    pl.semaphore_wait(barrier, len(peers))


class Place:
    def __init__(self, n_dp, n_seq):
        self.n_dp, self.n_seq = n_dp, n_seq
        self.d, self.s = lax.axis_index("dp"), lax.axis_index("seq")
        self.z, self.y = lax.div(self.d, 2), lax.rem(self.d, 2)
        self.hi, self.core = lax.div(self.s, 2), lax.rem(self.s, 2)
        self.depth, self.high = n_dp // 2, n_seq // 2
        self.mate = self.s + 1 - 2 * self.core
        self.flip = self.d + 1 - 2 * self.y
        self.seq_others = [lax.rem(self.s + k, n_seq) for k in range(1, n_seq)]
        self.dp_others = [lax.rem(self.d + k, n_dp) for k in range(1, n_dp)]

    def greet(self):
        greet(
            [(self.d, o) for o in self.seq_others] + [(o, self.s) for o in self.dp_others]
        )


class Gather:
    def __init__(self, place, parts, copies, base):
        self.at, self.parts, self.copies, self.base = place, parts, copies, base
        self.stride = self.sems(place.n_dp, place.n_seq)

    @staticmethod
    def sems(n_dp, n_seq):
        return 2 * (n_dp // 2) + n_dp * n_seq

    def split(self, p):
        high = self.at.high
        return p >= 3 and high > 1 and self.parts[p][3] % (32 * high) == 0

    def piece(self, p, shard, core, hi):
        _, whole, lead, rows = self.parts[p]
        n = rows // 2
        start = shard * rows + core * n
        if self.split(p):
            n = n // self.at.high
            start = start + hi * n
        start = pl.multiple_of(start, n)
        if lead is None:
            return whole.at[pl.ds(start, n), :]
        return whole.at[lead[0] : lead[1], pl.ds(start, n), :]

    def sem(self, p, stage, index):
        at = self.base + p * self.stride
        sizes = (self.at.depth, self.at.depth, self.at.n_dp * self.at.high)
        return at + sum(sizes[:stage]) + index

    def load(self, p):
        own, whole, lead, rows = self.parts[p]
        start = pl.multiple_of(self.at.d * rows, rows)
        if lead is None:
            whole[pl.ds(start, rows), :] = own[...].astype(BF)
        else:
            whole[lead[0] : lead[1], pl.ds(start, rows), :] = own[lead[0] : lead[1]].astype(BF)

    def start(self, p):
        me = self.at
        self.load(p)
        mine = self.piece(p, me.d, me.core, me.hi)
        for k in range(1, me.depth):
            other = lax.rem(me.z + k, me.depth) * 2 + me.y
            self.copies.push(mine, mine, self.sem(p, 0, k), self.sem(p, 0, me.z), (other, me.s))
        self.copies.push(mine, mine, self.sem(p, 1, 0), self.sem(p, 1, me.z), (me.flip, me.s))

    def onward(self, p, shard, k):
        me = self.at
        here = self.piece(p, shard, me.core, me.hi)
        if self.split(p):
            for kh in range(1, me.high):
                other = lax.rem(me.hi + kh, me.high) * 2 + me.core
                self.copies.push(
                    here,
                    here,
                    self.sem(p, 2, kh * me.n_dp + k),
                    self.sem(p, 2, me.hi * me.n_dp + shard),
                    (me.d, other),
                )
            which = me.hi
        else:
            which = 0
        self.copies.push(
            here, here, self.sem(p, 3, k), self.sem(p, 3, which * me.n_dp + shard), (me.d, me.mate)
        )

    def relay_z(self, p):
        me = self.at
        for k in range(1, me.depth):
            zz = lax.rem(me.z + k, me.depth)
            shard = zz * 2 + me.y
            here = self.piece(p, shard, me.core, me.hi)
            self.copies.arrived(here, self.sem(p, 0, zz), (shard, me.s))
            self.copies.push(
                here, here, self.sem(p, 1, k), self.sem(p, 1, zz), (me.flip, me.s)
            )
            self.onward(p, shard, k)

    def relay_y(self, p):
        me = self.at
        for k in range(me.depth):
            zz = lax.rem(me.z + k, me.depth)
            shard = zz * 2 + 1 - me.y
            here = self.piece(p, shard, me.core, me.hi)
            self.copies.arrived(here, self.sem(p, 1, zz), (me.flip, me.s))
            self.onward(p, shard, me.depth + k)

    def relay_x(self, p):
        me = self.at
        if not self.split(p):
            return
        for kh in range(1, me.high):
            h = lax.rem(me.hi + kh, me.high)
            for k in range(1, me.n_dp):
                shard = lax.rem(me.d + k, me.n_dp)
                here = self.piece(p, shard, me.core, h)
                self.copies.arrived(
                    here, self.sem(p, 2, h * me.n_dp + shard), (me.d, h * 2 + me.core)
                )
                self.copies.push(
                    here,
                    here,
                    self.sem(p, 3, kh * me.n_dp + k),
                    self.sem(p, 3, h * me.n_dp + shard),
                    (me.d, me.mate),
                )

    def settle(self, p):
        me = self.at
        for h in range(me.high if self.split(p) else 1):
            for k in range(1, me.n_dp):
                shard = lax.rem(me.d + k, me.n_dp)
                self.copies.arrived(
                    self.piece(p, shard, 1 - me.core, h),
                    self.sem(p, 3, h * me.n_dp + shard),
                    (me.d, me.mate),
                )


class Exchange:
    def __init__(self, place, personal, edge_in, far_in, edge_out, far_out, send, recv):
        self.at, self.personal = place, personal
        self.edge_in, self.far_in, self.edge_out, self.far_out = edge_in, far_in, edge_out, far_out
        self.send, self.recv = send, recv

    @staticmethod
    def sems(rows, n_seq):
        return rows * (2 + n_seq)

    def edge(self, row, way, device):
        base = row * (2 + self.at.n_seq)
        return pltpu.make_async_remote_copy(
            src_ref=self.edge_in.at[row, way],
            dst_ref=self.edge_out.at[row, 1 - way],
            send_sem=self.send.at[base + way],
            recv_sem=self.recv.at[base + 1 - way],
            device_id=(self.at.d, device),
            device_id_type=MESH,
        )

    def far(self, row, k, other):
        base = row * (2 + self.at.n_seq) + 2
        return pltpu.make_async_remote_copy(
            src_ref=self.far_in.at[row, other] if self.personal else self.far_in.at[row],
            dst_ref=self.far_out.at[row, self.at.s],
            send_sem=self.send.at[base + k],
            recv_sem=self.recv.at[base + self.at.s],
            device_id=(self.at.d, other),
            device_id_type=MESH,
        )

    def start(self, row):
        s, n_seq = self.at.s, self.at.n_seq

        @pl.when(s > 0)
        def _():
            self.edge(row, 0, s - 1).start()

        @pl.when(s < n_seq - 1)
        def _():
            self.edge(row, 1, s + 1).start()

        for k, other in enumerate(self.at.seq_others):
            self.far(row, k, other).start()
        self.far_out[row, s] = self.far_in[row, s] if self.personal else self.far_in[row]

    def arrive(self, row):
        s, n_seq = self.at.s, self.at.n_seq
        blank = jnp.zeros(self.edge_out.shape[2:], BF)

        @pl.when(s > 0)
        def _():
            self.edge(row, 1, s - 1).wait_recv()

        @pl.when(s == 0)
        def _():
            self.edge_out[row, 0] = blank

        @pl.when(s < n_seq - 1)
        def _():
            self.edge(row, 0, s + 1).wait_recv()

        @pl.when(s == n_seq - 1)
        def _():
            self.edge_out[row, 1] = blank

        base = row * (2 + n_seq) + 2
        for other in self.at.seq_others:
            here = self.far_out.at[row, other]
            pltpu.make_async_remote_copy(
                src_ref=here,
                dst_ref=here,
                send_sem=self.send.at[base],
                recv_sem=self.recv.at[base + other],
                device_id=(self.at.d, other),
                device_id_type=MESH,
            ).wait_recv()

    def finish(self, row):
        s, n_seq = self.at.s, self.at.n_seq

        @pl.when(s > 0)
        def _():
            self.edge(row, 0, s - 1).wait_send()

        @pl.when(s < n_seq - 1)
        def _():
            self.edge(row, 1, s + 1).wait_send()

        for k, other in enumerate(self.at.seq_others):
            self.far(row, k, other).wait_send()


def grad_parts(n_dp, n_seq):
    parts = [(0, 0, FF, True, True), (1, 0, FF, False, False)]
    if D // n_seq % 128:
        return parts + [(2, 0, 4 * D, True, True)]
    parts.append((2, 3 * D, 4 * D, True, True))
    parts += [(2, c * D, c * D + D, True, c % 2 == 1) for c in range(3)]
    return parts


def block_shape(part, n_dp, n_seq):
    _, lo, hi, by_rows, _ = part
    if by_rows:
        return (D // n_dp, (hi - lo) // n_seq)
    return (D // n_seq, (hi - lo) // n_dp)


class Reduce:
    def __init__(self, place, sources, finals, buffers, copies, base):
        self.at, self.sources, self.finals = place, sources, finals
        self.parts = grad_parts(place.n_dp, place.n_seq)
        n = len(self.parts)
        groups = [buffers[i * n : i * n + n] for i in range(5)]
        self.core_in, self.held, self.high_in, self.y_in, self.z_in = groups
        self.copies, self.base = copies, base
        self.stride = self.sems(place.n_dp, place.n_seq)

    @staticmethod
    def sems(n_dp, n_seq):
        return 2 + n_seq // 2 + n_dp // 2 + n_seq

    @staticmethod
    def scratch(n_dp, n_seq):
        high, depth = n_seq // 2, n_dp // 2
        groups = [[], [], [], [], []]
        for part in grad_parts(n_dp, n_seq):
            _, lo, up, by_rows, first = part
            a, b = block_shape(part, n_dp, n_seq)
            shapes = [
                (D, (up - lo) // 2) if by_rows else (D // 2, up - lo),
                (high, depth, 2, a, b),
                (high, depth, 2, a, b) if first else (high, depth, a, b),
                (depth, a, b) if first else (high, depth, a, b),
                (depth, a, b),
            ]
            for group, shape in zip(groups, shapes):
                group.append(pltpu.VMEM(shape, BF))
        return [item for group in groups for item in group]

    def sem(self, p, stage, index=0):
        sizes = (1, 1, self.at.high, self.at.depth, self.at.n_seq)
        return self.base + p * self.stride + sum(sizes[:stage]) + index

    def start(self, p):
        me = self.at
        src, lo, up, by_rows, _ = self.parts[p]
        ref = self.sources[src]
        which = 1 - me.core
        if by_rows:
            w = (up - lo) // 2
            half = ref.at[:, pl.ds(pl.multiple_of(lo + which * w, 128), w)]
        else:
            w = D // 2
            half = ref.at[pl.ds(pl.multiple_of(which * w, w), w), lo:up]
        self.copies.push(half, self.core_in[p], self.sem(p, 0), self.sem(p, 0), (me.d, me.mate))

    def push_y(self, p, held):
        me = self.at
        self.copies.push(held, self.y_in[p], self.sem(p, 1), self.sem(p, 1), (me.flip, me.s))

    def take_y(self, p):
        me = self.at
        self.copies.arrived(self.y_in[p], self.sem(p, 1), (me.flip, me.s))

    def push_high(self, p, y):
        me = self.at
        for k in range(1, me.high):
            h = lax.rem(me.hi + k, me.high)
            src = self.held[p].at[h] if y is None else self.held[p].at[h, :, y]
            self.copies.push(
                src,
                self.high_in[p].at[me.hi],
                self.sem(p, 2, k),
                self.sem(p, 2, me.hi),
                (me.d, h * 2 + me.core),
            )

    def take_high(self, p):
        me = self.at
        for k in range(1, me.high):
            h = lax.rem(me.hi + k, me.high)
            self.copies.arrived(
                self.high_in[p].at[h], self.sem(p, 2, h), (me.d, h * 2 + me.core)
            )

    def combine(self, p):
        me = self.at
        part = self.parts[p]
        src, lo, up, by_rows, first = part
        a, b = block_shape(part, me.n_dp, me.n_seq)
        self.copies.arrived(self.core_in[p], self.sem(p, 0), (me.d, me.mate))
        theirs, held = self.core_in[p], self.held[p]
        for h in range(me.high):
            for shard in range(me.n_dp):
                if by_rows:
                    r = slice(shard * a, shard * a + a)
                    own = pl.ds(pl.multiple_of(lo + (me.core * me.high + h) * b, 128), b)
                    left = self.sources[src][r, own]
                    right = theirs[r, h * b : h * b + b]
                else:
                    r = pl.ds(pl.multiple_of((me.core * me.high + h) * a, a), a)
                    left = self.sources[src][r, lo + shard * b : lo + shard * b + b]
                    right = theirs[h * a : h * a + a, shard * b : shard * b + b]
                total = left.astype(F32) + right.astype(F32)
                held[h, shard // 2, shard % 2] = total.astype(BF)
        if first:
            self.push_high(p, None)
        else:
            self.push_y(p, held.at[:, :, 1 - me.y])

    def second(self, p):
        me = self.at
        held = self.held[p]
        if self.parts[p][4]:
            self.take_high(p)
            for zz in range(me.depth):
                for yy in range(2):
                    value = held[me.hi, zz, yy].astype(F32)
                    for k in range(1, me.high):
                        value += self.high_in[p][lax.rem(me.hi + k, me.high), zz, yy].astype(F32)
                    held[me.hi, zz, yy] = value.astype(BF)
            self.push_y(p, held.at[me.hi, :, 1 - me.y])
        else:
            self.take_y(p)
            for h in range(me.high):
                for zz in range(me.depth):
                    value = held[h, zz, me.y].astype(F32) + self.y_in[p][h, zz].astype(F32)
                    held[h, zz, me.y] = value.astype(BF)
            self.push_high(p, me.y)

    def third(self, p):
        me = self.at
        held = self.held[p]
        if self.parts[p][4]:
            self.take_y(p)
            for zz in range(me.depth):
                value = held[me.hi, zz, me.y].astype(F32) + self.y_in[p][zz].astype(F32)
                held[me.hi, zz, me.y] = value.astype(BF)
        else:
            self.take_high(p)
            for zz in range(me.depth):
                value = held[me.hi, zz, me.y].astype(F32)
                for k in range(1, me.high):
                    value += self.high_in[p][lax.rem(me.hi + k, me.high), zz].astype(F32)
                held[me.hi, zz, me.y] = value.astype(BF)
        for k in range(1, me.depth):
            zz = lax.rem(me.z + k, me.depth)
            self.copies.push(
                held.at[me.hi, zz, me.y],
                self.z_in[p].at[me.z],
                self.sem(p, 3, k),
                self.sem(p, 3, me.z),
                (zz * 2 + me.y, me.s),
            )

    def place_of(self, p, owner):
        part = self.parts[p]
        src, lo, up, by_rows, _ = part
        a, b = block_shape(part, self.at.n_dp, self.at.n_seq)
        which = lax.rem(owner, 2) * self.at.high + lax.div(owner, 2)
        if by_rows:
            return self.finals[src].at[:, pl.ds(pl.multiple_of(lo + which * b, 128), b)]
        return self.finals[src].at[pl.ds(pl.multiple_of(which * a, a), a), :]

    def final(self, p):
        me = self.at
        for k in range(1, me.depth):
            zz = lax.rem(me.z + k, me.depth)
            self.copies.arrived(self.z_in[p].at[zz], self.sem(p, 3, zz), (zz * 2 + me.y, me.s))
        value = self.held[p][me.hi, me.z, me.y].astype(F32)
        for k in range(1, me.depth):
            value += self.z_in[p][lax.rem(me.z + k, me.depth)].astype(F32)
        low = value.astype(BF)
        here = self.place_of(p, me.s)
        here[...] = low
        for k, o in enumerate(me.seq_others):
            self.copies.push(here, here, self.sem(p, 4, 1 + k), self.sem(p, 4, me.s), (me.d, o))
        value = low.astype(F32)
        return jnp.sum(jnp.sum(value * value, axis=0, keepdims=True), axis=1, keepdims=True)

    def settle(self, p):
        me = self.at
        for o in me.seq_others:
            self.copies.arrived(self.place_of(p, o), self.sem(p, 4, o), (me.d, o))


def front_kernel(
    n_dp,
    n_seq,
    x_ref,
    wqkv,
    wout,
    wup,
    wdown,
    norm,
    seg_ref,
    fqkv,
    fout,
    fup,
    fdown,
    norm_ref,
    normed_ref,
    q_ref,
    kv_ref,
    coarse_ref,
    edge_near,
    far_all,
    mixed_ref,
    total_ref,
    slots,
    edge_own,
    far_own,
    keys,
    bias,
    *rest,
):
    ext, (send, recv, edge_send, edge_recv) = rest[:LEVELS], rest[LEVELS:]
    rows, local = x_ref.shape[0], x_ref.shape[1]
    seq_len = seg_ref.shape[1]
    me = Place(n_dp, n_seq)
    me.greet()
    copies = Copies(send, recv)
    shard = D // n_dp
    gather = Gather(
        me,
        [
            (wqkv, fqkv, (1, 3), shard),
            (wqkv, fqkv, (0, 1), shard),
            (wout, fout, None, shard),
            (wup, fup, None, shard),
            (wdown, fdown, None, FF // n_dp),
        ],
        copies,
        n_dp,
    )
    KV, Q, OUT, UP, DOWN = range(5)
    exchange = Exchange(me, False, edge_own, far_own, edge_near, far_all, edge_send, edge_recv)

    slots[me.d] = norm[...].astype(BF).astype(F32)
    for k, o in enumerate(me.dp_others):
        copies.push(slots.at[me.d], slots.at[me.d], 1 + k, me.d, (o, me.s))
    gather.start(KV)
    gather.start(Q)
    mean_of = averaging(local)
    for o in me.dp_others:
        copies.arrived(slots.at[o], o, (o, me.s))
    total = jnp.zeros((8, D), F32)
    for at in range(n_dp):
        i = lax.broadcasted_iota(jnp.int32, (128, D), 0)
        j = lax.broadcasted_iota(jnp.int32, (128, D), 1)
        pick = jnp.where((j == i + at * shard) & (i < shard), 1.0, 0.0).astype(BF)
        total += mm(slots[at].astype(BF), pick, NN)
    norm_ref[...] = total

    tile = min(local, 256)
    tiles = local // tile

    def normalize(i, carry):
        row, part = lax.div(i, tiles), pl.ds(pl.multiple_of(lax.rem(i, tiles) * tile, tile), tile)
        hat, _ = norm_parts(x_ref[row, part, :].astype(F32))
        normed_ref[row, part, :] = (hat * norm_ref[0:1, :] + norm_ref[1:2, :]).astype(BF)
        return carry

    lax.fori_loop(0, rows * tiles, normalize, 0)
    gather.relay_z(KV)
    gather.relay_z(Q)
    gather.start(OUT)
    gather.start(UP)
    gather.relay_y(KV)
    gather.relay_y(Q)
    gather.start(DOWN)
    gather.settle(KV)
    for row in range(rows):

        def project_kv(i, carry):
            part = pl.ds(pl.multiple_of(i * tile, tile), tile)
            low = normed_ref[row, part, :]
            kv_ref[row, part, 0:D] = mm(low, fqkv[1], NN).astype(BF)
            kv_ref[row, part, D : 2 * D] = mm(low, fqkv[2], NN).astype(BF)
            return carry

        lax.fori_loop(0, tiles, project_kv, 0)
        coarse_ref[row] = mm(mean_of, kv_ref[row], NN).astype(BF)
        for lv in edge_levels(local):
            n = local >> lv
            to = slice(16 * lv, 16 * lv + 16)
            if lv == 0:
                edge_own[row, 0, to, :] = kv_ref[row, 0:16, :]
                edge_own[row, 1, to, :] = kv_ref[row, n - 16 : n, :]
            else:
                at = level_offset(local, lv)
                edge_own[row, 0, to, :] = coarse_ref[row, at : at + 16, :]
                edge_own[row, 1, to, :] = coarse_ref[row, at + n - 16 : at + n, :]
        far_own[row] = coarse_ref[row, local - 16 : local, :]
        exchange.start(row)
    gather.settle(Q)

    def project_q(i, carry):
        row, part = lax.div(i, tiles), pl.ds(pl.multiple_of(lax.rem(i, tiles) * tile, tile), tile)
        q_ref[row, part, :] = mm(normed_ref[row, part, :], fqkv[0], NN).astype(BF)
        return carry

    lax.fori_loop(0, rows * tiles, project_q, 0)
    gather.relay_z(OUT)
    gather.relay_z(UP)

    offset = me.s * local
    blocks = local // QB
    for row in range(rows):
        exchange.arrive(row)
        build_ext(row, local, kv_ref, coarse_ref, edge_near, far_all, ext)
        starts = document_bounds(seg_ref[row : row + 1, :], seq_len)

        def step(block, carry):
            gather_keys(ext, block, offset, local, keys)
            fill_bias(starts, offset + block * QB, seq_len, bias)
            part = pl.ds(pl.multiple_of(block * QB, QB), QB)
            both = jnp.concatenate([bias[...], bias[...]], axis=1)
            for pair in range(PAIRS):
                lanes = slice(128 * pair, 128 * pair + 128)
                queries = lane_halves(q_ref[row, part, lanes] * BF(DH**-0.5))
                scores = mm(keys[:, lanes], queries, NT) + both
                peak = jnp.max(scores, axis=0, keepdims=True)
                weights = jnp.exp(scores - peak)
                denominator = jnp.sum(weights, axis=0, keepdims=True)
                total_ref[row, block, pair : pair + 1, :] = peak + jnp.log(denominator)
                values = keys[:, D + 128 * pair : D + 128 * pair + 128]
                mixed_t = mm(values, weights.astype(BF), TN) / denominator
                mixed_ref[row, part, lanes] = own_halves(mixed_t).T.astype(BF)
            return carry

        half = blocks // 2
        lax.fori_loop(0, half, step, 0)
        if row == 0:
            gather.relay_z(DOWN)
            gather.relay_y(OUT)
            gather.relay_y(UP)
        if row == rows - 1:
            gather.relay_x(UP)
        lax.fori_loop(half, blocks, step, 0)
        if row == 0:
            gather.relay_y(DOWN)
    gather.relay_x(DOWN)
    for p in (OUT, UP, DOWN):
        gather.settle(p)
    for row in range(rows):
        exchange.finish(row)
    copies.finish()


def back_kernel(
    n_dp,
    n_seq,
    x_ref,
    normed_ref,
    w_ref,
    norm_ref,
    gres_ref,
    q_ref,
    kv_ref,
    coarse_ref,
    edge_ref,
    far_ref,
    seg_ref,
    total_ref,
    gmix_ref,
    gup,
    gdown,
    gout,
    grow_in,
    ginput_ref,
    sup,
    smix,
    sdown,
    small,
    keys,
    bias,
    gkeys,
    gq_s,
    gkv_s,
    gcoarse_s,
    gedge,
    gfar,
    gedge_in,
    gfar_in,
    coarse_s,
    pair_s,
    normed_t,
    gmixed,
    grow,
    small_seq,
    small_dp,
    *rest,
):
    ext, gext, buffers = rest[:LEVELS], rest[LEVELS : 2 * LEVELS], rest[2 * LEVELS : -4]
    send, recv, edge_send, edge_recv = rest[-4:]
    rows, local = x_ref.shape[0], x_ref.shape[1]
    seq_len = seg_ref.shape[1]
    me = Place(n_dp, n_seq)
    me.greet()
    copies = Copies(send, recv)
    reduce = Reduce(me, (gup, gdown, gmixed), (sup, sdown, smix), buffers, copies, n_dp + n_seq)
    parts = len(reduce.parts)
    early = [0, 1] + ([2] if parts > 3 else [])
    late = [p for p in range(parts) if p not in early]
    exchange = Exchange(me, True, gedge, gfar, gedge_in, gfar_in, edge_send, edge_recv)

    gmixed[:, 3 * D : 4 * D] = gout[...]
    for p in early:
        reduce.start(p)
    grow[...] = grow_in[...]

    offset = me.s * local
    blocks = local // QB
    half = blocks // 2
    for row in range(rows):
        build_ext(row, local, kv_ref, coarse_ref, edge_ref, far_ref, ext)
        starts = document_bounds(seg_ref[row : row + 1, :], seq_len)
        for item in gext:
            item[...] = jnp.zeros_like(item)

        def step(block, carry):
            gather_keys(ext, block, offset, local, keys)
            fill_bias(starts, offset + block * QB, seq_len, bias)
            part = pl.ds(pl.multiple_of(block * QB, QB), QB)
            both = jnp.concatenate([bias[...], bias[...]], axis=1)
            for pair in range(PAIRS):
                lanes = slice(128 * pair, 128 * pair + 128)
                vlanes = slice(D + 128 * pair, D + 128 * pair + 128)
                queries = lane_halves(q_ref[row, part, lanes] * BF(DH**-0.5))
                grads = lane_halves(gmix_ref[row, part, lanes])
                scores = mm(keys[:, lanes], queries, NT) + both
                soft = jnp.exp(scores - total_ref[row, block, pair : pair + 1, :])
                gsoft = mm(keys[:, vlanes], grads, NT)
                row_total = jnp.sum(soft * gsoft, axis=0, keepdims=True)
                gscore = (soft * (gsoft - row_total)).astype(BF)
                gkeys[:, lanes] = mm(gscore, queries, NN)
                gkeys[:, vlanes] = mm(soft.astype(BF), grads, NN)
                gq_t = own_halves(mm(keys[:, lanes], gscore, TN)) * DH**-0.5
                gq_s[row, part, lanes] = gq_t.T.astype(BF)
            for lv in range(LEVELS):
                start = pl.multiple_of(window_start(lv, block, offset, local), 16)
                at = key_start(lv)
                gext[lv][pl.ds(start, key_rows(lv)), :] += gkeys[at : at + key_rows(lv), :]
            return carry

        lax.fori_loop(0, half, step, 0)
        for p in early:
            if row == 0:
                reduce.combine(p)
            if row == rows - 1:
                reduce.third(p)
        lax.fori_loop(half, blocks, step, 0)
        if row == 0:
            for p in early:
                reduce.second(p)
        gkv_s[row] = gext[0][16 : 16 + local, :]
        for lv in edge_levels(local):
            n = local >> lv
            to = slice(16 * lv, 16 * lv + 16)
            if lv > 0:
                at = level_offset(local, lv)
                gcoarse_s[row, at : at + n, :] = gext[lv][16 : 16 + n, :]
            gedge[row, 0, to, :] = gext[lv][0:16, :].astype(BF)
            gedge[row, 1, to, :] = gext[lv][16 + n : 32 + n, :].astype(BF)
        for owner in range(n_seq):
            pieces = []
            used = 0
            for lv in far_levels(local):
                n = local >> lv
                pieces.append(gext[lv][16 + owner * n : 16 + owner * n + n, :])
                used += n
            pieces.append(jnp.zeros((16 - used, 2 * D), F32))
            gfar[row, owner] = jnp.concatenate(pieces, axis=0).astype(BF)
        exchange.start(row)

    tile = min(local, 256)
    spans = [
        (row, slice(at, at + tile), slice(row * local + at, row * local + at + tile))
        for row in range(rows)
        for at in range(0, local, tile)
    ]
    for row, span, where in spans:
        normed_t[:, where] = normed_ref[row, span, :].T
    flat_q = gq_s[...].reshape(rows * local, D)
    gmixed[:, 0:D] = mm(normed_t[...], flat_q, NN).astype(BF)
    if len(late) > 1:
        reduce.start(late[0])
    square = jnp.zeros((1, 1), F32)
    for p in early:
        square += reduce.final(p)
    spread_of = averaging(local)
    for row in range(rows):
        exchange.arrive(row)
        for lv in edge_levels(local):
            n = local >> lv
            near = gedge_in[row, 0, 16 * lv : 16 * lv + 16, :].astype(F32)
            after = gedge_in[row, 1, 16 * lv : 16 * lv + 16, :].astype(F32)
            if lv == 0:
                gkv_s[row, 0:16, :] += near
                gkv_s[row, n - 16 : n, :] += after
            else:
                at = level_offset(local, lv)
                gcoarse_s[row, at : at + 16, :] += near
                gcoarse_s[row, at + n - 16 : at + n, :] += after
        total = gfar_in[row, 0].astype(F32)
        for owner in range(1, n_seq):
            total += gfar_in[row, owner].astype(F32)
        gcoarse_s[row, local - 16 : local, :] = total
        coarse_s[...] = gcoarse_s[row].astype(BF)
        for of, span, where in spans:
            if of == row:
                pair_s[where, :] = (
                    gkv_s[row, span, :] + mm(spread_of[:, span], coarse_s[...], TN)
                ).astype(BF)
    if len(late) > 1:
        reduce.combine(late[0])
    for c in (0, 1):
        lanes = slice(c * D, c * D + D)
        gmixed[:, D + c * D : 2 * D + c * D] = mm(normed_t[...], pair_s[:, lanes], NN).astype(BF)
        if len(late) > 1:
            reduce.start(late[1 + c])
    if len(late) == 1:
        reduce.start(late[0])

    def settle_inputs(row, span, where):
        gnormed = (
            mm(gq_s[row, span, :], w_ref[0], NT)
            + mm(pair_s[where, 0:D], w_ref[1], NT)
            + mm(pair_s[where, D : 2 * D], w_ref[2], NT)
        )
        hat, inverse = norm_parts(x_ref[row, span, :].astype(F32))
        ginput_ref[row, span, :] = gres_ref[row, span, :] + norm_back(
            gnormed, hat, inverse, norm_ref[0:1, :]
        )
        grow[0:1, :] += jnp.sum(gnormed * hat, axis=0, keepdims=True)
        grow[1:2, :] += jnp.sum(gnormed, axis=0, keepdims=True)

    actions = []
    if len(late) > 1:
        actions = [
            lambda: (reduce.second(late[0]), [reduce.combine(p) for p in late[1:]]),
            lambda: (reduce.third(late[0]), [reduce.second(p) for p in late[1:]]),
            lambda: [reduce.third(p) for p in late[1:]],
        ]
    else:
        actions = [
            lambda: reduce.combine(late[0]),
            lambda: reduce.second(late[0]),
            lambda: reduce.third(late[0]),
        ]
    for at in range(max(len(spans), len(actions))):
        if at < len(spans):
            settle_inputs(*spans[at])
        if at < len(actions):
            actions[at]()
    for p in late:
        square += reduce.final(p)
    grow[4:5, :] = jnp.broadcast_to(square, (1, D))
    small_seq[me.s] = grow[...]
    for k, o in enumerate(me.seq_others):
        copies.push(grow, small_seq.at[me.s], n_dp + 1 + k, n_dp + me.s, (me.d, o))
    for o in me.seq_others:
        copies.arrived(small_seq.at[o], n_dp + o, (me.d, o))
    total = small_seq[0]
    for o in range(1, n_seq):
        total += small_seq[o]
    small_dp[me.d] = total
    for k, o in enumerate(me.dp_others):
        copies.push(small_dp.at[me.d], small_dp.at[me.d], 1 + k, me.d, (o, me.s))
    for p in range(parts):
        reduce.settle(p)
    for o in me.dp_others:
        copies.arrived(small_dp.at[o], o, (o, me.s))
    total = small_dp[0]
    for o in range(1, n_dp):
        total += small_dp[o]
    small[...] = total
    for row in range(rows):
        exchange.finish(row)
    copies.finish()


def on_device(
    inputs,
    segment_ids,
    out_grad,
    w_qkv,
    w_out,
    w_up,
    w_down,
    norm_params,
    qkv_first,
    qkv_second,
    out_first,
    out_second,
    up_first,
    up_second,
    down_first,
    down_second,
    norm_first,
    norm_second,
):
    n_dp, n_seq = lax.axis_size("dp"), lax.axis_size("seq")
    rows, local = inputs.shape[0], inputs.shape[1]
    seq_len = segment_ids.shape[1]
    tokens = rows * local
    dma = pltpu.SemaphoreType.DMA
    edge = 16 * len(edge_levels(local))
    blocks = local // QB
    ext_shapes = [(ext_rows(local, seq_len, lv), 2 * D) for lv in range(LEVELS)]
    ext_low = [pltpu.VMEM(shape, BF) for shape in ext_shapes]
    ext_wide = [pltpu.VMEM(shape, F32) for shape in ext_shapes]
    edge_shape, far_shape = (rows, 2, edge, 2 * D), (rows, n_seq, 16, 2 * D)
    edge_sems = Exchange.sems(rows, n_seq)

    norm_pad = jnp.pad(norm_params, ((0, 4), (0, 128 - norm_params.shape[1])))
    sems = n_dp + 5 * Gather.sems(n_dp, n_seq)
    fqkv, fout, fup, fdown, fnorm, normed, q, kv, coarse, edge_near, far_all, mixed, totals = (
        pl.pallas_call(
            functools.partial(front_kernel, n_dp, n_seq),
            out_shape=[
                sds((3, D, D), BF),
                sds((D, D), BF),
                sds((D, FF), BF),
                sds((FF, D), BF),
                sds((8, D), F32),
                sds((rows, local, D), BF),
                sds((rows, local, D), BF),
                sds((rows, local, 2 * D), BF),
                sds((rows, local, 2 * D), BF),
                sds(edge_shape, BF),
                sds(far_shape, BF),
                sds((rows, local, D), BF),
                sds((rows, blocks, PAIRS, 2 * QB), F32),
            ],
            in_specs=[VM] * 7,
            out_specs=[VM] * 13,
            scratch_shapes=[
                pltpu.VMEM((n_dp, 8, 128), F32),
                pltpu.VMEM(edge_shape, BF),
                pltpu.VMEM((rows, 16, 2 * D), BF),
                pltpu.VMEM((NKEY, 2 * D), BF),
                pltpu.VMEM((NKEY, QB), F32),
                *ext_low,
                dma((sems,)),
                dma((sems,)),
                dma((edge_sems,)),
                dma((edge_sems,)),
            ],
            compiler_params=params(0),
            name="front",
        )(inputs, w_qkv, w_out, w_up, w_down, norm_pad, segment_ids)
    )

    outputs, gres, gmixed, gout, gup, gdown, grow = pl.pallas_call(
        feed_kernel,
        out_shape=[
            sds((tokens, D), BF),
            sds((tokens, D), F32),
            sds((tokens, D), BF),
            sds((D, D), BF),
            sds((D, FF), BF),
            sds((D, FF), BF),
            sds((8, D), F32),
        ],
        in_specs=[VM] * 7,
        out_specs=[VM] * 7,
        scratch_shapes=[
            pltpu.VMEM((tokens, D), F32),
            pltpu.VMEM((tokens, D), BF),
            pltpu.VMEM((D, tokens), BF),
            pltpu.VMEM((D, tokens), BF),
            pltpu.VMEM((tokens, D), F32),
            pltpu.VMEM((tokens, D), F32),
            pltpu.VMEM((tokens, 512), BF),
            pltpu.VMEM((tokens, 512), BF),
            pltpu.VMEM((tokens, D), BF),
        ],
        compiler_params=params(),
        name="feed",
    )(
        inputs.reshape(tokens, D),
        mixed.reshape(tokens, D),
        out_grad.reshape(tokens, D),
        fout,
        fup,
        fdown,
        fnorm,
    )

    parts = len(grad_parts(n_dp, n_seq))
    sems = n_dp + n_seq + parts * Reduce.sems(n_dp, n_seq)
    input_grad, sup, smix, sdown, small = pl.pallas_call(
        functools.partial(back_kernel, n_dp, n_seq),
        out_shape=[
            sds((rows, local, D), F32),
            sds((D // n_dp, FF), BF),
            sds((D // n_dp, 4 * D), BF),
            sds((D, FF // n_dp), BF),
            sds((8, D), F32),
        ],
        in_specs=[VM] * 17,
        out_specs=[VM] * 5,
        scratch_shapes=[
            pltpu.VMEM((NKEY, 2 * D), BF),
            pltpu.VMEM((NKEY, QB), F32),
            pltpu.VMEM((NKEY, 2 * D), F32),
            pltpu.VMEM((rows, local, D), BF),
            pltpu.VMEM((rows, local, 2 * D), F32),
            pltpu.VMEM((rows, local, 2 * D), F32),
            pltpu.VMEM(edge_shape, BF),
            pltpu.VMEM(far_shape, BF),
            pltpu.VMEM(edge_shape, BF),
            pltpu.VMEM(far_shape, BF),
            pltpu.VMEM((local, 2 * D), BF),
            pltpu.VMEM((tokens, 2 * D), BF),
            pltpu.VMEM((D, tokens), BF),
            pltpu.VMEM((D, 4 * D), BF),
            pltpu.VMEM((8, D), F32),
            pltpu.VMEM((n_seq, 8, D), F32),
            pltpu.VMEM((n_dp, 8, D), F32),
            *ext_low,
            *ext_wide,
            *Reduce.scratch(n_dp, n_seq),
            dma((sems,)),
            dma((sems,)),
            dma((edge_sems,)),
            dma((edge_sems,)),
        ],
        compiler_params=params(1),
        name="back",
    )(
        inputs,
        normed,
        fqkv,
        fnorm,
        gres.reshape(rows, local, D),
        q,
        kv,
        coarse,
        edge_near,
        far_all,
        segment_ids,
        totals,
        gmixed.reshape(rows, local, D),
        gup,
        gdown,
        gout,
        grow,
    )

    masters = [w_qkv, w_out, w_up, w_down]
    firsts = [qkv_first, out_first, up_first, down_first, norm_first]
    seconds = [qkv_second, out_second, up_second, down_second, norm_second]
    shapes = [sds(w.shape, F32) for w in masters]
    norm_shape = sds(norm_first.shape, F32)
    updated = pl.pallas_call(
        functools.partial(adam_kernel, n_dp),
        out_shape=shapes
        + [norm_shape]
        + shapes
        + [norm_shape]
        + shapes
        + [norm_shape, sds((1, 1), F32)],
        in_specs=[VM] * 18,
        out_specs=[VM] * 16,
        compiler_params=params(),
        name="adam",
    )(sup, smix, sdown, small, *masters, *firsts, *seconds)
    return (
        outputs.reshape(rows, local, D),
        input_grad,
        updated[15].reshape(()),
        *updated[0:15],
    )


def solution(mesh):
    tokens = P("dp", "seq", None)
    rows, stack, lanes = P("dp", None), P(None, "dp", None), P(None, "dp")
    moments = (stack, stack, rows, rows, rows, rows, rows, rows, lanes, lanes)
    weights = (stack, rows, rows, rows)
    return jax.shard_map(
        on_device,
        mesh=mesh,
        in_specs=(tokens, rows, tokens, *weights, lanes, *moments),
        out_specs=(tokens, tokens, P(), *weights, lanes, *weights, lanes, *weights, lanes),
        check_vma=False,
    )
```

```python
import functools
import math

import jax
import jax.numpy as jnp
from jax import lax
from jax.experimental import pallas as pl
from jax.experimental.pallas import tpu as pltpu
from jax.sharding import PartitionSpec as P

D = 512
HEADS = 8
DH = 64
FF = 2048
LEVELS = 7
DOCS = 4
QB = 128
NKEY = 512
CHUNK = 512
LIMIT = 63
PAIRS = HEADS // 2

masked_score = -1e30
beta_one = 0.9
beta_two = 0.999
bias_first = 1.0 - 0.9**10
bias_second = 1.0 - 0.999**10
learn_rate = 0.1
weight_decay = 0.1
epsilon = 1e-08
clip_norm = 1.0

BF = jnp.bfloat16
F32 = jnp.float32
MESH = pl.DeviceIdType.MESH
VM = pl.BlockSpec(memory_space=pltpu.VMEM)

NN = ((1,), (0,))
NT = ((1,), (1,))
TN = ((0,), (0,))


def mm(left, right, dims):
    return lax.dot_general(left, right, (dims, ((), ())), preferred_element_type=F32)


def params(cid=None):
    if cid is None:
        return pltpu.CompilerParams(vmem_limit_bytes=LIMIT * 2**20)
    return pltpu.CompilerParams(
        vmem_limit_bytes=LIMIT * 2**20, collective_id=cid, has_side_effects=True
    )


def sds(shape, dtype):
    return jax.ShapeDtypeStruct(shape, dtype)


def level_offset(local, level):
    return local - (local >> (level - 1))


def edge_levels(local):
    return [lv for lv in range(LEVELS) if (local >> lv) >= 16]


def far_levels(local):
    return [lv for lv in range(LEVELS) if (local >> lv) < 16]


def ext_rows(local, seq_len, level):
    return ((local >> level) if (local >> level) >= 16 else (seq_len >> level)) + 32


def key_rows(level):
    return max(QB >> level, 16) + 32


def key_start(level):
    return sum(key_rows(lv) for lv in range(level))


def window_start(level, block, offset, local):
    span = 16 << level
    if (local >> level) >= 16:
        if span <= QB:
            return block * (QB >> level)
        return (block * QB) // span * 16
    return (offset + block * QB) // span * 16


def averaging(local):
    row = lax.broadcasted_iota(jnp.int32, (local, local), 0)
    col = lax.broadcasted_iota(jnp.int32, (local, local), 1)
    total = jnp.zeros((local, local), F32)
    for lv in range(1, LEVELS):
        at = lax.shift_right_logical(col, lv) + level_offset(local, lv)
        total = jnp.where(at == row, 2.0**-lv, total)
    return total.astype(BF)


def norm_parts(values):
    center = jnp.mean(values, axis=-1, keepdims=True)
    centered = values - center
    spread = jnp.mean(centered * centered, axis=-1, keepdims=True)
    inverse = lax.rsqrt(spread + 1e-05)
    return centered * inverse, inverse


def norm_back(grad_in, normed, inverse, gain):
    scaled = grad_in * gain
    return inverse * (
        scaled
        - jnp.mean(scaled, axis=-1, keepdims=True)
        - normed * jnp.mean(scaled * normed, axis=-1, keepdims=True)
    )


def document_bounds(seg_row, seq_len):
    return [
        jnp.sum(jnp.where(seg_row < doc, 1.0, 0.0), axis=1, keepdims=True)
        for doc in range(1, DOCS)
    ]


def fill_bias(starts, first_query, seq_len, bias_ref):
    qpos = first_query + lax.broadcasted_iota(jnp.int32, (1, QB), 1)
    qf = qpos.astype(F32)
    low = jnp.zeros((1, QB), F32)
    high = jnp.full((1, QB), float(seq_len), F32)
    for start in starts:
        low = jnp.where(qf >= start, jnp.maximum(low, start), low)
        high = jnp.where(qf < start, jnp.minimum(high, start), high)
    for lv in range(LEVELS):
        span = 16 << lv
        rows = key_rows(lv)
        if span <= QB:
            key_first = first_query // (1 << lv) - 16
        else:
            key_first = first_query // span * 16 - 16
        index = key_first + lax.broadcasted_iota(jnp.int32, (rows, QB), 0)
        begin = (index * (1 << lv)).astype(F32)
        end = begin + float((1 << lv) - 1)
        block = lax.div(qpos, span)
        lo = jnp.maximum(low, ((block - 1) * span).astype(F32))
        hi = jnp.minimum(high, ((block + 2) * span).astype(F32))
        allowed = (begin >= lo) & (end < hi)
        if lv > 0:
            half = span // 2
            parent = lax.div(qpos, half)
            inner_lo = ((parent - 1) * half).astype(F32)
            inner_hi = ((parent + 2) * half).astype(F32)
            allowed = allowed & ((begin < inner_lo) | (begin >= inner_hi))
        bias_ref[key_start(lv) : key_start(lv) + rows, :] = jnp.where(
            allowed, lv * math.log(2.0), masked_score
        )


def build_ext(row, local, kv_ref, coarse_ref, edge_ref, far_ref, ext):
    count = far_ref.shape[1]
    for lv in range(LEVELS):
        rows = local >> lv
        if rows >= 16:
            ext[lv][0:16, :] = edge_ref[row, 0, 16 * lv : 16 * lv + 16, :]
            if lv == 0:
                ext[lv][16 : 16 + rows, :] = kv_ref[row]
            else:
                at = level_offset(local, lv)
                ext[lv][16 : 16 + rows, :] = coarse_ref[row, at : at + rows, :]
            ext[lv][16 + rows : 32 + rows, :] = edge_ref[row, 1, 16 * lv : 16 * lv + 16, :]
        else:
            at = level_offset(local, lv) - (local - 16)
            blank = jnp.zeros((16, 2 * D), F32)
            pieces = [blank]
            for owner in range(count):
                pieces.append(far_ref[row, owner].astype(F32)[at : at + rows, :])
            pieces.append(blank)
            ext[lv][...] = jnp.concatenate(pieces, axis=0).astype(BF)


def gather_keys(ext, block, offset, local, keys_ref):
    for lv in range(LEVELS):
        start = pl.multiple_of(window_start(lv, block, offset, local), 16)
        at = key_start(lv)
        keys_ref[at : at + key_rows(lv), :] = ext[lv][pl.ds(start, key_rows(lv)), :]


def lane_halves(values):
    lane = lax.broadcasted_iota(jnp.int32, values.shape, 1)
    zero = jnp.zeros_like(values)
    return jnp.concatenate(
        [jnp.where(lane < DH, values, zero), jnp.where(lane >= DH, values, zero)], axis=0
    )


def own_halves(pair_t):
    n = pair_t.shape[1] // 2
    sub = lax.broadcasted_iota(jnp.int32, (2 * DH, n), 0)
    return jnp.where(sub < DH, pair_t[:, :n], pair_t[:, n:])


def adam_kernel(n_dp, *refs):
    gup, gmix, gdown, small = refs[0:4]
    weights, firsts, seconds = refs[4:8], refs[8:13], refs[13:18]
    outs = refs[18:]
    new_w, norm_grad, new_m, new_s, grad_norm = (
        outs[0:4],
        outs[4],
        outs[5:10],
        outs[10:15],
        outs[15],
    )
    own = small[0:4, :]
    square = jnp.sum(jnp.sum(own * own, axis=0, keepdims=True), axis=1, keepdims=True)
    root = jnp.sqrt(square + small[4:5, 0:1])
    grad_norm[...] = root
    factor = jnp.minimum(1.0, clip_norm / root)

    def moments(clipped, first, second):
        return (
            beta_one * first + (1.0 - beta_one) * clipped,
            beta_two * second + (1.0 - beta_two) * clipped * clipped,
        )

    def update(weight, grad, first, second):
        mean, sq = moments(grad * factor, first, second)
        change = mean / bias_first / (jnp.sqrt(sq / bias_second) + epsilon) + weight_decay * weight
        return weight - learn_rate * change, mean, sq

    for c in range(3):
        w, m, s = update(
            weights[0][c], gmix[:, c * D : c * D + D].astype(F32), firsts[0][c], seconds[0][c]
        )
        new_w[0][c], new_m[0][c], new_s[0][c] = w, m, s
    for at, grad in ((1, gmix[:, 3 * D : 4 * D]), (2, gup[...]), (3, gdown[...])):
        grad = grad.astype(F32)
        if at == 3:
            grad = grad.T
        w, m, s = update(weights[at][...], grad, firsts[at][...], seconds[at][...])
        new_w[at][...], new_m[at][...], new_s[at][...] = w, m, s
    width = D // n_dp
    lane = lax.axis_index("dp") * width
    rolled = pltpu.roll(small[...], D - lane, 1)[0:4, 0:width]
    clipped = rolled * factor
    norm_grad[...] = clipped
    m, s = moments(clipped, firsts[4][...], seconds[4][...])
    new_m[4][...], new_s[4][...] = m, s


class Copies:
    def __init__(self, send, recv):
        self.send, self.recv = send, recv
        self.started = []

    def push(self, src, dst, send_at, recv_at, device):
        copy = pltpu.make_async_remote_copy(
            src_ref=src,
            dst_ref=dst,
            send_sem=self.send.at[send_at],
            recv_sem=self.recv.at[recv_at],
            device_id=device,
            device_id_type=MESH,
        )
        copy.start()
        self.started.append(copy)

    def arrived(self, dst, recv_at, device):
        pltpu.make_async_remote_copy(
            src_ref=dst,
            dst_ref=dst,
            send_sem=self.send.at[0],
            recv_sem=self.recv.at[recv_at],
            device_id=device,
            device_id_type=MESH,
        ).wait_recv()

    def finish(self):
        for copy in self.started:
            copy.wait_send()
        self.started = []


def greet(peers):
    barrier = pltpu.get_barrier_semaphore()
    for peer in peers:
        pl.semaphore_signal(barrier, inc=1, device_id=peer, device_id_type=MESH)
    pl.semaphore_wait(barrier, len(peers))


class Place:
    def __init__(self, n_dp, n_seq):
        self.n_dp, self.n_seq = n_dp, n_seq
        self.d, self.s = lax.axis_index("dp"), lax.axis_index("seq")
        self.z, self.y = lax.div(self.d, 2), lax.rem(self.d, 2)
        self.hi, self.core = lax.div(self.s, 2), lax.rem(self.s, 2)
        self.depth, self.high = n_dp // 2, n_seq // 2
        self.mate = self.s + 1 - 2 * self.core
        self.flip = self.d + 1 - 2 * self.y
        self.seq_others = [lax.rem(self.s + k, n_seq) for k in range(1, n_seq)]
        self.dp_others = [lax.rem(self.d + k, n_dp) for k in range(1, n_dp)]

    def greet(self):
        greet(
            [(self.d, o) for o in self.seq_others] + [(o, self.s) for o in self.dp_others]
        )


class Gather:
    def __init__(self, place, parts, copies, base):
        self.at, self.parts, self.copies, self.base = place, parts, copies, base
        self.stride = self.sems(place.n_dp, place.n_seq)

    @staticmethod
    def sems(n_dp, n_seq):
        return 2 * (n_dp // 2) + n_dp * n_seq

    def split(self, p):
        high = self.at.high
        return p >= 3 and high > 1 and self.parts[p][3] % (32 * high) == 0

    def piece(self, p, shard, core, hi):
        _, whole, lead, rows = self.parts[p]
        n = rows // 2
        start = shard * rows + core * n
        if self.split(p):
            n = n // self.at.high
            start = start + hi * n
        if lead is None:
            return whole.at[pl.ds(pl.multiple_of(start, n), n), :]
        if lead == "blocks":
            row = pl.multiple_of(lax.rem(start, CHUNK), n)
            return whole.at[lax.div(start, CHUNK), pl.ds(row, n), :]
        return whole.at[lead[0] : lead[1], pl.ds(pl.multiple_of(start, n), n), :]

    def sem(self, p, stage, index):
        at = self.base + p * self.stride
        sizes = (self.at.depth, self.at.depth, self.at.n_dp * self.at.high)
        return at + sum(sizes[:stage]) + index

    def load(self, p):
        own, whole, lead, rows = self.parts[p]
        start = pl.multiple_of(self.at.d * rows, rows)
        if lead is None:
            whole[pl.ds(start, rows), :] = own[...].astype(BF)
        elif lead == "blocks":
            row = pl.multiple_of(lax.rem(start, CHUNK), rows)
            whole[lax.div(start, CHUNK), pl.ds(row, rows), :] = own[...].astype(BF)
        else:
            whole[lead[0] : lead[1], pl.ds(start, rows), :] = own[lead[0] : lead[1]].astype(BF)

    def start(self, p):
        me = self.at
        self.load(p)
        mine = self.piece(p, me.d, me.core, me.hi)
        for k in range(1, me.depth):
            other = lax.rem(me.z + k, me.depth) * 2 + me.y
            self.copies.push(mine, mine, self.sem(p, 0, k), self.sem(p, 0, me.z), (other, me.s))
        self.copies.push(mine, mine, self.sem(p, 1, 0), self.sem(p, 1, me.z), (me.flip, me.s))

    def onward(self, p, shard, k):
        me = self.at
        here = self.piece(p, shard, me.core, me.hi)
        if self.split(p):
            for kh in range(1, me.high):
                other = lax.rem(me.hi + kh, me.high) * 2 + me.core
                self.copies.push(
                    here,
                    here,
                    self.sem(p, 2, kh * me.n_dp + k),
                    self.sem(p, 2, me.hi * me.n_dp + shard),
                    (me.d, other),
                )
            which = me.hi
        else:
            which = 0
        self.copies.push(
            here, here, self.sem(p, 3, k), self.sem(p, 3, which * me.n_dp + shard), (me.d, me.mate)
        )

    def relay_z(self, p):
        me = self.at
        for k in range(1, me.depth):
            zz = lax.rem(me.z + k, me.depth)
            shard = zz * 2 + me.y
            here = self.piece(p, shard, me.core, me.hi)
            self.copies.arrived(here, self.sem(p, 0, zz), (shard, me.s))
            self.copies.push(
                here, here, self.sem(p, 1, k), self.sem(p, 1, zz), (me.flip, me.s)
            )
            self.onward(p, shard, k)

    def relay_y(self, p):
        me = self.at
        for k in range(me.depth):
            zz = lax.rem(me.z + k, me.depth)
            shard = zz * 2 + 1 - me.y
            here = self.piece(p, shard, me.core, me.hi)
            self.copies.arrived(here, self.sem(p, 1, zz), (me.flip, me.s))
            self.onward(p, shard, me.depth + k)

    def relay_x(self, p):
        me = self.at
        if not self.split(p):
            return
        for kh in range(1, me.high):
            h = lax.rem(me.hi + kh, me.high)
            for k in range(1, me.n_dp):
                shard = lax.rem(me.d + k, me.n_dp)
                here = self.piece(p, shard, me.core, h)
                self.copies.arrived(
                    here, self.sem(p, 2, h * me.n_dp + shard), (me.d, h * 2 + me.core)
                )
                self.copies.push(
                    here,
                    here,
                    self.sem(p, 3, kh * me.n_dp + k),
                    self.sem(p, 3, h * me.n_dp + shard),
                    (me.d, me.mate),
                )

    def settle(self, p):
        me = self.at
        for h in range(me.high if self.split(p) else 1):
            for k in range(1, me.n_dp):
                shard = lax.rem(me.d + k, me.n_dp)
                self.copies.arrived(
                    self.piece(p, shard, 1 - me.core, h),
                    self.sem(p, 3, h * me.n_dp + shard),
                    (me.d, me.mate),
                )


class Exchange:
    def __init__(self, place, personal, edge_in, far_in, edge_out, far_out, send, recv):
        self.at, self.personal = place, personal
        self.edge_in, self.far_in, self.edge_out, self.far_out = edge_in, far_in, edge_out, far_out
        self.send, self.recv = send, recv

    @staticmethod
    def sems(rows, n_seq):
        return rows * (2 + n_seq)

    def edge(self, row, way, device):
        base = row * (2 + self.at.n_seq)
        return pltpu.make_async_remote_copy(
            src_ref=self.edge_in.at[row, way],
            dst_ref=self.edge_out.at[row, 1 - way],
            send_sem=self.send.at[base + way],
            recv_sem=self.recv.at[base + 1 - way],
            device_id=(self.at.d, device),
            device_id_type=MESH,
        )

    def far(self, row, k, other):
        base = row * (2 + self.at.n_seq) + 2
        return pltpu.make_async_remote_copy(
            src_ref=self.far_in.at[row, other] if self.personal else self.far_in.at[row],
            dst_ref=self.far_out.at[row, self.at.s],
            send_sem=self.send.at[base + k],
            recv_sem=self.recv.at[base + self.at.s],
            device_id=(self.at.d, other),
            device_id_type=MESH,
        )

    def start(self, row):
        s, n_seq = self.at.s, self.at.n_seq

        @pl.when(s > 0)
        def _():
            self.edge(row, 0, s - 1).start()

        @pl.when(s < n_seq - 1)
        def _():
            self.edge(row, 1, s + 1).start()

        for k, other in enumerate(self.at.seq_others):
            self.far(row, k, other).start()
        self.far_out[row, s] = self.far_in[row, s] if self.personal else self.far_in[row]

    def arrive(self, row):
        s, n_seq = self.at.s, self.at.n_seq
        blank = jnp.zeros(self.edge_out.shape[2:], BF)

        @pl.when(s > 0)
        def _():
            self.edge(row, 1, s - 1).wait_recv()

        @pl.when(s == 0)
        def _():
            self.edge_out[row, 0] = blank

        @pl.when(s < n_seq - 1)
        def _():
            self.edge(row, 0, s + 1).wait_recv()

        @pl.when(s == n_seq - 1)
        def _():
            self.edge_out[row, 1] = blank

        base = row * (2 + n_seq) + 2
        for other in self.at.seq_others:
            here = self.far_out.at[row, other]
            pltpu.make_async_remote_copy(
                src_ref=here,
                dst_ref=here,
                send_sem=self.send.at[base],
                recv_sem=self.recv.at[base + other],
                device_id=(self.at.d, other),
                device_id_type=MESH,
            ).wait_recv()

    def finish(self, row):
        s, n_seq = self.at.s, self.at.n_seq

        @pl.when(s > 0)
        def _():
            self.edge(row, 0, s - 1).wait_send()

        @pl.when(s < n_seq - 1)
        def _():
            self.edge(row, 1, s + 1).wait_send()

        for k, other in enumerate(self.at.seq_others):
            self.far(row, k, other).wait_send()


def grad_parts(n_dp, n_seq):
    if D // n_seq % 128:
        return [
            (0, 0, FF, True, True, "up"),
            (1, 0, FF, False, False, "down"),
            (2, 0, 4 * D, True, True, "kv"),
        ]
    return [
        (0, 0, FF // 2, True, True, "first"),
        (0, FF // 2, FF, True, True, "up"),
        (1, 0, FF, False, False, "down"),
        (2, 3 * D, 4 * D, True, True, "out"),
        (2, 0, D, True, False, "q"),
        (2, D, 2 * D, True, True, "kv"),
        (2, 2 * D, 3 * D, True, False, "kv"),
    ]


def block_shape(part, n_dp, n_seq):
    _, lo, hi, by_rows, _, _ = part
    if by_rows:
        return (D // n_dp, (hi - lo) // n_seq)
    return (D // n_seq, (hi - lo) // n_dp)


class Reduce:
    def __init__(self, place, sources, finals, buffers, copies, base):
        self.at, self.sources, self.finals = place, sources, finals
        self.parts = grad_parts(place.n_dp, place.n_seq)
        n = len(self.parts)
        groups = [buffers[i * n : i * n + n] for i in range(5)]
        self.core_in, self.held, self.high_in, self.y_in, self.z_in = groups
        self.copies, self.base = copies, base
        self.stride = self.sems(place.n_dp, place.n_seq)

    @staticmethod
    def sems(n_dp, n_seq):
        return 2 + n_seq // 2 + n_dp // 2 + n_seq

    @staticmethod
    def scratch(n_dp, n_seq):
        high, depth = n_seq // 2, n_dp // 2
        groups = [[], [], [], [], []]
        for part in grad_parts(n_dp, n_seq):
            _, lo, up, by_rows, first, _ = part
            a, b = block_shape(part, n_dp, n_seq)
            shapes = [
                (D, (up - lo) // 2) if by_rows else (FF // CHUNK, D // 2, CHUNK),
                (high, depth, 2, a, b),
                (high - 1, depth, 2, a, b) if first else (high - 1, depth, a, b),
                (depth, a, b) if first else (high, depth, a, b),
                (depth - 1, a, b),
            ]
            for group, shape in zip(groups, shapes):
                group.append(pltpu.VMEM(shape, BF))
        return [item for group in groups for item in group]

    def of(self, *stages):
        return [p for p, part in enumerate(self.parts) if part[5] in stages]

    def sem(self, p, stage, index=0):
        sizes = (1, 1, self.at.high, self.at.depth, self.at.n_seq)
        return self.base + p * self.stride + sum(sizes[:stage]) + index

    def start(self, p):
        me = self.at
        src, lo, up, by_rows, _, _ = self.parts[p]
        ref = self.sources[src]
        which = 1 - me.core
        if by_rows:
            w = (up - lo) // 2
            half = ref.at[:, pl.ds(pl.multiple_of(lo + which * w, 128), w)]
        else:
            w = D // 2
            half = ref.at[:, pl.ds(pl.multiple_of(which * w, w), w), :]
        self.copies.push(half, self.core_in[p], self.sem(p, 0), self.sem(p, 0), (me.d, me.mate))

    def push_y(self, p, held):
        me = self.at
        self.copies.push(held, self.y_in[p], self.sem(p, 1), self.sem(p, 1), (me.flip, me.s))

    def take_y(self, p):
        me = self.at
        self.copies.arrived(self.y_in[p], self.sem(p, 1), (me.flip, me.s))


    def push_high(self, p, y):
        me = self.at
        for k in range(1, me.high):
            h = lax.rem(me.hi + k, me.high)
            src = self.held[p].at[h] if y is None else self.held[p].at[h, :, y]
            self.copies.push(
                src,
                self.high_in[p].at[me.high - k - 1],
                self.sem(p, 2, k),
                self.sem(p, 2, me.high - k),
                (me.d, h * 2 + me.core),
            )

    def take_high(self, p):
        me = self.at
        for k in range(1, me.high):
            h = lax.rem(me.hi + k, me.high)
            self.copies.arrived(
                self.high_in[p].at[k - 1], self.sem(p, 2, k), (me.d, h * 2 + me.core)
            )

    def combine(self, p):
        me = self.at
        part = self.parts[p]
        src, lo, up, by_rows, first, _ = part
        a, b = block_shape(part, me.n_dp, me.n_seq)
        self.copies.arrived(self.core_in[p], self.sem(p, 0), (me.d, me.mate))
        theirs, held, source = self.core_in[p], self.held[p], self.sources[src]
        for h in range(me.high):
            for shard in range(me.n_dp):
                which = me.core * me.high + h
                if by_rows:
                    r = slice(shard * a, shard * a + a)
                    left = source[r, pl.ds(pl.multiple_of(lo + which * b, 128), b)]
                    right = theirs[r, h * b : h * b + b]
                else:
                    block, lane = shard * b // CHUNK, shard * b % CHUNK
                    lanes = slice(lane, lane + b)
                    left = source[block, pl.ds(pl.multiple_of(which * a, a), a), lanes]
                    right = theirs[block, h * a : h * a + a, lanes]
                total = left.astype(F32) + right.astype(F32)
                held[h, shard // 2, shard % 2] = total.astype(BF)
        if first:
            self.push_high(p, None)
        else:
            self.push_y(p, held.at[:, :, 1 - me.y])

    def add_high(self, p):
        me = self.at
        held = self.held[p]
        self.take_high(p)
        first = self.parts[p][4]
        for zz in range(me.depth):
            for yy in (0, 1) if first else (me.y,):
                value = held[me.hi, zz, yy].astype(F32)
                for k in range(me.high - 1):
                    more = self.high_in[p][k, zz, yy] if first else self.high_in[p][k, zz]
                    value += more.astype(F32)
                held[me.hi, zz, yy] = value.astype(BF)

    def second(self, p):
        me = self.at
        held = self.held[p]
        if self.parts[p][4]:
            self.add_high(p)
            self.push_y(p, held.at[me.hi, :, 1 - me.y])
        else:
            self.take_y(p)
            for h in range(me.high):
                for zz in range(me.depth):
                    value = held[h, zz, me.y].astype(F32) + self.y_in[p][h, zz].astype(F32)
                    held[h, zz, me.y] = value.astype(BF)
            self.push_high(p, me.y)

    def third(self, p):
        me = self.at
        held = self.held[p]
        if self.parts[p][4]:
            self.take_y(p)
            for zz in range(me.depth):
                value = held[me.hi, zz, me.y].astype(F32) + self.y_in[p][zz].astype(F32)
                held[me.hi, zz, me.y] = value.astype(BF)
        else:
            self.add_high(p)
        for k in range(1, me.depth):
            zz = lax.rem(me.z + k, me.depth)
            self.copies.push(
                held.at[me.hi, zz, me.y],
                self.z_in[p].at[me.depth - k - 1],
                self.sem(p, 3, k),
                self.sem(p, 3, me.depth - k),
                (zz * 2 + me.y, me.s),
            )

    def place_of(self, p, owner):
        part = self.parts[p]
        src, lo, up, by_rows, _, _ = part
        a, b = block_shape(part, self.at.n_dp, self.at.n_seq)
        which = lax.rem(owner, 2) * self.at.high + lax.div(owner, 2)
        if by_rows:
            return self.finals[src].at[:, pl.ds(pl.multiple_of(lo + which * b, 128), b)]
        return self.finals[src].at[pl.ds(pl.multiple_of(which * a, a), a), :]

    def final(self, p):
        me = self.at
        value = self.held[p][me.hi, me.z, me.y].astype(F32)
        for k in range(1, me.depth):
            zz = lax.rem(me.z + k, me.depth)
            self.copies.arrived(self.z_in[p].at[k - 1], self.sem(p, 3, k), (zz * 2 + me.y, me.s))
            value += self.z_in[p][k - 1].astype(F32)
        low = value.astype(BF)
        here = self.place_of(p, me.s)
        here[...] = low
        for k, o in enumerate(me.seq_others):
            self.copies.push(here, here, self.sem(p, 4, 1 + k), self.sem(p, 4, me.s), (me.d, o))
        value = low.astype(F32)
        return jnp.sum(jnp.sum(value * value, axis=0, keepdims=True), axis=1, keepdims=True)

    def settle(self, p):
        me = self.at
        for o in me.seq_others:
            self.copies.arrived(self.place_of(p, o), self.sem(p, 4, o), (me.d, o))


class Named:
    def __init__(self, names, refs):
        for name, ref in zip(names, refs):
            setattr(self, name, ref)


INPUTS = ["x", "seg", "og", "wqkv", "wout", "wup", "wdown", "norm_own"]
OUTPUTS = ["out", "ginput", "sup", "smix", "sdown", "small"]


def layer_scratch(z):
    tokens = (z.tokens, D)
    return {
        "slots": pltpu.VMEM((z.n_dp, 8, 128), F32),
        "norm": pltpu.VMEM((8, D), F32),
        "fqkv": pltpu.VMEM((3, D, D), BF),
        "fout": pltpu.VMEM((D, D), BF),
        "fup": pltpu.VMEM((D, FF), BF),
        "fdown": pltpu.VMEM((FF // CHUNK, CHUNK, D), BF),
        "normed": pltpu.VMEM(tokens, BF),
        "q": pltpu.VMEM(tokens, BF),
        "kv": pltpu.VMEM(z.pairs, BF),
        "coarse": pltpu.VMEM(z.pairs, BF),
        "edge_own": pltpu.VMEM(z.edge, BF),
        "edge_near": pltpu.VMEM(z.edge, BF),
        "edge_back": pltpu.VMEM(z.edge, BF),
        "far_own": pltpu.VMEM((z.rows, 16, 2 * D), BF),
        "far_all": pltpu.VMEM(z.far, BF),
        "gfar": pltpu.VMEM(z.far, BF),
        "far_back": pltpu.VMEM(z.far, BF),
        "keys": pltpu.VMEM((NKEY, 2 * D), BF),
        "bias": pltpu.VMEM((NKEY, QB), F32),
        "mixed": pltpu.VMEM(tokens, BF),
        "totals": pltpu.VMEM((z.rows, z.blocks, PAIRS, 2 * QB), F32),
        "second": pltpu.VMEM(tokens, BF),
        "second_t": pltpu.VMEM((D, z.tokens), BF),
        "og_t": pltpu.VMEM((D, z.tokens), BF),
        "acc": pltpu.VMEM(tokens, F32),
        "gsec": pltpu.VMEM(tokens, F32),
        "hid": pltpu.VMEM((z.tokens, CHUNK), BF),
        "gpre": pltpu.VMEM((z.tokens, CHUNK), BF),
        "low": pltpu.VMEM(tokens, BF),
        "gmix": pltpu.VMEM((D, 4 * D), BF),
        "gcoarse": pltpu.VMEM(z.pairs, BF),
        "grow": pltpu.VMEM((8, D), F32),
        "small_seq": pltpu.VMEM((z.n_seq, 8, D), F32),
        "small_dp": pltpu.VMEM((z.n_dp, 8, D), F32),
        "send": DMA((z.sems,)),
        "recv": DMA((z.sems,)),
        "edge_send": DMA((z.edge_sems,)),
        "edge_recv": DMA((z.edge_sems,)),
        "back_send": DMA((z.edge_sems,)),
        "back_recv": DMA((z.edge_sems,)),
    }


def layer_kernel(z, names, *refs):
    count = len(INPUTS) + len(OUTPUTS) + len(names)
    r = Named(INPUTS + OUTPUTS + names, refs[:count])
    ext = refs[count : count + LEVELS]
    gext = refs[count + LEVELS : count + 2 * LEVELS]
    buffers = refs[count + 2 * LEVELS :]
    rows, local, tokens, seq_len = z.rows, z.local, z.tokens, z.seq_len
    n_dp, n_seq = z.n_dp, z.n_seq
    shard = D // n_dp
    me = Place(n_dp, n_seq)
    me.greet()
    copies = Copies(r.send, r.recv)
    gather_base = 2 * n_dp + n_seq
    gather = Gather(
        me,
        [
            (r.wqkv, r.fqkv, (1, 3), shard),
            (r.wqkv, r.fqkv, (0, 1), shard),
            (r.wout, r.fout, None, shard),
            (r.wup, r.fup, None, shard),
            (r.wdown, r.fdown, "blocks", FF // n_dp),
        ],
        copies,
        gather_base,
    )
    KV, Q, OUT, UP, DOWN = range(5)
    reduce = Reduce(
        me,
        (r.fup, r.fdown, r.gmix),
        (r.sup, r.sdown, r.smix),
        buffers,
        copies,
        gather_base + 5 * gather.stride,
    )
    exchange = Exchange(
        me, False, r.edge_own, r.far_own, r.edge_near, r.far_all, r.edge_send, r.edge_recv
    )
    exchange_back = Exchange(
        me, True, r.edge_own, r.gfar, r.edge_back, r.far_back, r.back_send, r.back_recv
    )
    tile = min(local, 256)
    tiles = tokens // tile
    row_tiles = local // tile

    def tile_of(i):
        return pl.ds(pl.multiple_of(i * tile, tile), tile)


    r.slots[me.d] = r.norm_own[...].astype(BF).astype(F32)
    gather.start(KV)
    for k, o in enumerate(me.dp_others):
        copies.push(r.slots.at[me.d], r.slots.at[me.d], 1 + k, me.d, (o, me.s))
    gather.start(Q)
    mean_of = averaging(local)
    for o in me.dp_others:
        copies.arrived(r.slots.at[o], o, (o, me.s))
    total = jnp.zeros((8, D), F32)
    for at in range(n_dp):
        i = lax.broadcasted_iota(jnp.int32, (128, D), 0)
        j = lax.broadcasted_iota(jnp.int32, (128, D), 1)
        pick = jnp.where((j == i + at * shard) & (i < shard), 1.0, 0.0).astype(BF)
        total += mm(r.slots[at].astype(BF), pick, NN)
    r.norm[...] = total
    gather.relay_z(KV)

    def normalize(i, carry):
        part = tile_of(i)
        hat, _ = norm_parts(r.x[part, :].astype(F32))
        r.normed[part, :] = (hat * r.norm[0:1, :] + r.norm[1:2, :]).astype(BF)
        r.og_t[:, part] = r.og[part, :].T
        return carry

    lax.fori_loop(0, tiles, normalize, 0)
    gather.relay_z(Q)
    gather.start(OUT)
    gather.start(UP)
    gather.relay_y(KV)
    gather.relay_y(Q)
    gather.start(DOWN)
    gather.settle(KV)
    for row in range(rows):

        def project_kv(i, carry):
            part = tile_of(i)
            normed = r.normed[tile_of(row * row_tiles + i), :]
            r.kv[row, part, 0:D] = mm(normed, r.fqkv[1], NN).astype(BF)
            r.kv[row, part, D : 2 * D] = mm(normed, r.fqkv[2], NN).astype(BF)
            return carry

        lax.fori_loop(0, row_tiles, project_kv, 0)
        r.coarse[row] = mm(mean_of, r.kv[row], NN).astype(BF)
        for lv in edge_levels(local):
            n = local >> lv
            to = slice(16 * lv, 16 * lv + 16)
            if lv == 0:
                r.edge_own[row, 0, to, :] = r.kv[row, 0:16, :]
                r.edge_own[row, 1, to, :] = r.kv[row, n - 16 : n, :]
            else:
                at = level_offset(local, lv)
                r.edge_own[row, 0, to, :] = r.coarse[row, at : at + 16, :]
                r.edge_own[row, 1, to, :] = r.coarse[row, at + n - 16 : at + n, :]
        r.far_own[row] = r.coarse[row, local - 16 : local, :]
        exchange.start(row)
    gather.settle(Q)

    def project_q(i, carry):
        part = tile_of(i)
        r.q[part, :] = mm(r.normed[part, :], r.fqkv[0], NN).astype(BF)
        return carry

    lax.fori_loop(0, tiles, project_q, 0)
    gather.relay_z(OUT)
    gather.relay_z(UP)


    offset = me.s * local
    blocks = local // QB
    half = blocks // 2

    def part_of(row, block):
        return pl.ds(pl.multiple_of(row * local + block * QB, QB), QB)

    for row in range(rows):
        exchange.arrive(row)
        build_ext(row, local, r.kv, r.coarse, r.edge_near, r.far_all, ext)
        starts = document_bounds(r.seg[row : row + 1, :], seq_len)

        def attend(block, carry):
            gather_keys(ext, block, offset, local, r.keys)
            fill_bias(starts, offset + block * QB, seq_len, r.bias)
            part = part_of(row, block)
            both = jnp.concatenate([r.bias[...], r.bias[...]], axis=1)
            for pair in range(PAIRS):
                lanes = slice(128 * pair, 128 * pair + 128)
                queries = lane_halves(r.q[part, lanes] * BF(DH**-0.5))
                scores = mm(r.keys[:, lanes], queries, NT) + both
                peak = jnp.max(scores, axis=0, keepdims=True)
                weights = jnp.exp(scores - peak)
                denominator = jnp.sum(weights, axis=0, keepdims=True)
                r.totals[row, block, pair : pair + 1, :] = peak + jnp.log(denominator)
                values = r.keys[:, D + 128 * pair : D + 128 * pair + 128]
                mixed_t = mm(values, weights.astype(BF), TN) / denominator
                r.mixed[part, lanes] = own_halves(mixed_t).T.astype(BF)
            return carry

        lax.fori_loop(0, half, attend, 0)
        if row == 0:
            gather.relay_z(DOWN)
            gather.relay_y(OUT)
            gather.relay_y(UP)
        if row == rows - 1:
            gather.relay_x(UP)
        lax.fori_loop(half, blocks, attend, 0)
        if row == 0:
            gather.relay_y(DOWN)
    gather.relay_x(DOWN)
    for p in (OUT, UP, DOWN):
        gather.settle(p)
    for row in range(rows):
        exchange.finish(row)
    copies.finish()


    def feed_first(i, carry):
        part = tile_of(i)
        resid = r.x[part, :].astype(F32) + mm(r.mixed[part, :], r.fout[...], NN)
        r.ginput[part, :] = resid
        r.acc[part, :] = resid
        hat, _ = norm_parts(resid)
        second = (hat * r.norm[2:3, :] + r.norm[3:4, :]).astype(BF)
        r.second[part, :] = second
        r.second_t[:, part] = second.T
        r.gsec[part, :] = jnp.zeros((tile, D), F32)
        return carry

    lax.fori_loop(0, tiles, feed_first, 0)

    def feed_chunk(f, carry):
        cols = pl.ds(pl.multiple_of(f * CHUNK, CHUNK), CHUNK)

        def inner(i, inner_carry):
            part = tile_of(i)
            pre = mm(r.second[part, :], r.fup[:, cols], NN)
            square = pre * pre
            tangent = jnp.tanh(0.7978845608 * (pre + 0.044715 * pre * square))
            upper = 0.5 + 0.5 * tangent
            hidden = (pre * upper).astype(BF)
            slope = upper + 0.5 * pre * (1.0 - tangent * tangent) * (
                0.7978845608 + 0.7978845608 * 3.0 * 0.044715 * square
            )
            grad_pre = (mm(r.og[part, :], r.fdown[f], NT) * slope).astype(BF)
            r.hid[part, :] = hidden
            r.gpre[part, :] = grad_pre
            r.acc[part, :] += mm(hidden, r.fdown[f], NN)
            r.gsec[part, :] += mm(grad_pre, r.fup[:, cols], NT)
            return inner_carry

        lax.fori_loop(0, tiles, inner, 0)
        r.fdown[f] = mm(r.og_t[...], r.hid[...], NN).astype(BF)
        r.fup[:, cols] = mm(r.second_t[...], r.gpre[...], NN).astype(BF)
        return carry

    chunks = FF // CHUNK
    lax.fori_loop(0, chunks // 2, feed_chunk, 0)
    for p in reduce.of("first"):
        reduce.start(p)
    lax.fori_loop(chunks // 2, chunks - 1, feed_chunk, 0)
    for p in reduce.of("first"):
        reduce.combine(p)
    lax.fori_loop(chunks - 1, chunks, feed_chunk, 0)
    for p in reduce.of("up", "down"):
        reduce.start(p)
    r.grow[...] = jnp.zeros_like(r.grow)

    def feed_last(i, carry):
        part = tile_of(i)
        r.out[part, :] = r.acc[part, :].astype(BF)
        hat, inverse = norm_parts(r.ginput[part, :])
        grad = r.gsec[part, :]
        gres = r.og[part, :].astype(F32) + norm_back(grad, hat, inverse, r.norm[2:3, :])
        r.ginput[part, :] = gres
        r.low[part, :] = gres.astype(BF)
        r.grow[2:3, :] += jnp.sum(grad * hat, axis=0, keepdims=True)
        r.grow[3:4, :] += jnp.sum(grad, axis=0, keepdims=True)
        return carry

    lax.fori_loop(0, tiles, feed_last, 0)
    for p in reduce.of("first"):
        reduce.second(p)
    for p in reduce.of("up", "down"):
        reduce.combine(p)
    r.gmix[:, 3 * D : 4 * D] = mm(r.mixed[...], r.low[...], TN).astype(BF)
    for p in reduce.of("out"):
        reduce.start(p)

    def mixed_back(i, carry):
        part = tile_of(i)
        r.mixed[part, :] = mm(r.low[part, :], r.fout[...], NT).astype(BF)
        r.og_t[:, part] = r.normed[part, :].T
        return carry

    lax.fori_loop(0, tiles, mixed_back, 0)


    square = jnp.zeros((1, 1), F32)
    for row in range(rows):
        build_ext(row, local, r.kv, r.coarse, r.edge_near, r.far_all, ext)
        starts = document_bounds(r.seg[row : row + 1, :], seq_len)
        for item in gext:
            item[...] = jnp.zeros_like(item)

        def attend_back(block, carry):
            gather_keys(ext, block, offset, local, r.keys)
            fill_bias(starts, offset + block * QB, seq_len, r.bias)
            part = part_of(row, block)
            both = jnp.concatenate([r.bias[...], r.bias[...]], axis=1)
            for pair in range(PAIRS):
                lanes = slice(128 * pair, 128 * pair + 128)
                vlanes = slice(D + 128 * pair, D + 128 * pair + 128)
                queries = lane_halves(r.q[part, lanes] * BF(DH**-0.5))
                grads = lane_halves(r.mixed[part, lanes])
                scores = mm(r.keys[:, lanes], queries, NT) + both
                soft = jnp.exp(scores - r.totals[row, block, pair : pair + 1, :])
                gsoft = mm(r.keys[:, vlanes], grads, NT)
                row_total = jnp.sum(soft * gsoft, axis=0, keepdims=True)
                gscore = (soft * (gsoft - row_total)).astype(BF)
                gkeys = mm(gscore, queries, NN)
                gvalues = mm(soft.astype(BF), grads, NN)
                for lv in range(LEVELS):
                    n, at = key_rows(lv), key_start(lv)
                    to = pl.ds(pl.multiple_of(window_start(lv, block, offset, local), 16), n)
                    gext[lv][to, lanes] += gkeys[at : at + n, :]
                    gext[lv][to, vlanes] += gvalues[at : at + n, :]
                gq_t = own_halves(mm(r.keys[:, lanes], gscore, TN)) * DH**-0.5
                r.low[part, lanes] = gq_t.T.astype(BF)
            return carry

        lax.fori_loop(0, half, attend_back, 0)
        if row == 0:
            for p in reduce.of("out"):
                reduce.combine(p)
            for p in reduce.of("first"):
                reduce.third(p)
            for p in reduce.of("up"):
                reduce.second(p)
        if row == rows - 1:
            for p in reduce.of("out"):
                reduce.second(p)
            for p in reduce.of("down"):
                reduce.third(p)
            for p in reduce.of("up"):
                square += reduce.final(p)
        lax.fori_loop(half, blocks, attend_back, 0)
        if row == 0:
            for p in reduce.of("down"):
                reduce.second(p)
            for p in reduce.of("first"):
                square += reduce.final(p)
            for p in reduce.of("up"):
                reduce.third(p)
        here = slice(row * local, row * local + local)
        r.acc[here, :] = gext[0][16 : 16 + local, 0:D]
        r.gsec[here, :] = gext[0][16 : 16 + local, D : 2 * D]
        for lv in edge_levels(local):
            n = local >> lv
            to = slice(16 * lv, 16 * lv + 16)
            if lv > 0:
                at = level_offset(local, lv)
                r.gcoarse[row, at : at + n, :] = gext[lv][16 : 16 + n, :].astype(BF)
            r.edge_own[row, 0, to, :] = gext[lv][0:16, :].astype(BF)
            r.edge_own[row, 1, to, :] = gext[lv][16 + n : 32 + n, :].astype(BF)
        for owner in range(n_seq):
            pieces = []
            used = 0
            for lv in far_levels(local):
                n = local >> lv
                pieces.append(gext[lv][16 + owner * n : 16 + owner * n + n, :])
                used += n
            pieces.append(jnp.zeros((16 - used, 2 * D), F32))
            r.gfar[row, owner] = jnp.concatenate(pieces, axis=0).astype(BF)
        exchange_back.start(row)


    for p in reduce.of("out"):
        reduce.third(p)
    for p in reduce.of("down"):
        square += reduce.final(p)
    r.gmix[:, 0:D] = mm(r.og_t[...], r.low[...], NN).astype(BF)
    for p in reduce.of("q"):
        reduce.start(p)
    spread_of = averaging(local)
    for row in range(rows):
        exchange_back.arrive(row)
        base = row * local
        for lv in edge_levels(local):
            n = local >> lv
            for way in range(2):
                more = r.edge_back[row, way, 16 * lv : 16 * lv + 16, :].astype(F32)
                low_row = 0 if way == 0 else n - 16
                if lv == 0:
                    to = slice(base + low_row, base + low_row + 16)
                    r.acc[to, :] += more[:, 0:D]
                    r.gsec[to, :] += more[:, D : 2 * D]
                else:
                    at = level_offset(local, lv) + low_row
                    sums = r.gcoarse[row, at : at + 16, :].astype(F32) + more
                    r.gcoarse[row, at : at + 16, :] = sums.astype(BF)
        total = r.far_back[row, 0].astype(F32)
        for owner in range(1, n_seq):
            total += r.far_back[row, owner].astype(F32)
        r.gcoarse[row, local - 16 : local, :] = total.astype(BF)
        for at in range(0, local, tile):
            span, where = slice(at, at + tile), slice(base + at, base + at + tile)
            spread = mm(spread_of[:, span], r.gcoarse[row], TN)
            r.hid[where, :] = (r.acc[where, :] + spread[:, 0:D]).astype(BF)
            r.gpre[where, :] = (r.gsec[where, :] + spread[:, D : 2 * D]).astype(BF)
    for p in reduce.of("q"):
        reduce.combine(p)
    for p in reduce.of("out"):
        square += reduce.final(p)
    late = reduce.of("kv")
    r.gmix[:, D : 2 * D] = mm(r.og_t[...], r.hid[...], NN).astype(BF)
    if len(late) > 1:
        reduce.start(late[0])
    r.gmix[:, 2 * D : 3 * D] = mm(r.og_t[...], r.gpre[...], NN).astype(BF)
    reduce.start(late[-1])

    def settle_inputs(i):
        part = tile_of(i)
        gnormed = (
            mm(r.low[part, :], r.fqkv[0], NT)
            + mm(r.hid[part, :], r.fqkv[1], NT)
            + mm(r.gpre[part, :], r.fqkv[2], NT)
        )
        hat, inverse = norm_parts(r.x[part, :].astype(F32))
        r.ginput[part, :] += norm_back(gnormed, hat, inverse, r.norm[0:1, :])
        r.grow[0:1, :] += jnp.sum(gnormed * hat, axis=0, keepdims=True)
        r.grow[1:2, :] += jnp.sum(gnormed, axis=0, keepdims=True)

    for i in range(max(tiles, 4)):
        if i < tiles:
            settle_inputs(i)
        if i == 0:
            for p in reduce.of("q"):
                reduce.second(p)
            for p in late:
                reduce.combine(p)
        if i == 1:
            for p in reduce.of("q"):
                reduce.third(p)
            for p in late:
                reduce.second(p)
        if i == 2:
            for p in late:
                reduce.third(p)
            for p in reduce.of("q"):
                square += reduce.final(p)
    for p in late:
        square += reduce.final(p)
    r.grow[4:5, :] = jnp.broadcast_to(square, (1, D))
    r.small_seq[me.s] = r.grow[...]
    for k, o in enumerate(me.seq_others):
        copies.push(
            r.grow, r.small_seq.at[me.s], 2 * n_dp + 1 + k, 2 * n_dp + me.s, (me.d, o)
        )
    for o in me.seq_others:
        copies.arrived(r.small_seq.at[o], 2 * n_dp + o, (me.d, o))
    total = r.small_seq[0]
    for o in range(1, n_seq):
        total += r.small_seq[o]
    r.small_dp[me.d] = total
    for k, o in enumerate(me.dp_others):
        copies.push(
            r.small_dp.at[me.d], r.small_dp.at[me.d], n_dp + 1 + k, n_dp + me.d, (o, me.s)
        )
    for p in range(len(reduce.parts)):
        reduce.settle(p)
    for o in me.dp_others:
        copies.arrived(r.small_dp.at[o], n_dp + o, (o, me.s))
    total = r.small_dp[0]
    for o in range(1, n_dp):
        total += r.small_dp[o]
    r.small[...] = total
    for row in range(rows):
        exchange_back.finish(row)
    copies.finish()


DMA = pltpu.SemaphoreType.DMA


class Shapes:
    def __init__(self, inputs, segment_ids):
        self.n_dp, self.n_seq = lax.axis_size("dp"), lax.axis_size("seq")
        self.rows, self.local = inputs.shape[0], inputs.shape[1]
        self.seq_len = segment_ids.shape[1]
        self.tokens = self.rows * self.local
        self.blocks = self.local // QB
        edge = 16 * len(edge_levels(self.local))
        self.edge = (self.rows, 2, edge, 2 * D)
        self.far = (self.rows, self.n_seq, 16, 2 * D)
        ext = [(ext_rows(self.local, self.seq_len, lv), 2 * D) for lv in range(LEVELS)]
        self.ext_low = [pltpu.VMEM(shape, BF) for shape in ext]
        self.ext_wide = [pltpu.VMEM(shape, F32) for shape in ext]
        self.edge_sems = Exchange.sems(self.rows, self.n_seq)
        self.heads = (self.rows, self.local, D)
        parts = len(grad_parts(self.n_dp, self.n_seq))
        self.sems = 2 * self.n_dp + self.n_seq
        self.sems += 5 * Gather.sems(self.n_dp, self.n_seq)
        self.sems += parts * Reduce.sems(self.n_dp, self.n_seq)
        self.pairs = (self.rows, self.local, 2 * D)


def run_layer(z, inputs, segment_ids, out_grad, w_qkv, w_out, w_up, w_down, norm_params):
    norm_pad = jnp.pad(norm_params, ((0, 4), (0, 128 - norm_params.shape[1])))
    flat = (z.tokens, D)
    named = layer_scratch(z)
    return pl.pallas_call(
        functools.partial(layer_kernel, z, list(named)),
        out_shape=[
            sds(flat, BF),
            sds(flat, F32),
            sds((D // z.n_dp, FF), BF),
            sds((D // z.n_dp, 4 * D), BF),
            sds((D, FF // z.n_dp), BF),
            sds((8, D), F32),
        ],
        in_specs=[VM] * len(INPUTS),
        out_specs=[VM] * len(OUTPUTS),
        scratch_shapes=[
            *named.values(),
            *z.ext_low,
            *z.ext_wide,
            *Reduce.scratch(z.n_dp, z.n_seq),
        ],
        compiler_params=params(0),
        name="layer",
    )(
        inputs.reshape(flat),
        segment_ids,
        out_grad.reshape(flat),
        w_qkv,
        w_out,
        w_up,
        w_down,
        norm_pad,
    )


def run_adam(z, sums, masters, firsts, seconds):
    shapes = [sds(w.shape, F32) for w in masters]
    norm_shape = sds(firsts[4].shape, F32)
    return pl.pallas_call(
        functools.partial(adam_kernel, z.n_dp),
        out_shape=shapes
        + [norm_shape]
        + shapes
        + [norm_shape]
        + shapes
        + [norm_shape, sds((1, 1), F32)],
        in_specs=[VM] * 18,
        out_specs=[VM] * 16,
        compiler_params=params(),
        name="adam",
    )(*sums, *masters, *firsts, *seconds)


def on_device(
    inputs,
    segment_ids,
    out_grad,
    w_qkv,
    w_out,
    w_up,
    w_down,
    norm_params,
    qkv_first,
    qkv_second,
    out_first,
    out_second,
    up_first,
    up_second,
    down_first,
    down_second,
    norm_first,
    norm_second,
):
    z = Shapes(inputs, segment_ids)
    masters = [w_qkv, w_out, w_up, w_down]
    firsts = [qkv_first, out_first, up_first, down_first, norm_first]
    seconds = [qkv_second, out_second, up_second, down_second, norm_second]
    outputs, input_grad, *sums = run_layer(
        z, inputs, segment_ids, out_grad, *masters, norm_params
    )
    updated = run_adam(z, sums, masters, firsts, seconds)
    return (
        outputs.reshape(z.heads),
        input_grad.reshape(z.heads),
        updated[15].reshape(()),
        *updated[0:15],
    )


def solution(mesh):
    tokens = P("dp", "seq", None)
    rows, stack, lanes = P("dp", None), P(None, "dp", None), P(None, "dp")
    moments = (stack, stack, rows, rows, rows, rows, rows, rows, lanes, lanes)
    weights = (stack, rows, rows, rows)
    return jax.shard_map(
        on_device,
        mesh=mesh,
        in_specs=(tokens, rows, tokens, *weights, lanes, *moments),
        out_specs=(tokens, tokens, P(), *weights, lanes, *weights, lanes, *weights, lanes),
        check_vma=False,
    )
```

```python
import functools
import math

import jax
import jax.numpy as jnp
from jax import lax
from jax.experimental import pallas as pl
from jax.experimental.pallas import tpu as pltpu
from jax.sharding import PartitionSpec as P

D = 512
HEADS = 8
DH = 64
FF = 2048
LEVELS = 7
DOCS = 4
QB = 128
NKEY = 512
CHUNK = 512
LIMIT = 63
PAIRS = HEADS // 2

masked_score = -1e30
beta_one = 0.9
beta_two = 0.999
bias_first = 1.0 - 0.9**10
bias_second = 1.0 - 0.999**10
learn_rate = 0.1
weight_decay = 0.1
epsilon = 1e-08
clip_norm = 1.0

BF = jnp.bfloat16
F32 = jnp.float32
MESH = pl.DeviceIdType.MESH
VM = pl.BlockSpec(memory_space=pltpu.VMEM)
ANY = pl.BlockSpec(memory_space=pl.ANY)

NN = ((1,), (0,))
NT = ((1,), (1,))
TN = ((0,), (0,))


def mm(left, right, dims):
    return lax.dot_general(left, right, (dims, ((), ())), preferred_element_type=F32)


def params(cid=None):
    if cid is None:
        return pltpu.CompilerParams(vmem_limit_bytes=LIMIT * 2**20)
    return pltpu.CompilerParams(
        vmem_limit_bytes=LIMIT * 2**20, collective_id=cid, has_side_effects=True
    )


def sds(shape, dtype):
    return jax.ShapeDtypeStruct(shape, dtype)


def level_offset(local, level):
    return local - (local >> (level - 1))


def edge_levels(local):
    return [lv for lv in range(LEVELS) if (local >> lv) >= 16]


def far_levels(local):
    return [lv for lv in range(LEVELS) if (local >> lv) < 16]


def ext_rows(local, seq_len, level):
    return ((local >> level) if (local >> level) >= 16 else (seq_len >> level)) + 32


def key_rows(level):
    return max(QB >> level, 16) + 32


def key_start(level):
    return sum(key_rows(lv) for lv in range(level))


def window_start(level, block, offset, local):
    span = 16 << level
    if (local >> level) >= 16:
        if span <= QB:
            return block * (QB >> level)
        return (block * QB) // span * 16
    return (offset + block * QB) // span * 16


def averaging(local):
    row = lax.broadcasted_iota(jnp.int32, (local, local), 0)
    col = lax.broadcasted_iota(jnp.int32, (local, local), 1)
    total = jnp.zeros((local, local), F32)
    for lv in range(1, LEVELS):
        at = lax.shift_right_logical(col, lv) + level_offset(local, lv)
        total = jnp.where(at == row, 2.0**-lv, total)
    return total.astype(BF)


def norm_parts(values):
    center = jnp.mean(values, axis=-1, keepdims=True)
    centered = values - center
    spread = jnp.mean(centered * centered, axis=-1, keepdims=True)
    inverse = lax.rsqrt(spread + 1e-05)
    return centered * inverse, inverse


def norm_back(grad_in, normed, inverse, gain):
    scaled = grad_in * gain
    return inverse * (
        scaled
        - jnp.mean(scaled, axis=-1, keepdims=True)
        - normed * jnp.mean(scaled * normed, axis=-1, keepdims=True)
    )


def document_bounds(seg_row, seq_len):
    return [
        jnp.sum(jnp.where(seg_row < doc, 1.0, 0.0), axis=1, keepdims=True)
        for doc in range(1, DOCS)
    ]


def fill_bias(starts, first_query, seq_len, bias_ref):
    qpos = first_query + lax.broadcasted_iota(jnp.int32, (1, QB), 1)
    qf = qpos.astype(F32)
    low = jnp.zeros((1, QB), F32)
    high = jnp.full((1, QB), float(seq_len), F32)
    for start in starts:
        low = jnp.where(qf >= start, jnp.maximum(low, start), low)
        high = jnp.where(qf < start, jnp.minimum(high, start), high)
    for lv in range(LEVELS):
        span = 16 << lv
        rows = key_rows(lv)
        if span <= QB:
            key_first = first_query // (1 << lv) - 16
        else:
            key_first = first_query // span * 16 - 16
        index = key_first + lax.broadcasted_iota(jnp.int32, (rows, QB), 0)
        begin = (index * (1 << lv)).astype(F32)
        end = begin + float((1 << lv) - 1)
        block = lax.div(qpos, span)
        lo = jnp.maximum(low, ((block - 1) * span).astype(F32))
        hi = jnp.minimum(high, ((block + 2) * span).astype(F32))
        allowed = (begin >= lo) & (end < hi)
        if lv > 0:
            half = span // 2
            parent = lax.div(qpos, half)
            inner_lo = ((parent - 1) * half).astype(F32)
            inner_hi = ((parent + 2) * half).astype(F32)
            allowed = allowed & ((begin < inner_lo) | (begin >= inner_hi))
        bias_ref[key_start(lv) : key_start(lv) + rows, :] = jnp.where(
            allowed, lv * math.log(2.0), masked_score
        )


def build_ext(row, local, kv_ref, coarse_ref, edge_ref, far_ref, ext):
    count = far_ref.shape[1]
    for lv in range(LEVELS):
        rows = local >> lv
        if rows >= 16:
            ext[lv][0:16, :] = edge_ref[row, 0, 16 * lv : 16 * lv + 16, :]
            if lv == 0:
                ext[lv][16 : 16 + rows, :] = kv_ref[row]
            else:
                at = level_offset(local, lv)
                ext[lv][16 : 16 + rows, :] = coarse_ref[row, at : at + rows, :]
            ext[lv][16 + rows : 32 + rows, :] = edge_ref[row, 1, 16 * lv : 16 * lv + 16, :]
        else:
            at = level_offset(local, lv) - (local - 16)
            blank = jnp.zeros((16, 2 * D), F32)
            pieces = [blank]
            for owner in range(count):
                pieces.append(far_ref[row, owner].astype(F32)[at : at + rows, :])
            pieces.append(blank)
            ext[lv][...] = jnp.concatenate(pieces, axis=0).astype(BF)


def gather_keys(ext, block, offset, local, keys_ref):
    for lv in range(LEVELS):
        start = pl.multiple_of(window_start(lv, block, offset, local), 16)
        at = key_start(lv)
        keys_ref[at : at + key_rows(lv), :] = ext[lv][pl.ds(start, key_rows(lv)), :]


def lane_halves(values):
    lane = lax.broadcasted_iota(jnp.int32, values.shape, 1)
    zero = jnp.zeros_like(values)
    return jnp.concatenate(
        [jnp.where(lane < DH, values, zero), jnp.where(lane >= DH, values, zero)], axis=0
    )


def own_halves(pair_t):
    n = pair_t.shape[1] // 2
    sub = lax.broadcasted_iota(jnp.int32, (2 * DH, n), 0)
    return jnp.where(sub < DH, pair_t[:, :n], pair_t[:, n:])


def adam_kernel(n_dp, *refs):
    gup, gmix, gdown, small = refs[0:4]
    weights, firsts, seconds = refs[4:8], refs[8:13], refs[13:18]
    passed, outs, passed_out = refs[18:20], refs[20:36], refs[36:38]
    for here, there in zip(passed, passed_out):
        there[...] = here[...]

    new_w, norm_grad, new_m, new_s, grad_norm = (
        outs[0:4],
        outs[4],
        outs[5:10],
        outs[10:15],
        outs[15],
    )
    own = small[0:4, :]
    square = jnp.sum(jnp.sum(own * own, axis=0, keepdims=True), axis=1, keepdims=True)
    root = jnp.sqrt(square + small[4:5, 0:1])
    grad_norm[...] = root
    factor = jnp.minimum(1.0, clip_norm / root)

    def moments(clipped, first, second):
        return (
            beta_one * first + (1.0 - beta_one) * clipped,
            beta_two * second + (1.0 - beta_two) * clipped * clipped,
        )

    def update(weight, grad, first, second):
        mean, sq = moments(grad * factor, first, second)
        change = mean / bias_first / (jnp.sqrt(sq / bias_second) + epsilon) + weight_decay * weight
        return weight - learn_rate * change, mean, sq

    for c in range(3):
        w, m, s = update(
            weights[0][c], gmix[:, c * D : c * D + D].astype(F32), firsts[0][c], seconds[0][c]
        )
        new_w[0][c], new_m[0][c], new_s[0][c] = w, m, s
    for at, grad in ((1, gmix[:, 3 * D : 4 * D]), (2, gup[...]), (3, gdown[...])):
        grad = grad.astype(F32)
        if at == 3:
            grad = grad.T
        w, m, s = update(weights[at][...], grad, firsts[at][...], seconds[at][...])
        new_w[at][...], new_m[at][...], new_s[at][...] = w, m, s
    width = D // n_dp
    lane = lax.axis_index("dp") * width
    rolled = pltpu.roll(small[...], D - lane, 1)[0:4, 0:width]
    clipped = rolled * factor
    norm_grad[...] = clipped
    m, s = moments(clipped, firsts[4][...], seconds[4][...])
    new_m[4][...], new_s[4][...] = m, s


class Copies:
    def __init__(self, send, recv):
        self.send, self.recv = send, recv
        self.started = []

    def push(self, src, dst, send_at, recv_at, device, alone=True):
        copy = pltpu.make_async_remote_copy(
            src_ref=src,
            dst_ref=dst,
            send_sem=self.send.at[send_at],
            recv_sem=self.recv.at[recv_at],
            device_id=device,
            device_id_type=MESH,
        )
        copy.start()
        if alone:
            self.started.append(copy)

    def arrived(self, dst, recv_at, device):
        pltpu.make_async_remote_copy(
            src_ref=dst,
            dst_ref=dst,
            send_sem=self.send.at[0],
            recv_sem=self.recv.at[recv_at],
            device_id=device,
            device_id_type=MESH,
        ).wait_recv()

    def left(self, src, send_at, device):
        pltpu.make_async_remote_copy(
            src_ref=src,
            dst_ref=src,
            send_sem=self.send.at[send_at],
            recv_sem=self.recv.at[0],
            device_id=device,
            device_id_type=MESH,
        ).wait_send()

    def finish(self):
        for copy in self.started:
            copy.wait_send()
        self.started = []


def greet(peers):
    barrier = pltpu.get_barrier_semaphore()
    for peer in peers:
        pl.semaphore_signal(barrier, inc=1, device_id=peer, device_id_type=MESH)
    pl.semaphore_wait(barrier, len(peers))


class Place:
    def __init__(self, n_dp, n_seq):
        self.n_dp, self.n_seq = n_dp, n_seq
        self.d, self.s = lax.axis_index("dp"), lax.axis_index("seq")
        self.z, self.y = lax.div(self.d, 2), lax.rem(self.d, 2)
        self.hi, self.core = lax.div(self.s, 2), lax.rem(self.s, 2)
        self.depth, self.high = n_dp // 2, n_seq // 2
        self.mate = self.s + 1 - 2 * self.core
        self.flip = self.d + 1 - 2 * self.y
        self.seq_others = [lax.rem(self.s + k, n_seq) for k in range(1, n_seq)]
        self.dp_others = [lax.rem(self.d + k, n_dp) for k in range(1, n_dp)]

    def greet(self):
        greet(
            [(self.d, o) for o in self.seq_others] + [(o, self.s) for o in self.dp_others]
        )


class Gather:
    def __init__(self, place, parts, copies, base, send_base, measure):
        self.at, self.parts, self.copies, self.base = place, parts, copies, base
        self.send_base, self.measure = send_base, measure
        self.stride = self.sems(place.n_dp, place.n_seq)

    @staticmethod
    def sems(n_dp, n_seq):
        return 2 * (n_dp // 2) + 2

    def split(self, p):
        high = self.at.high
        return p >= 3 and high > 1 and self.parts[p][3] % (32 * high) == 0

    def piece(self, p, shard, core, hi):
        _, whole, lead, rows = self.parts[p]
        n = rows // 2
        start = shard * rows + core * n
        if self.split(p):
            n = n // self.at.high
            start = start + hi * n
        if lead is None:
            return whole.at[pl.ds(pl.multiple_of(start, n), n), :]
        if lead == "blocks":
            row = pl.multiple_of(lax.rem(start, CHUNK), n)
            return whole.at[lax.div(start, CHUNK), pl.ds(row, n), :]
        return whole.at[lead[0] : lead[1], pl.ds(pl.multiple_of(start, n), n), :]

    def sem(self, p, stage, index=0):
        at = self.base + p * self.stride
        sizes = (self.at.depth, self.at.depth, 1)
        return at + sum(sizes[:stage]) + index

    def push(self, p, here, recv_at, device):
        self.copies.push(here, here, self.send_base + p, recv_at, device, alone=False)

    def share(self, p, rows):
        _, whole, lead, _ = self.parts[p]
        if lead is None:
            return whole.at[0:rows, :]
        if lead == "blocks":
            return self.measure.at[0 : rows * D // FF, :]
        return whole.at[lead[0] : lead[1], 0:rows, :]

    def load(self, p):
        own, whole, lead, rows = self.parts[p]
        start = pl.multiple_of(self.at.d * rows, rows)
        if isinstance(lead, tuple):
            for c in range(*lead):
                whole[c, pl.ds(start, rows), :] = own[c][...].astype(BF)
        elif isinstance(own, list):
            for c, item in enumerate(own):
                whole[pl.ds(start, rows), c * D : c * D + D] = item[...].astype(BF)
        elif lead is None:
            whole[pl.ds(start, rows), :] = own[...].astype(BF)
        elif lead == "blocks":
            row = pl.multiple_of(lax.rem(start, CHUNK), rows)
            whole[lax.div(start, CHUNK), pl.ds(row, rows), :] = own[...].astype(BF)

    def start(self, p):
        me = self.at
        self.load(p)
        mine = self.piece(p, me.d, me.core, me.hi)
        for k in range(1, me.depth):
            other = lax.rem(me.z + k, me.depth) * 2 + me.y
            self.push(p, mine, self.sem(p, 0, me.z), (other, me.s))
        self.push(p, mine, self.sem(p, 1, me.z), (me.flip, me.s))

    def onward(self, p, shard):
        me = self.at
        here = self.piece(p, shard, me.core, me.hi)
        if self.split(p):
            for kh in range(1, me.high):
                other = lax.rem(me.hi + kh, me.high) * 2 + me.core
                self.push(p, here, self.sem(p, 2), (me.d, other))
        self.push(p, here, self.sem(p, 3), (me.d, me.mate))

    def relay_z(self, p):
        me = self.at
        for k in range(1, me.depth):
            zz = lax.rem(me.z + k, me.depth)
            shard = zz * 2 + me.y
            here = self.piece(p, shard, me.core, me.hi)
            self.copies.arrived(here, self.sem(p, 0, zz), (shard, me.s))
            self.push(p, here, self.sem(p, 1, zz), (me.flip, me.s))
            self.onward(p, shard)

    def relay_y(self, p):
        me = self.at
        for k in range(me.depth):
            zz = lax.rem(me.z + k, me.depth)
            shard = zz * 2 + 1 - me.y
            here = self.piece(p, shard, me.core, me.hi)
            self.copies.arrived(here, self.sem(p, 1, zz), (me.flip, me.s))
            self.onward(p, shard)

    def relay_x(self, p):
        me = self.at
        if not self.split(p):
            return
        rows = self.parts[p][3] // (2 * me.high) * (me.n_dp - 1) * (me.high - 1)
        mirror = lax.rem(me.hi + 1, me.high) * 2 + me.core
        self.copies.arrived(self.share(p, rows), self.sem(p, 2), (me.d, mirror))
        for kh in range(1, me.high):
            h = lax.rem(me.hi + kh, me.high)
            for k in range(1, me.n_dp):
                shard = lax.rem(me.d + k, me.n_dp)
                here = self.piece(p, shard, me.core, h)
                self.push(p, here, self.sem(p, 3), (me.d, me.mate))

    def settle(self, p):
        me = self.at
        rows = self.parts[p][3] // 2 * (me.n_dp - 1)
        self.copies.arrived(self.share(p, rows), self.sem(p, 3), (me.d, me.mate))

    def finish(self):
        me = self.at
        for p, part in enumerate(self.parts):
            ref = self.share(p, part[3] * (me.n_dp - 1))
            self.copies.left(ref, self.send_base + p, (me.d, me.mate))


class Exchange:
    def __init__(self, place, personal, edge_in, far_in, edge_out, far_out, send, recv):
        self.at, self.personal = place, personal
        self.edge_in, self.far_in, self.edge_out, self.far_out = edge_in, far_in, edge_out, far_out
        self.send, self.recv = send, recv

    @staticmethod
    def sems(rows, n_seq):
        return rows * (2 + n_seq)

    def edge(self, row, way, device):
        base = row * (2 + self.at.n_seq)
        return pltpu.make_async_remote_copy(
            src_ref=self.edge_in.at[row, way],
            dst_ref=self.edge_out.at[row, 1 - way],
            send_sem=self.send.at[base + way],
            recv_sem=self.recv.at[base + 1 - way],
            device_id=(self.at.d, device),
            device_id_type=MESH,
        )

    def far_rows(self, row, other):
        if self.personal:
            return self.far_in.at[row, other]
        local = self.far_in.shape[1]
        return self.far_in.at[row, local - 16 : local, :]

    def far(self, row, k, other):
        base = row * (2 + self.at.n_seq) + 2
        return pltpu.make_async_remote_copy(
            src_ref=self.far_rows(row, other),
            dst_ref=self.far_out.at[row, self.at.s],
            send_sem=self.send.at[base + k],
            recv_sem=self.recv.at[base + self.at.s],
            device_id=(self.at.d, other),
            device_id_type=MESH,
        )

    def start(self, row):
        s, n_seq = self.at.s, self.at.n_seq

        @pl.when(s > 0)
        def _():
            self.edge(row, 0, s - 1).start()

        @pl.when(s < n_seq - 1)
        def _():
            self.edge(row, 1, s + 1).start()

        for k, other in enumerate(self.at.seq_others):
            self.far(row, k, other).start()
        self.far_out[row, s] = self.far_rows(row, s)[...]

    def arrive(self, row):
        s, n_seq = self.at.s, self.at.n_seq
        blank = jnp.zeros(self.edge_out.shape[2:], BF)

        @pl.when(s > 0)
        def _():
            self.edge(row, 1, s - 1).wait_recv()

        @pl.when(s == 0)
        def _():
            self.edge_out[row, 0] = blank

        @pl.when(s < n_seq - 1)
        def _():
            self.edge(row, 0, s + 1).wait_recv()

        @pl.when(s == n_seq - 1)
        def _():
            self.edge_out[row, 1] = blank

        base = row * (2 + n_seq) + 2
        for other in self.at.seq_others:
            here = self.far_out.at[row, other]
            pltpu.make_async_remote_copy(
                src_ref=here,
                dst_ref=here,
                send_sem=self.send.at[base],
                recv_sem=self.recv.at[base + other],
                device_id=(self.at.d, other),
                device_id_type=MESH,
            ).wait_recv()

    def finish(self, row):
        s, n_seq = self.at.s, self.at.n_seq

        @pl.when(s > 0)
        def _():
            self.edge(row, 0, s - 1).wait_send()

        @pl.when(s < n_seq - 1)
        def _():
            self.edge(row, 1, s + 1).wait_send()

        for k, other in enumerate(self.at.seq_others):
            self.far(row, k, other).wait_send()


class SmallSum:
    def __init__(self, place, copies, own, seq_in, dp_in, base):
        self.at, self.copies, self.own = place, copies, own
        self.seq_in, self.dp_in, self.base = seq_in, dp_in, base

    def start(self):
        me = self.at
        self.seq_in[me.s] = self.own[...]
        for k, o in enumerate(me.seq_others):
            self.copies.push(
                self.own, self.seq_in.at[me.s], self.base + 1 + k, self.base + me.s, (me.d, o)
            )

    def turn(self):
        me = self.at
        for o in me.seq_others:
            self.copies.arrived(self.seq_in.at[o], self.base + o, (me.d, o))
        total = self.seq_in[0]
        for o in range(1, me.n_seq):
            total += self.seq_in[o]
        self.dp_in[me.d] = total
        base = self.base + me.n_seq
        for k, o in enumerate(me.dp_others):
            here = self.dp_in.at[me.d]
            self.copies.push(here, here, base + 1 + k, base + me.d, (o, me.s))

    def finish(self):
        me = self.at
        for o in me.dp_others:
            self.copies.arrived(self.dp_in.at[o], self.base + me.n_seq + o, (o, me.s))
        total = self.dp_in[0]
        for o in range(1, me.n_dp):
            total += self.dp_in[o]
        return total


def grad_parts(n_dp, n_seq):
    if D // n_seq % 128:
        return [
            (0, 0, FF, True, True, "up"),
            (1, 0, FF, False, False, "down"),
            (2, 0, 4 * D, True, True, "kv"),
        ]
    return [
        (0, 0, FF // 2, True, True, "first"),
        (0, FF // 2, FF, True, True, "up"),
        (1, 0, FF, False, False, "down"),
        (2, 3 * D, 4 * D, True, True, "out"),
        (2, 0, D, True, False, "q"),
        (2, D, 2 * D, True, True, "kv"),
        (2, 2 * D, 3 * D, True, False, "kv"),
    ]


def block_shape(part, n_dp, n_seq):
    _, lo, hi, by_rows, _, _ = part
    if by_rows:
        return (D // n_dp, (hi - lo) // n_seq)
    return (D // n_seq, (hi - lo) // n_dp)


class Reduce:
    def __init__(self, place, sources, finals, buffers, copies, base):
        self.at, self.sources, self.finals = place, sources, finals
        self.parts = grad_parts(place.n_dp, place.n_seq)
        n = len(self.parts)
        groups = [buffers[i * n : i * n + n] for i in range(5)]
        self.core_in, self.held, self.high_in, self.y_in, self.z_in = groups
        self.copies, self.base = copies, base
        self.stride = self.sems(place.n_dp, place.n_seq)

    @staticmethod
    def sems(n_dp, n_seq):
        return 2 + (n_seq // 2 - 1) + (n_dp // 2 - 1) + 1

    @staticmethod
    def scratch(n_dp, n_seq):
        high, depth = n_seq // 2, n_dp // 2
        groups = [[], [], [], [], []]
        for part in grad_parts(n_dp, n_seq):
            _, lo, up, by_rows, first, _ = part
            a, b = block_shape(part, n_dp, n_seq)
            shapes = [
                (D, (up - lo) // 2) if by_rows else (FF // CHUNK, D // 2, CHUNK),
                (high, depth, 2, a, b),
                (high - 1, depth, 2, a, b) if first else (high - 1, depth, a, b),
                (depth, a, b) if first else (high, depth, a, b),
                (depth - 1, a, b),
            ]
            for group, shape in zip(groups, shapes):
                group.append(pltpu.VMEM(shape, BF))
        return [item for group in groups for item in group]

    def of(self, *stages):
        return [p for p, part in enumerate(self.parts) if part[5] in stages]

    def sem(self, p, stage, index=0):
        sizes = (1, 1, self.at.high - 1, self.at.depth - 1)
        return self.base + p * self.stride + sum(sizes[:stage]) + index

    def start(self, p):
        me = self.at
        src, lo, up, by_rows, _, _ = self.parts[p]
        ref = self.sources[src]
        which = 1 - me.core
        if by_rows:
            w = (up - lo) // 2
            half = ref.at[:, pl.ds(pl.multiple_of(lo + which * w, 128), w)]
        else:
            w = D // 2
            half = ref.at[:, pl.ds(pl.multiple_of(which * w, w), w), :]
        self.copies.push(half, self.core_in[p], self.sem(p, 0), self.sem(p, 0), (me.d, me.mate))

    def push_y(self, p, held):
        me = self.at
        self.copies.push(held, self.y_in[p], self.sem(p, 1), self.sem(p, 1), (me.flip, me.s))

    def take_y(self, p):
        me = self.at
        self.copies.arrived(self.y_in[p], self.sem(p, 1), (me.flip, me.s))


    def push_high(self, p, y):
        me = self.at
        for k in range(1, me.high):
            h = lax.rem(me.hi + k, me.high)
            src = self.held[p].at[h] if y is None else self.held[p].at[h, :, y]
            self.copies.push(
                src,
                self.high_in[p].at[me.high - k - 1],
                self.sem(p, 2, k - 1),
                self.sem(p, 2, me.high - k - 1),
                (me.d, h * 2 + me.core),
            )

    def take_high(self, p):
        me = self.at
        for k in range(1, me.high):
            h = lax.rem(me.hi + k, me.high)
            self.copies.arrived(
                self.high_in[p].at[k - 1], self.sem(p, 2, k - 1), (me.d, h * 2 + me.core)
            )

    def combine(self, p):
        me = self.at
        part = self.parts[p]
        src, lo, up, by_rows, first, _ = part
        a, b = block_shape(part, me.n_dp, me.n_seq)
        self.copies.arrived(self.core_in[p], self.sem(p, 0), (me.d, me.mate))
        theirs, held, source = self.core_in[p], self.held[p], self.sources[src]
        for h in range(me.high):
            for shard in range(me.n_dp):
                which = me.core * me.high + h
                if by_rows:
                    r = slice(shard * a, shard * a + a)
                    left = source[r, pl.ds(pl.multiple_of(lo + which * b, 128), b)]
                    right = theirs[r, h * b : h * b + b]
                else:
                    block, lane = shard * b // CHUNK, shard * b % CHUNK
                    lanes = slice(lane, lane + b)
                    left = source[block, pl.ds(pl.multiple_of(which * a, a), a), lanes]
                    right = theirs[block, h * a : h * a + a, lanes]
                total = left.astype(F32) + right.astype(F32)
                held[h, shard // 2, shard % 2] = total.astype(BF)
        if first:
            self.push_high(p, None)
        else:
            self.push_y(p, held.at[:, :, 1 - me.y])

    def add_high(self, p):
        me = self.at
        held = self.held[p]
        self.take_high(p)
        first = self.parts[p][4]
        for zz in range(me.depth):
            for yy in (0, 1) if first else (me.y,):
                value = held[me.hi, zz, yy].astype(F32)
                for k in range(me.high - 1):
                    more = self.high_in[p][k, zz, yy] if first else self.high_in[p][k, zz]
                    value += more.astype(F32)
                held[me.hi, zz, yy] = value.astype(BF)

    def second(self, p):
        me = self.at
        held = self.held[p]
        if self.parts[p][4]:
            self.add_high(p)
            self.push_y(p, held.at[me.hi, :, 1 - me.y])
        else:
            self.take_y(p)
            for h in range(me.high):
                for zz in range(me.depth):
                    value = held[h, zz, me.y].astype(F32) + self.y_in[p][h, zz].astype(F32)
                    held[h, zz, me.y] = value.astype(BF)
            self.push_high(p, me.y)

    def third(self, p):
        me = self.at
        held = self.held[p]
        if self.parts[p][4]:
            self.take_y(p)
            for zz in range(me.depth):
                value = held[me.hi, zz, me.y].astype(F32) + self.y_in[p][zz].astype(F32)
                held[me.hi, zz, me.y] = value.astype(BF)
        else:
            self.add_high(p)
        for k in range(1, me.depth):
            zz = lax.rem(me.z + k, me.depth)
            self.copies.push(
                held.at[me.hi, zz, me.y],
                self.z_in[p].at[me.depth - k - 1],
                self.sem(p, 3, k - 1),
                self.sem(p, 3, me.depth - k - 1),
                (zz * 2 + me.y, me.s),
            )

    def place_of(self, p, owner):
        part = self.parts[p]
        src, lo, up, by_rows, _, _ = part
        a, b = block_shape(part, self.at.n_dp, self.at.n_seq)
        which = lax.rem(owner, 2) * self.at.high + lax.div(owner, 2)
        if by_rows:
            return self.finals[src].at[:, pl.ds(pl.multiple_of(lo + which * b, 128), b)]
        return self.finals[src].at[pl.ds(pl.multiple_of(which * a, a), a), :]

    def final(self, p):
        me = self.at
        value = self.held[p][me.hi, me.z, me.y].astype(F32)
        for k in range(1, me.depth):
            zz = lax.rem(me.z + k, me.depth)
            self.copies.arrived(self.z_in[p].at[k - 1], self.sem(p, 3, k - 1), (zz * 2 + me.y, me.s))
            value += self.z_in[p][k - 1].astype(F32)
        low = value.astype(BF)
        here = self.place_of(p, me.s)
        here[...] = low
        value = low.astype(F32)
        return jnp.sum(jnp.sum(value * value, axis=0, keepdims=True), axis=1, keepdims=True)

    def publish(self, p):
        me = self.at
        here = self.place_of(p, me.s)
        for o in me.seq_others:
            self.copies.push(here, here, self.sem(p, 4), self.sem(p, 4), (me.d, o), alone=False)

    def share(self, p):
        part = self.parts[p]
        a, b = block_shape(part, self.at.n_dp, self.at.n_seq)
        n = self.at.n_seq - 1
        if part[3]:
            return self.finals[part[0]].at[:, 0 : n * b]
        return self.finals[part[0]].at[0 : n * a, :]

    def settle(self, p):
        me = self.at
        self.copies.arrived(self.share(p), self.sem(p, 4), (me.d, me.mate))
        self.copies.left(self.share(p), self.sem(p, 4), (me.d, me.mate))


class Named:
    def __init__(self, names, refs):
        for name, ref in zip(names, refs):
            setattr(self, name, ref)


INPUTS = ["x_far", "seg", "og_far", "wqkv_far", "wout_far", "wup_far", "wdown_far", "norm_own"]
OUTPUTS = ["out_far", "ginput_far", "sup", "smix", "sdown", "small"]
FETCHES = 8 + FF // D


def layer_scratch(z):
    tokens = (z.tokens, D)
    tall = (max(z.tokens, 2 * NKEY), D)
    return {
        "slots": pltpu.VMEM((z.n_dp, 8, 128), F32),
        "norm": pltpu.VMEM((8, D), F32),
        "fqkv": pltpu.VMEM((3, D, D), BF),
        "fout": pltpu.VMEM((D, D), BF),
        "fup": pltpu.VMEM((D, FF), BF),
        "fdown": pltpu.VMEM((FF // CHUNK, CHUNK, D), BF),
        "normed": pltpu.VMEM(tokens, BF),
        "q": pltpu.VMEM(tokens, BF),
        "kv": pltpu.VMEM(z.pairs, BF),
        "coarse": pltpu.VMEM(z.pairs, BF),
        "edge_own": pltpu.VMEM(z.edge, BF),
        "edge_near": pltpu.VMEM(z.edge, BF),
        "edge_back": pltpu.VMEM(z.edge, BF),
        "far_all": pltpu.VMEM(z.far, BF),
        "gfar": pltpu.VMEM(z.far, BF),
        "far_back": pltpu.VMEM(z.far, BF),
        "keys": pltpu.VMEM((NKEY, 2 * D), BF),
        "bias": pltpu.VMEM((NKEY, QB), F32),
        "mixed": pltpu.VMEM(tokens, BF),
        "totals": pltpu.VMEM((z.rows, z.blocks, PAIRS, 2 * QB), F32),
        "second_t": pltpu.VMEM((D, z.tokens), BF),
        "og_t": pltpu.VMEM((D, z.tokens), BF),
        "acc": pltpu.VMEM(tall, F32),
        "gsec": pltpu.VMEM(tall, F32),
        "hid": pltpu.VMEM(tall, BF),
        "gpre": pltpu.VMEM(tall, BF),
        "gmix": pltpu.VMEM((D, 4 * D), BF),
        "grow": pltpu.VMEM((8, D), F32),
        "small_seq": pltpu.VMEM((z.n_seq, 8, D), F32),
        "small_dp": pltpu.VMEM((z.n_dp, 8, D), F32),
        "square": pltpu.VMEM((8, 128), F32),
        "square_seq": pltpu.VMEM((z.n_seq, 8, 128), F32),
        "square_dp": pltpu.VMEM((z.n_dp, 8, 128), F32),
        "send": DMA((z.sems,)),
        "recv": DMA((z.sems,)),
        "edge_send": DMA((z.edge_sems,)),
        "edge_recv": DMA((z.edge_sems,)),
        "back_send": DMA((z.edge_sems,)),
        "back_recv": DMA((z.edge_sems,)),
        "local_sem": DMA((FETCHES + 1 + z.tokens // QB,)),
        "x": pltpu.VMEM(tokens, BF),
        "og": pltpu.VMEM(tokens, BF),
        "ginput": pltpu.VMEM(tokens, F32),
    }


def layer_kernel(z, names, *refs):
    count = len(INPUTS) + len(OUTPUTS) + len(names)
    r = Named(INPUTS + OUTPUTS + names, refs[:count])
    ext = refs[count : count + LEVELS]
    gext = refs[count + LEVELS : count + 2 * LEVELS]
    buffers = refs[count + 2 * LEVELS :]
    rows, local, tokens, seq_len = z.rows, z.local, z.tokens, z.seq_len
    n_dp, n_seq = z.n_dp, z.n_seq
    shard = D // n_dp
    down = FF // n_dp
    own_down = r.gsec.at[0:down, :]
    own_out = r.gsec.at[down : down + shard, :]
    own_up = [
        r.gsec.at[down + shard * (c + 1) : down + shard * (c + 2), :] for c in range(FF // D)
    ]
    moves = [(r.x_far, r.x), (r.og_far, r.og), (r.wdown_far, own_down), (r.wout_far, own_out)]
    moves += [(r.wup_far.at[:, c * D : c * D + D], to) for c, to in enumerate(own_up)]
    own_qkv = [r.acc.at[c * shard : c * shard + shard, :] for c in range(3)]
    moves += [(r.wqkv_far.at[c], to) for c, to in enumerate(own_qkv)]
    fetch = [
        pltpu.make_async_copy(here, there, r.local_sem.at[at])
        for at, (here, there) in enumerate(moves)
    ]
    for copy in fetch[-3:] + fetch[:-3]:
        copy.start()
    me = Place(n_dp, n_seq)
    me.greet()
    copies = Copies(r.send, r.recv)
    gather_base = 3 * n_dp + 2 * n_seq
    gather = Gather(
        me,
        [
            (own_qkv, r.fqkv, (1, 3), shard),
            (own_qkv, r.fqkv, (0, 1), shard),
            (own_out, r.fout, None, shard),
            (own_up, r.fup, None, shard),
            (own_down, r.fdown, "blocks", down),
        ],
        copies,
        gather_base,
        gather_base,
        r.fup,
    )
    KV, Q, OUT, UP, DOWN = range(5)
    reduce = Reduce(
        me,
        (r.fup, r.fdown, r.gmix),
        (r.sup, r.sdown, r.smix),
        buffers,
        copies,
        gather_base + 5 * gather.stride,
    )
    exchange = Exchange(
        me, False, r.edge_own, r.coarse, r.edge_near, r.far_all, r.edge_send, r.edge_recv
    )
    exchange_back = Exchange(
        me, True, r.edge_own, r.gfar, r.edge_back, r.far_back, r.back_send, r.back_recv
    )
    tile = min(local, 512)
    tiles = tokens // tile
    row_tiles = local // tile

    def tile_of(i):
        return pl.ds(pl.multiple_of(i * tile, tile), tile)


    r.slots[me.d] = jnp.zeros((8, 128), F32)
    r.slots[me.d, 0:4, 0:shard] = r.norm_own[...].astype(BF).astype(F32)
    for k, o in enumerate(me.dp_others):
        copies.push(r.slots.at[me.d], r.slots.at[me.d], 1 + k, me.d, (o, me.s))
    for copy in fetch[-3:]:
        copy.wait()
    gather.start(KV)
    mean_of = averaging(local)
    for o in me.dp_others:
        copies.arrived(r.slots.at[o], o, (o, me.s))
    total = jnp.zeros((8, D), F32)
    for at in range(n_dp):
        i = lax.broadcasted_iota(jnp.int32, (128, D), 0)
        j = lax.broadcasted_iota(jnp.int32, (128, D), 1)
        pick = jnp.where((j == i + at * shard) & (i < shard), 1.0, 0.0).astype(BF)
        total += mm(r.slots[at].astype(BF), pick, NN)
    r.norm[...] = total
    fetch[0].wait()
    fetch[1].wait()

    def normalize(i, carry):
        part = tile_of(i)
        hat, _ = norm_parts(r.x[part, :].astype(F32))
        r.normed[part, :] = (hat * r.norm[0:1, :] + r.norm[1:2, :]).astype(BF)
        r.og_t[:, part] = r.og[part, :].T
        return carry

    lax.fori_loop(0, tiles, normalize, 0)
    gather.relay_z(KV)
    gather.start(Q)
    gather.relay_y(KV)
    gather.relay_z(Q)
    for copy in fetch[4:-3]:
        copy.wait()
    gather.start(UP)
    gather.settle(KV)
    for row in range(rows):

        def project_kv(i, carry):
            part = tile_of(i)
            normed = r.normed[tile_of(row * row_tiles + i), :]
            r.kv[row, part, 0:D] = mm(normed, r.fqkv[1], NN).astype(BF)
            r.kv[row, part, D : 2 * D] = mm(normed, r.fqkv[2], NN).astype(BF)
            return carry

        lax.fori_loop(0, row_tiles, project_kv, 0)
        r.coarse[row] = mm(mean_of, r.kv[row], NN).astype(BF)
        for lv in edge_levels(local):
            n = local >> lv
            to = slice(16 * lv, 16 * lv + 16)
            if lv == 0:
                r.edge_own[row, 0, to, :] = r.kv[row, 0:16, :]
                r.edge_own[row, 1, to, :] = r.kv[row, n - 16 : n, :]
            else:
                at = level_offset(local, lv)
                r.edge_own[row, 0, to, :] = r.coarse[row, at : at + 16, :]
                r.edge_own[row, 1, to, :] = r.coarse[row, at + n - 16 : at + n, :]
        exchange.start(row)
        if row == 0:
            gather.relay_y(Q)
            fetch[2].wait()
            gather.start(DOWN)
    gather.settle(Q)

    def project_q(i, carry):
        part = tile_of(i)
        r.q[part, :] = mm(r.normed[part, :], r.fqkv[0], NN).astype(BF)
        return carry

    lax.fori_loop(0, tiles, project_q, 0)
    gather.relay_z(UP)


    offset = me.s * local
    blocks = local // QB
    half = blocks // 2

    score_at = [
        (slice(p // 2 * NKEY, p // 2 * NKEY + NKEY), slice(p % 2 * 2 * QB, p % 2 * 2 * QB + 2 * QB))
        for p in range(PAIRS)
    ]
    lanes_of = [slice(128 * p, 128 * p + 128) for p in range(PAIRS)]
    vlanes_of = [slice(D + 128 * p, D + 128 * p + 128) for p in range(PAIRS)]

    def queries(part, pair):
        return lane_halves(r.q[part, lanes_of[pair]] * BF(DH**-0.5))

    def part_of(row, block):
        return pl.ds(pl.multiple_of(row * local + block * QB, QB), QB)

    for row in range(rows):
        exchange.arrive(row)
        build_ext(row, local, r.kv, r.coarse, r.edge_near, r.far_all, ext)
        starts = document_bounds(r.seg[row : row + 1, :], seq_len)

        def attend(block, carry):
            gather_keys(ext, block, offset, local, r.keys)
            fill_bias(starts, offset + block * QB, seq_len, r.bias)
            part = part_of(row, block)
            both = jnp.concatenate([r.bias[...], r.bias[...]], axis=1)
            for pair in range(PAIRS):
                r.acc[score_at[pair]] = mm(r.keys[:, lanes_of[pair]], queries(part, pair), NT) + both
            sums = []
            for pair in range(PAIRS):
                scores = r.acc[score_at[pair]]
                peak = jnp.max(scores, axis=0, keepdims=True)
                weights = jnp.exp(scores - peak)
                sums.append(jnp.sum(weights, axis=0, keepdims=True))
                r.totals[row, block, pair : pair + 1, :] = peak + jnp.log(sums[pair])
                r.hid[score_at[pair]] = weights.astype(BF)
            for pair in range(PAIRS):
                mixed_t = mm(r.keys[:, vlanes_of[pair]], r.hid[score_at[pair]], TN) / sums[pair]
                r.mixed[part, lanes_of[pair]] = own_halves(mixed_t).T.astype(BF)
            return carry

        lax.fori_loop(0, half, attend, 0)
        if row == 0:
            gather.relay_y(UP)
            gather.relay_z(DOWN)
            fetch[3].wait()
            gather.start(OUT)
        if row == rows - 1:
            gather.relay_y(DOWN)
            gather.relay_y(OUT)
            gather.relay_x(UP)
        lax.fori_loop(half, blocks, attend, 0)
        if row == 0:
            gather.relay_z(OUT)
    gather.settle(OUT)
    for row in range(rows):
        exchange.finish(row)


    def feed_first(i, carry):
        part = tile_of(i)
        resid = r.x[part, :].astype(F32) + mm(r.mixed[part, :], r.fout[...], NN)
        r.ginput[part, :] = resid
        r.acc[part, :] = resid
        hat, _ = norm_parts(resid)
        second = (hat * r.norm[2:3, :] + r.norm[3:4, :]).astype(BF)
        r.x[part, :] = second
        r.second_t[:, part] = second.T
        r.gsec[part, :] = jnp.zeros((tile, D), F32)
        return carry

    lax.fori_loop(0, tiles, feed_first, 0)
    gather.relay_x(DOWN)
    gather.settle(UP)
    gather.settle(DOWN)
    gather.finish()
    copies.finish()

    def feed_chunk(f, carry):
        cols = pl.ds(pl.multiple_of(f * CHUNK, CHUNK), CHUNK)

        everything = slice(0, tokens)
        pre = mm(r.x[...], r.fup[:, cols], NN)
        square = pre * pre
        tangent = jnp.tanh(pre * (0.7978845608 + (0.7978845608 * 0.044715) * square))
        upper = 0.5 + 0.5 * tangent
        hidden = pre * upper
        slope = upper + (hidden * (1.0 - tangent)) * (
            0.7978845608 + (0.7978845608 * 3.0 * 0.044715) * square
        )
        hidden = hidden.astype(BF)
        grad_pre = (mm(r.og[...], r.fdown[f], NT) * slope).astype(BF)
        r.hid[everything, :] = hidden
        r.gpre[everything, :] = grad_pre
        r.acc[everything, :] += mm(hidden, r.fdown[f], NN)
        r.gsec[everything, :] += mm(grad_pre, r.fup[:, cols], NT)
        r.fdown[f] = mm(r.og_t[...], r.hid[everything, :], NN).astype(BF)
        r.fup[:, cols] = mm(r.second_t[...], r.gpre[everything, :], NN).astype(BF)
        return carry

    chunks = FF // CHUNK
    lax.fori_loop(0, chunks // 2, feed_chunk, 0)
    for p in reduce.of("first"):
        reduce.start(p)
    lax.fori_loop(chunks // 2, chunks - 1, feed_chunk, 0)
    for p in reduce.of("first"):
        reduce.combine(p)
    lax.fori_loop(chunks - 1, chunks, feed_chunk, 0)
    for p in reduce.of("up", "down"):
        reduce.start(p)
    again = pltpu.make_async_copy(r.x_far, r.x, r.local_sem.at[FETCHES - 1])
    again.start()
    r.grow[...] = jnp.zeros_like(r.grow)

    def feed_last(i, carry):
        part = tile_of(i)
        r.gpre[part, :] = r.acc[part, :].astype(BF)
        hat, inverse = norm_parts(r.ginput[part, :])
        grad = r.gsec[part, :]
        gres = r.og[part, :].astype(F32) + norm_back(grad, hat, inverse, r.norm[2:3, :])
        r.ginput[part, :] = gres
        r.og[part, :] = gres.astype(BF)
        r.grow[2:3, :] += jnp.sum(grad * hat, axis=0, keepdims=True)
        r.grow[3:4, :] += jnp.sum(grad, axis=0, keepdims=True)
        return carry

    lax.fori_loop(0, tiles, feed_last, 0)
    store_out = pltpu.make_async_copy(
        r.gpre.at[0:tokens, :], r.out_far, r.local_sem.at[FETCHES]
    )
    store_out.start()
    for p in reduce.of("first"):
        reduce.second(p)
    for p in reduce.of("up", "down"):
        reduce.combine(p)
    r.gmix[:, 3 * D : 4 * D] = mm(r.mixed[...], r.og[...], TN).astype(BF)
    for p in reduce.of("out"):
        reduce.start(p)

    def mixed_back(i, carry):
        part = tile_of(i)
        r.mixed[part, :] = mm(r.og[part, :], r.fout[...], NT).astype(BF)
        r.og_t[:, part] = r.normed[part, :].T
        return carry

    lax.fori_loop(0, tiles, mixed_back, 0)


    store_out.wait()

    square = jnp.zeros((1, 1), F32)
    for row in range(rows):
        build_ext(row, local, r.kv, r.coarse, r.edge_near, r.far_all, ext)
        starts = document_bounds(r.seg[row : row + 1, :], seq_len)
        for item in gext:
            item[...] = jnp.zeros_like(item)

        def attend_back(block, carry):
            gather_keys(ext, block, offset, local, r.keys)
            fill_bias(starts, offset + block * QB, seq_len, r.bias)
            part = part_of(row, block)
            both = jnp.concatenate([r.bias[...], r.bias[...]], axis=1)
            def grads(pair):
                return lane_halves(r.mixed[part, lanes_of[pair]])

            for pair in range(PAIRS):
                at = score_at[pair]
                r.acc[at] = mm(r.keys[:, lanes_of[pair]], queries(part, pair), NT) + both
                r.gsec[at] = mm(r.keys[:, vlanes_of[pair]], grads(pair), NT)
            for pair in range(PAIRS):
                at = score_at[pair]
                soft = jnp.exp(r.acc[at] - r.totals[row, block, pair : pair + 1, :])
                gsoft = r.gsec[at]
                row_total = jnp.sum(soft * gsoft, axis=0, keepdims=True)
                r.hid[at] = soft.astype(BF)
                r.gpre[at] = (soft * (gsoft - row_total)).astype(BF)
            for pair in range(PAIRS):
                at = score_at[pair]
                gkeys = mm(r.gpre[at], queries(part, pair), NN)
                gvalues = mm(r.hid[at], grads(pair), NN)
                for lv in range(LEVELS):
                    n, at_key = key_rows(lv), key_start(lv)
                    to = pl.ds(pl.multiple_of(window_start(lv, block, offset, local), 16), n)
                    gext[lv][to, lanes_of[pair]] += gkeys[at_key : at_key + n, :]
                    gext[lv][to, vlanes_of[pair]] += gvalues[at_key : at_key + n, :]
                gq_t = own_halves(mm(r.keys[:, lanes_of[pair]], r.gpre[at], TN)) * DH**-0.5
                r.og[part, lanes_of[pair]] = gq_t.T.astype(BF)
            return carry

        lax.fori_loop(0, half, attend_back, 0)
        if row == 0:
            for p in reduce.of("out"):
                reduce.combine(p)
            for p in reduce.of("first"):
                reduce.third(p)
            for p in reduce.of("up"):
                reduce.second(p)
        if row == rows - 1:
            for p in reduce.of("down", "out"):
                reduce.second(p)
            for p in reduce.of("up"):
                reduce.third(p)
        lax.fori_loop(half, blocks, attend_back, 0)
        if row == 0:
            for p in reduce.of("first"):
                square += reduce.final(p)
                reduce.publish(p)
        r.kv[row] = gext[0][16 : 16 + local, :].astype(BF)
        for lv in edge_levels(local):
            n = local >> lv
            to = slice(16 * lv, 16 * lv + 16)
            if lv > 0:
                at = level_offset(local, lv)
                r.coarse[row, at : at + n, :] = gext[lv][16 : 16 + n, :].astype(BF)
            r.edge_own[row, 0, to, :] = gext[lv][0:16, :].astype(BF)
            r.edge_own[row, 1, to, :] = gext[lv][16 + n : 32 + n, :].astype(BF)
        for owner in range(n_seq):
            pieces = []
            used = 0
            for lv in far_levels(local):
                n = local >> lv
                pieces.append(gext[lv][16 + owner * n : 16 + owner * n + n, :])
                used += n
            pieces.append(jnp.zeros((16 - used, 2 * D), F32))
            r.gfar[row, owner] = jnp.concatenate(pieces, axis=0).astype(BF)
        exchange_back.start(row)


    for p in reduce.of("out"):
        reduce.third(p)
    r.gmix[:, 0:D] = mm(r.og_t[...], r.og[...], NN).astype(BF)
    for p in reduce.of("q"):
        reduce.start(p)
    for p in reduce.of("down"):
        reduce.third(p)
    for p in reduce.of("up"):
        square += reduce.final(p)
        reduce.publish(p)

    def settle_inputs(i):
        part = tile_of(i)
        gnormed = (
            mm(r.og[part, :], r.fqkv[0], NT)
            + mm(r.hid[part, :], r.fqkv[1], NT)
            + mm(r.gpre[part, :], r.fqkv[2], NT)
        )
        hat, inverse = norm_parts(r.x[part, :].astype(F32))
        r.ginput[part, :] += norm_back(gnormed, hat, inverse, r.norm[0:1, :])
        r.grow[0:1, :] += jnp.sum(gnormed * hat, axis=0, keepdims=True)
        r.grow[1:2, :] += jnp.sum(gnormed, axis=0, keepdims=True)
        store = pltpu.make_async_copy(
            r.ginput.at[part, :], r.ginput_far.at[part, :], r.local_sem.at[FETCHES + 1 + i]
        )
        store.start()
        return store

    stores = []
    again.wait()
    spread_of = averaging(local)
    for row in range(rows):
        exchange_back.arrive(row)
        base = row * local
        for lv in edge_levels(local):
            n = local >> lv
            for way in range(2):
                more = r.edge_back[row, way, 16 * lv : 16 * lv + 16, :].astype(F32)
                low_row = 0 if way == 0 else n - 16
                if lv == 0:
                    sums = r.kv[row, low_row : low_row + 16, :].astype(F32) + more
                    r.kv[row, low_row : low_row + 16, :] = sums.astype(BF)
                else:
                    at = level_offset(local, lv) + low_row
                    sums = r.coarse[row, at : at + 16, :].astype(F32) + more
                    r.coarse[row, at : at + 16, :] = sums.astype(BF)
        total = r.far_back[row, 0].astype(F32)
        for owner in range(1, n_seq):
            total += r.far_back[row, owner].astype(F32)
        r.coarse[row, local - 16 : local, :] = total.astype(BF)
        for at in range(0, local, tile):
            span, where = slice(at, at + tile), slice(base + at, base + at + tile)
            spread = mm(spread_of[:, span], r.coarse[row], TN)
            pair = (r.kv[row, span, :].astype(F32) + spread).astype(BF)
            r.hid[where, :] = pair[:, 0:D]
            r.gpre[where, :] = pair[:, D : 2 * D]
        if row < rows - 1:
            stores += [settle_inputs(row * row_tiles + i) for i in range(row_tiles)]
    for p in reduce.of("q"):
        reduce.combine(p)
    late = reduce.of("kv")
    r.gmix[:, D : 2 * D] = mm(r.og_t[...], r.hid[0:tokens, :], NN).astype(BF)
    if len(late) > 1:
        reduce.start(late[0])
    r.gmix[:, 2 * D : 3 * D] = mm(r.og_t[...], r.gpre[0:tokens, :], NN).astype(BF)
    reduce.start(late[-1])

    stores += [settle_inputs((rows - 1) * row_tiles + i) for i in range(row_tiles)]
    rows_total = SmallSum(me, copies, r.grow, r.small_seq, r.small_dp, n_dp)
    square_total = SmallSum(me, copies, r.square, r.square_seq, r.square_dp, 2 * n_dp + n_seq)
    rows_total.start()
    for p in late:
        reduce.combine(p)
    for p in reduce.of("q"):
        reduce.second(p)
    for p in reduce.of("out"):
        square += reduce.final(p)
        reduce.publish(p)
    rows_total.turn()
    for p in late:
        reduce.second(p)
    for p in reduce.of("q"):
        reduce.third(p)
    for p in reduce.of("down"):
        square += reduce.final(p)
        reduce.publish(p)
    for p in late:
        reduce.third(p)
    for p in reduce.of("q"):
        square += reduce.final(p)
        reduce.publish(p)
    r.small[...] = rows_total.finish()
    for p in late:
        square += reduce.final(p)
    r.square[...] = jnp.broadcast_to(square, (8, 128))
    square_total.start()
    for p in late:
        reduce.publish(p)
    square_total.turn()
    for p in range(len(reduce.parts)):
        reduce.settle(p)
    total = square_total.finish()
    r.small[4:5, 0:128] = total[0:1, :]
    for row in range(rows):
        exchange_back.finish(row)
    for store in stores:
        store.wait()
    copies.finish()


DMA = pltpu.SemaphoreType.DMA


class Shapes:
    def __init__(self, inputs, segment_ids):
        self.n_dp, self.n_seq = lax.axis_size("dp"), lax.axis_size("seq")
        self.rows, self.local = inputs.shape[0], inputs.shape[1]
        self.seq_len = segment_ids.shape[1]
        self.tokens = self.rows * self.local
        self.blocks = self.local // QB
        edge = 16 * len(edge_levels(self.local))
        self.edge = (self.rows, 2, edge, 2 * D)
        self.far = (self.rows, self.n_seq, 16, 2 * D)
        ext = [(ext_rows(self.local, self.seq_len, lv), 2 * D) for lv in range(LEVELS)]
        self.ext_low = [pltpu.VMEM(shape, BF) for shape in ext]
        self.ext_wide = [pltpu.VMEM(shape, F32) for shape in ext]
        self.edge_sems = Exchange.sems(self.rows, self.n_seq)
        self.heads = (self.rows, self.local, D)
        parts = len(grad_parts(self.n_dp, self.n_seq))
        self.sems = 3 * self.n_dp + 2 * self.n_seq
        self.sems += 5 * Gather.sems(self.n_dp, self.n_seq)
        self.sems += parts * Reduce.sems(self.n_dp, self.n_seq)
        self.pairs = (self.rows, self.local, 2 * D)


def run_layer(z, inputs, segment_ids, out_grad, w_qkv, w_out, w_up, w_down, norm_params):
    flat = (z.tokens, D)
    named = layer_scratch(z)
    return pl.pallas_call(
        functools.partial(layer_kernel, z, list(named)),
        out_shape=[
            sds(flat, BF),
            sds(flat, F32),
            sds((D // z.n_dp, FF), BF),
            sds((D // z.n_dp, 4 * D), BF),
            sds((D, FF // z.n_dp), BF),
            sds((8, D), F32),
        ],
        in_specs=[ANY if name.endswith("_far") else VM for name in INPUTS],
        out_specs=[ANY if name.endswith("_far") else VM for name in OUTPUTS],
        scratch_shapes=[
            *named.values(),
            *z.ext_low,
            *z.ext_wide,
            *Reduce.scratch(z.n_dp, z.n_seq),
        ],
        compiler_params=params(0),
        name="layer",
    )(
        inputs.reshape(flat),
        segment_ids,
        out_grad.reshape(flat),
        w_qkv,
        w_out,
        w_up,
        w_down,
        norm_params,
    )


def run_adam(z, sums, masters, firsts, seconds, passed):
    shapes = [sds(w.shape, F32) for w in masters]
    norm_shape = sds(firsts[4].shape, F32)
    steps = 2 if FF // z.n_dp % 256 == 0 else 1

    def rows_of(shape):
        if len(shape) == 3:
            return pl.BlockSpec((shape[0], shape[1] // steps, shape[2]), lambda i: (0, i, 0))
        return pl.BlockSpec((shape[0] // steps, shape[1]), lambda i: (i, 0))

    def whole(shape):
        return pl.BlockSpec(shape, lambda i: (0, 0))

    big = [rows_of(w.shape) for w in masters]
    norm_spec = whole(firsts[4].shape)
    down_spec = pl.BlockSpec((D, FF // z.n_dp // steps), lambda i: (0, i))
    through = [rows_of(item.shape) for item in passed]
    sums_spec = [rows_of(sums[0].shape), rows_of(sums[1].shape), down_spec, whole((8, D))]
    return pl.pallas_call(
        functools.partial(adam_kernel, z.n_dp),
        grid=(steps,),
        out_shape=shapes
        + [norm_shape]
        + shapes
        + [norm_shape]
        + shapes
        + [norm_shape, sds((1, 1), F32)]
        + [sds(item.shape, item.dtype) for item in passed],
        in_specs=sums_spec + big + big + [norm_spec] + big + [norm_spec] + through,
        out_specs=(big + [norm_spec]) * 3 + [whole((1, 1))] + through,
        compiler_params=params(),
        name="adam",
    )(*sums, *masters, *firsts, *seconds, *passed)


def on_device(
    inputs,
    segment_ids,
    out_grad,
    w_qkv,
    w_out,
    w_up,
    w_down,
    norm_params,
    qkv_first,
    qkv_second,
    out_first,
    out_second,
    up_first,
    up_second,
    down_first,
    down_second,
    norm_first,
    norm_second,
):
    z = Shapes(inputs, segment_ids)
    masters = [w_qkv, w_out, w_up, w_down]
    firsts = [qkv_first, out_first, up_first, down_first, norm_first]
    seconds = [qkv_second, out_second, up_second, down_second, norm_second]
    outputs, input_grad, *sums = run_layer(
        z, inputs, segment_ids, out_grad, *masters, norm_params
    )
    updated = run_adam(z, sums, masters, firsts, seconds, (outputs, input_grad))
    return (
        updated[16].reshape(z.heads),
        updated[17].reshape(z.heads),
        updated[15].reshape(()),
        *updated[0:15],
    )


def solution(mesh):
    tokens = P("dp", "seq", None)
    rows, stack, lanes = P("dp", None), P(None, "dp", None), P(None, "dp")
    moments = (stack, stack, rows, rows, rows, rows, rows, rows, lanes, lanes)
    weights = (stack, rows, rows, rows)
    return jax.shard_map(
        on_device,
        mesh=mesh,
        in_specs=(tokens, rows, tokens, *weights, lanes, *moments),
        out_specs=(tokens, tokens, P(), *weights, lanes, *weights, lanes, *weights, lanes),
        check_vma=False,
    )
```

```python
import functools
import math

import jax
import jax.numpy as jnp
from jax import lax
from jax.experimental import pallas as pl
from jax.experimental.pallas import tpu as pltpu
from jax.sharding import PartitionSpec as P

D = 512
HEADS = 8
DH = 64
FF = 2048
LEVELS = 7
DOCS = 4
QB = 128
NKEY = 512
CHUNK = 512
LIMIT = 63
PAIRS = HEADS // 2

masked_score = -1e30
beta_one = 0.9
beta_two = 0.999
bias_first = 1.0 - 0.9**10
bias_second = 1.0 - 0.999**10
learn_rate = 0.1
weight_decay = 0.1
epsilon = 1e-08
clip_norm = 1.0

BF = jnp.bfloat16
F32 = jnp.float32
MESH = pl.DeviceIdType.MESH
VM = pl.BlockSpec(memory_space=pltpu.VMEM)
ANY = pl.BlockSpec(memory_space=pl.ANY)

NN = ((1,), (0,))
NT = ((1,), (1,))
TN = ((0,), (0,))


def mm(left, right, dims):
    return lax.dot_general(left, right, (dims, ((), ())), preferred_element_type=F32)


def params(cid=None):
    if cid is None:
        return pltpu.CompilerParams(vmem_limit_bytes=LIMIT * 2**20)
    return pltpu.CompilerParams(
        vmem_limit_bytes=LIMIT * 2**20, collective_id=cid, has_side_effects=True
    )


def sds(shape, dtype):
    return jax.ShapeDtypeStruct(shape, dtype)


def level_offset(local, level):
    return local - (local >> (level - 1))


def edge_levels(local):
    return [lv for lv in range(LEVELS) if (local >> lv) >= 16]


def far_levels(local):
    return [lv for lv in range(LEVELS) if (local >> lv) < 16]


def ext_rows(local, seq_len, level):
    return ((local >> level) if (local >> level) >= 16 else (seq_len >> level)) + 32


def key_rows(level):
    return max(QB >> level, 16) + 32


def key_start(level):
    return sum(key_rows(lv) for lv in range(level))


def window_start(level, block, offset, local):
    span = 16 << level
    if (local >> level) >= 16:
        if span <= QB:
            return block * (QB >> level)
        return (block * QB) // span * 16
    return (offset + block * QB) // span * 16


def averaging(local):
    row = lax.broadcasted_iota(jnp.int32, (local, local), 0)
    col = lax.broadcasted_iota(jnp.int32, (local, local), 1)
    total = jnp.zeros((local, local), F32)
    for lv in range(1, LEVELS):
        at = lax.shift_right_logical(col, lv) + level_offset(local, lv)
        total = jnp.where(at == row, 2.0**-lv, total)
    return total.astype(BF)


def norm_parts(values):
    center = jnp.mean(values, axis=-1, keepdims=True)
    centered = values - center
    spread = jnp.mean(centered * centered, axis=-1, keepdims=True)
    inverse = lax.rsqrt(spread + 1e-05)
    return centered * inverse, inverse


def norm_back(grad_in, normed, inverse, gain):
    scaled = grad_in * gain
    return inverse * (
        scaled
        - jnp.mean(scaled, axis=-1, keepdims=True)
        - normed * jnp.mean(scaled * normed, axis=-1, keepdims=True)
    )


def document_bounds(seg_row, seq_len):
    return [
        jnp.sum(jnp.where(seg_row < doc, 1.0, 0.0), axis=1, keepdims=True)
        for doc in range(1, DOCS)
    ]


def fill_bias(starts, first_query, seq_len, bias_ref):
    qpos = first_query + lax.broadcasted_iota(jnp.int32, (1, QB), 1)
    qf = qpos.astype(F32)
    low = jnp.zeros((1, QB), F32)
    high = jnp.full((1, QB), float(seq_len), F32)
    for start in starts:
        low = jnp.where(qf >= start, jnp.maximum(low, start), low)
        high = jnp.where(qf < start, jnp.minimum(high, start), high)
    for lv in range(LEVELS):
        span = 16 << lv
        rows = key_rows(lv)
        if span <= QB:
            key_first = first_query // (1 << lv) - 16
        else:
            key_first = first_query // span * 16 - 16
        index = key_first + lax.broadcasted_iota(jnp.int32, (rows, QB), 0)
        begin = (index * (1 << lv)).astype(F32)
        end = begin + float((1 << lv) - 1)
        block = lax.div(qpos, span)
        lo = jnp.maximum(low, ((block - 1) * span).astype(F32))
        hi = jnp.minimum(high, ((block + 2) * span).astype(F32))
        allowed = (begin >= lo) & (end < hi)
        if lv > 0:
            half = span // 2
            parent = lax.div(qpos, half)
            inner_lo = ((parent - 1) * half).astype(F32)
            inner_hi = ((parent + 2) * half).astype(F32)
            allowed = allowed & ((begin < inner_lo) | (begin >= inner_hi))
        bias_ref[key_start(lv) : key_start(lv) + rows, :] = jnp.where(
            allowed, lv * math.log(2.0), masked_score
        )


def build_ext(row, local, kv_ref, coarse_ref, edge_ref, far_ref, ext):
    count = far_ref.shape[1]
    for lv in range(LEVELS):
        rows = local >> lv
        if rows >= 16:
            ext[lv][0:16, :] = edge_ref[row, 0, 16 * lv : 16 * lv + 16, :]
            if lv == 0:
                ext[lv][16 : 16 + rows, :] = kv_ref[row]
            else:
                at = level_offset(local, lv)
                ext[lv][16 : 16 + rows, :] = coarse_ref[row, at : at + rows, :]
            ext[lv][16 + rows : 32 + rows, :] = edge_ref[row, 1, 16 * lv : 16 * lv + 16, :]
        else:
            at = level_offset(local, lv) - (local - 16)
            blank = jnp.zeros((16, 2 * D), F32)
            pieces = [blank]
            for owner in range(count):
                pieces.append(far_ref[row, owner].astype(F32)[at : at + rows, :])
            pieces.append(blank)
            ext[lv][...] = jnp.concatenate(pieces, axis=0).astype(BF)


def gather_keys(ext, block, offset, local, keys_ref):
    for lv in range(LEVELS):
        start = pl.multiple_of(window_start(lv, block, offset, local), 16)
        at = key_start(lv)
        keys_ref[at : at + key_rows(lv), :] = ext[lv][pl.ds(start, key_rows(lv)), :]


def lane_halves(values):
    lane = lax.broadcasted_iota(jnp.int32, values.shape, 1)
    zero = jnp.zeros_like(values)
    return jnp.concatenate(
        [jnp.where(lane < DH, values, zero), jnp.where(lane >= DH, values, zero)], axis=0
    )


def own_halves(pair_t):
    n = pair_t.shape[1] // 2
    sub = lax.broadcasted_iota(jnp.int32, (2 * DH, n), 0)
    return jnp.where(sub < DH, pair_t[:, :n], pair_t[:, n:])


def adam_kernel(n_dp, *refs):
    gup, gmix, gdown, small = refs[0:4]
    weights, firsts, seconds = refs[4:8], refs[8:13], refs[13:18]
    passed, outs, passed_out = refs[18:20], refs[20:36], refs[36:38]
    for here, there in zip(passed, passed_out):
        there[...] = here[...]

    new_w, norm_grad, new_m, new_s, grad_norm = (
        outs[0:4],
        outs[4],
        outs[5:10],
        outs[10:15],
        outs[15],
    )
    own = small[0:4, :]
    square = jnp.sum(jnp.sum(own * own, axis=0, keepdims=True), axis=1, keepdims=True)
    root = jnp.sqrt(square + small[4:5, 0:1])
    grad_norm[...] = root
    factor = jnp.minimum(1.0, clip_norm / root)

    def moments(clipped, first, second):
        return (
            beta_one * first + (1.0 - beta_one) * clipped,
            beta_two * second + (1.0 - beta_two) * clipped * clipped,
        )

    def update(weight, grad, first, second):
        mean, sq = moments(grad * factor, first, second)
        change = mean / bias_first / (jnp.sqrt(sq / bias_second) + epsilon) + weight_decay * weight
        return weight - learn_rate * change, mean, sq

    for c in range(3):
        w, m, s = update(
            weights[0][c], gmix[:, c * D : c * D + D].astype(F32), firsts[0][c], seconds[0][c]
        )
        new_w[0][c], new_m[0][c], new_s[0][c] = w, m, s
    for at, grad in ((1, gmix[:, 3 * D : 4 * D]), (2, gup[...]), (3, gdown[...])):
        grad = grad.astype(F32)
        if at == 3:
            grad = grad.T
        w, m, s = update(weights[at][...], grad, firsts[at][...], seconds[at][...])
        new_w[at][...], new_m[at][...], new_s[at][...] = w, m, s
    width = D // n_dp
    lane = lax.axis_index("dp") * width
    rolled = pltpu.roll(small[...], D - lane, 1)[0:4, 0:width]
    clipped = rolled * factor
    norm_grad[...] = clipped
    m, s = moments(clipped, firsts[4][...], seconds[4][...])
    new_m[4][...], new_s[4][...] = m, s


class Copies:
    def __init__(self, send, recv):
        self.send, self.recv = send, recv
        self.started = []

    def push(self, src, dst, send_at, recv_at, device, alone=True):
        copy = pltpu.make_async_remote_copy(
            src_ref=src,
            dst_ref=dst,
            send_sem=self.send.at[send_at],
            recv_sem=self.recv.at[recv_at],
            device_id=device,
            device_id_type=MESH,
        )
        copy.start()
        if alone:
            self.started.append(copy)

    def arrived(self, dst, recv_at, device):
        pltpu.make_async_remote_copy(
            src_ref=dst,
            dst_ref=dst,
            send_sem=self.send.at[0],
            recv_sem=self.recv.at[recv_at],
            device_id=device,
            device_id_type=MESH,
        ).wait_recv()

    def left(self, src, send_at, device):
        pltpu.make_async_remote_copy(
            src_ref=src,
            dst_ref=src,
            send_sem=self.send.at[send_at],
            recv_sem=self.recv.at[0],
            device_id=device,
            device_id_type=MESH,
        ).wait_send()

    def finish(self):
        for copy in self.started:
            copy.wait_send()
        self.started = []


def greet(peers):
    barrier = pltpu.get_barrier_semaphore()
    for peer in peers:
        pl.semaphore_signal(barrier, inc=1, device_id=peer, device_id_type=MESH)
    pl.semaphore_wait(barrier, len(peers))


class Place:
    def __init__(self, n_dp, n_seq):
        self.n_dp, self.n_seq = n_dp, n_seq
        self.d, self.s = lax.axis_index("dp"), lax.axis_index("seq")
        self.z, self.y = lax.div(self.d, 2), lax.rem(self.d, 2)
        self.hi, self.core = lax.div(self.s, 2), lax.rem(self.s, 2)
        self.depth, self.high = n_dp // 2, n_seq // 2
        self.mate = self.s + 1 - 2 * self.core
        self.flip = self.d + 1 - 2 * self.y
        self.seq_others = [lax.rem(self.s + k, n_seq) for k in range(1, n_seq)]
        self.dp_others = [lax.rem(self.d + k, n_dp) for k in range(1, n_dp)]

    def greet(self):
        greet(
            [(self.d, o) for o in self.seq_others] + [(o, self.s) for o in self.dp_others]
        )


class Gather:
    def __init__(self, place, parts, copies, base, send_base, measure):
        self.at, self.parts, self.copies, self.base = place, parts, copies, base
        self.send_base, self.measure = send_base, measure
        self.stride = self.sems(place.n_dp, place.n_seq)

    @staticmethod
    def sems(n_dp, n_seq):
        return 2 * (n_dp // 2) + 2

    def split(self, p):
        high = self.at.high
        return self.parts[p][4] and high > 1 and self.parts[p][3] % (32 * high) == 0

    def piece(self, p, shard, core, hi):
        _, whole, lead, rows, _ = self.parts[p]
        n = rows // 2
        start = shard * rows + core * n
        if self.split(p):
            n = n // self.at.high
            start = start + hi * n
        if lead is None:
            return whole.at[pl.ds(pl.multiple_of(start, n), n), :]
        if lead == "blocks":
            row = pl.multiple_of(lax.rem(start, CHUNK), n)
            return whole.at[lax.div(start, CHUNK), pl.ds(row, n), :]
        return whole.at[lead[0] : lead[1], pl.ds(pl.multiple_of(start, n), n), :]

    def sem(self, p, stage, index=0):
        at = self.base + p * self.stride
        sizes = (self.at.depth, self.at.depth, 1)
        return at + sum(sizes[:stage]) + index

    def push(self, p, here, recv_at, device):
        self.copies.push(here, here, self.send_base + p, recv_at, device, alone=False)

    def share(self, p, rows):
        _, whole, lead, _, _ = self.parts[p]
        if lead is None:
            return whole.at[0:rows, :]
        if lead == "blocks":
            return self.measure.at[0 : rows * D // FF, :]
        return whole.at[lead[0] : lead[1], 0:rows, :]

    def load(self, p):
        own, whole, lead, rows, _ = self.parts[p]
        start = pl.multiple_of(self.at.d * rows, rows)
        if isinstance(lead, tuple):
            for c in range(*lead):
                whole[c, pl.ds(start, rows), :] = own[c][...].astype(BF)
        elif isinstance(own, list):
            for c, item in enumerate(own):
                whole.at[pl.ds(start, rows), c * D : c * D + D][...] = item[...].astype(BF)
        elif lead is None:
            whole[pl.ds(start, rows), :] = own[...].astype(BF)
        elif lead == "blocks":
            row = pl.multiple_of(lax.rem(start, CHUNK), rows)
            whole[lax.div(start, CHUNK), pl.ds(row, rows), :] = own[...].astype(BF)

    def start(self, p):
        me = self.at
        self.load(p)
        mine = self.piece(p, me.d, me.core, me.hi)
        for k in range(1, me.depth):
            other = lax.rem(me.z + k, me.depth) * 2 + me.y
            self.push(p, mine, self.sem(p, 0, me.z), (other, me.s))
        self.push(p, mine, self.sem(p, 1, me.z), (me.flip, me.s))

    def onward(self, p, shard):
        me = self.at
        here = self.piece(p, shard, me.core, me.hi)
        if self.split(p):
            for kh in range(1, me.high):
                other = lax.rem(me.hi + kh, me.high) * 2 + me.core
                self.push(p, here, self.sem(p, 2), (me.d, other))
        self.push(p, here, self.sem(p, 3), (me.d, me.mate))

    def relay_z(self, p):
        me = self.at
        for k in range(1, me.depth):
            zz = lax.rem(me.z + k, me.depth)
            shard = zz * 2 + me.y
            here = self.piece(p, shard, me.core, me.hi)
            self.copies.arrived(here, self.sem(p, 0, zz), (shard, me.s))
            self.push(p, here, self.sem(p, 1, zz), (me.flip, me.s))
            self.onward(p, shard)

    def relay_y(self, p):
        me = self.at
        for k in range(me.depth):
            zz = lax.rem(me.z + k, me.depth)
            shard = zz * 2 + 1 - me.y
            here = self.piece(p, shard, me.core, me.hi)
            self.copies.arrived(here, self.sem(p, 1, zz), (me.flip, me.s))
            self.onward(p, shard)

    def relay_x(self, p):
        me = self.at
        if not self.split(p):
            return
        rows = self.parts[p][3] // (2 * me.high) * (me.n_dp - 1) * (me.high - 1)
        mirror = lax.rem(me.hi + 1, me.high) * 2 + me.core
        self.copies.arrived(self.share(p, rows), self.sem(p, 2), (me.d, mirror))
        for kh in range(1, me.high):
            h = lax.rem(me.hi + kh, me.high)
            for k in range(1, me.n_dp):
                shard = lax.rem(me.d + k, me.n_dp)
                here = self.piece(p, shard, me.core, h)
                self.push(p, here, self.sem(p, 3), (me.d, me.mate))

    def settle(self, p):
        me = self.at
        rows = self.parts[p][3] // 2 * (me.n_dp - 1)
        self.copies.arrived(self.share(p, rows), self.sem(p, 3), (me.d, me.mate))

    def finish(self):
        me = self.at
        for p, part in enumerate(self.parts):
            ref = self.share(p, part[3] * (me.n_dp - 1))
            self.copies.left(ref, self.send_base + p, (me.d, me.mate))


class Exchange:
    def __init__(self, place, personal, edge_in, far_in, edge_out, far_out, send, recv):
        self.at, self.personal = place, personal
        self.edge_in, self.far_in, self.edge_out, self.far_out = edge_in, far_in, edge_out, far_out
        self.send, self.recv = send, recv

    @staticmethod
    def sems(rows, n_seq):
        return rows * (2 + n_seq)

    def edge(self, row, way, device):
        base = row * (2 + self.at.n_seq)
        return pltpu.make_async_remote_copy(
            src_ref=self.edge_in.at[row, way],
            dst_ref=self.edge_out.at[row, 1 - way],
            send_sem=self.send.at[base + way],
            recv_sem=self.recv.at[base + 1 - way],
            device_id=(self.at.d, device),
            device_id_type=MESH,
        )

    def far_rows(self, row, other):
        if self.personal:
            return self.far_in.at[row, other]
        local = self.far_in.shape[1]
        return self.far_in.at[row, local - 16 : local, :]

    def far(self, row, k, other):
        base = row * (2 + self.at.n_seq) + 2
        return pltpu.make_async_remote_copy(
            src_ref=self.far_rows(row, other),
            dst_ref=self.far_out.at[row, self.at.s],
            send_sem=self.send.at[base + k],
            recv_sem=self.recv.at[base + self.at.s],
            device_id=(self.at.d, other),
            device_id_type=MESH,
        )

    def start(self, row):
        s, n_seq = self.at.s, self.at.n_seq

        @pl.when(s > 0)
        def _():
            self.edge(row, 0, s - 1).start()

        @pl.when(s < n_seq - 1)
        def _():
            self.edge(row, 1, s + 1).start()

        for k, other in enumerate(self.at.seq_others):
            self.far(row, k, other).start()
        self.far_out[row, s] = self.far_rows(row, s)[...]

    def arrive(self, row):
        s, n_seq = self.at.s, self.at.n_seq
        blank = jnp.zeros(self.edge_out.shape[2:], BF)

        @pl.when(s > 0)
        def _():
            self.edge(row, 1, s - 1).wait_recv()

        @pl.when(s == 0)
        def _():
            self.edge_out[row, 0] = blank

        @pl.when(s < n_seq - 1)
        def _():
            self.edge(row, 0, s + 1).wait_recv()

        @pl.when(s == n_seq - 1)
        def _():
            self.edge_out[row, 1] = blank

        base = row * (2 + n_seq) + 2
        for other in self.at.seq_others:
            here = self.far_out.at[row, other]
            pltpu.make_async_remote_copy(
                src_ref=here,
                dst_ref=here,
                send_sem=self.send.at[base],
                recv_sem=self.recv.at[base + other],
                device_id=(self.at.d, other),
                device_id_type=MESH,
            ).wait_recv()

    def finish(self, row):
        s, n_seq = self.at.s, self.at.n_seq

        @pl.when(s > 0)
        def _():
            self.edge(row, 0, s - 1).wait_send()

        @pl.when(s < n_seq - 1)
        def _():
            self.edge(row, 1, s + 1).wait_send()

        for k, other in enumerate(self.at.seq_others):
            self.far(row, k, other).wait_send()


class SmallSum:
    def __init__(self, place, copies, own, seq_in, dp_in, base):
        self.at, self.copies, self.own = place, copies, own
        self.seq_in, self.dp_in, self.base = seq_in, dp_in, base

    def start(self):
        me = self.at
        self.seq_in[me.s] = self.own[...]
        for k, o in enumerate(me.seq_others):
            self.copies.push(
                self.own, self.seq_in.at[me.s], self.base + 1 + k, self.base + me.s, (me.d, o)
            )

    def turn(self):
        me = self.at
        for o in me.seq_others:
            self.copies.arrived(self.seq_in.at[o], self.base + o, (me.d, o))
        total = self.seq_in[0]
        for o in range(1, me.n_seq):
            total += self.seq_in[o]
        self.dp_in[me.d] = total
        base = self.base + me.n_seq
        for k, o in enumerate(me.dp_others):
            here = self.dp_in.at[me.d]
            self.copies.push(here, here, base + 1 + k, base + me.d, (o, me.s))

    def finish(self):
        me = self.at
        for o in me.dp_others:
            self.copies.arrived(self.dp_in.at[o], self.base + me.n_seq + o, (o, me.s))
        total = self.dp_in[0]
        for o in range(1, me.n_dp):
            total += self.dp_in[o]
        return total


def grad_parts(n_dp, n_seq):
    if D // n_seq % 128:
        return [
            (0, 0, FF, True, True, "up"),
            (1, 0, FF, False, False, "down"),
            (2, 0, 4 * D, True, True, "kv"),
        ]
    return [
        (0, 0, FF // 2, True, True, "first"),
        (0, FF // 2, FF, True, True, "up"),
        (1, 0, FF, False, False, "down"),
        (2, 3 * D, 4 * D, True, True, "out"),
        (2, 0, D, True, False, "q"),
        (2, D, 2 * D, True, True, "kv"),
        (2, 2 * D, 3 * D, True, False, "kv"),
    ]


def block_shape(part, n_dp, n_seq):
    _, lo, hi, by_rows, _, _ = part
    if by_rows:
        return (D // n_dp, (hi - lo) // n_seq)
    return (D // n_seq, (hi - lo) // n_dp)


class Reduce:
    def __init__(self, place, sources, finals, buffers, copies, base):
        self.at, self.sources, self.finals = place, sources, finals
        self.parts = grad_parts(place.n_dp, place.n_seq)
        n = len(self.parts)
        groups = [buffers[i * n : i * n + n] for i in range(5)]
        self.core_in, self.held, self.high_in, self.y_in, self.z_in = groups
        self.copies, self.base = copies, base
        self.stride = self.sems(place.n_dp, place.n_seq)

    @staticmethod
    def sems(n_dp, n_seq):
        return 2 + (n_seq // 2 - 1) + (n_dp // 2 - 1) + 1

    @staticmethod
    def scratch(n_dp, n_seq):
        high, depth = n_seq // 2, n_dp // 2
        groups = [[], [], [], [], []]
        for part in grad_parts(n_dp, n_seq):
            _, lo, up, by_rows, first, _ = part
            a, b = block_shape(part, n_dp, n_seq)
            shapes = [
                (D, (up - lo) // 2) if by_rows else (FF // CHUNK, D // 2, CHUNK),
                (high, depth, 2, a, b),
                (high - 1, depth, 2, a, b) if first else (high - 1, depth, a, b),
                (depth, a, b) if first else (high, depth, a, b),
                (depth - 1, a, b),
            ]
            for group, shape in zip(groups, shapes):
                group.append(pltpu.VMEM(shape, BF))
        return [item for group in groups for item in group]

    def of(self, *stages):
        return [p for p, part in enumerate(self.parts) if part[5] in stages]

    def sem(self, p, stage, index=0):
        sizes = (1, 1, self.at.high - 1, self.at.depth - 1)
        return self.base + p * self.stride + sum(sizes[:stage]) + index

    def start(self, p):
        me = self.at
        src, lo, up, by_rows, _, _ = self.parts[p]
        ref = self.sources[src]
        which = 1 - me.core
        if by_rows:
            w = (up - lo) // 2
            half = ref.at[:, pl.ds(pl.multiple_of(lo + which * w, 128), w)]
        else:
            w = D // 2
            half = ref.at[:, pl.ds(pl.multiple_of(which * w, w), w), :]
        self.copies.push(half, self.core_in[p], self.sem(p, 0), self.sem(p, 0), (me.d, me.mate))

    def push_y(self, p, held):
        me = self.at
        self.copies.push(held, self.y_in[p], self.sem(p, 1), self.sem(p, 1), (me.flip, me.s))

    def take_y(self, p):
        me = self.at
        self.copies.arrived(self.y_in[p], self.sem(p, 1), (me.flip, me.s))


    def push_high(self, p, y):
        me = self.at
        for k in range(1, me.high):
            h = lax.rem(me.hi + k, me.high)
            src = self.held[p].at[h] if y is None else self.held[p].at[h, :, y]
            self.copies.push(
                src,
                self.high_in[p].at[me.high - k - 1],
                self.sem(p, 2, k - 1),
                self.sem(p, 2, me.high - k - 1),
                (me.d, h * 2 + me.core),
            )

    def take_high(self, p):
        me = self.at
        for k in range(1, me.high):
            h = lax.rem(me.hi + k, me.high)
            self.copies.arrived(
                self.high_in[p].at[k - 1], self.sem(p, 2, k - 1), (me.d, h * 2 + me.core)
            )

    def combine(self, p):
        me = self.at
        part = self.parts[p]
        src, lo, up, by_rows, first, _ = part
        a, b = block_shape(part, me.n_dp, me.n_seq)
        self.copies.arrived(self.core_in[p], self.sem(p, 0), (me.d, me.mate))
        theirs, held, source = self.core_in[p], self.held[p], self.sources[src]
        for h in range(me.high):
            for shard in range(me.n_dp):
                which = me.core * me.high + h
                if by_rows:
                    r = slice(shard * a, shard * a + a)
                    left = source[r, pl.ds(pl.multiple_of(lo + which * b, 128), b)]
                    right = theirs[r, h * b : h * b + b]
                else:
                    block, lane = shard * b // CHUNK, shard * b % CHUNK
                    lanes = slice(lane, lane + b)
                    left = source[block, pl.ds(pl.multiple_of(which * a, a), a), lanes]
                    right = theirs[block, h * a : h * a + a, lanes]
                total = left.astype(F32) + right.astype(F32)
                held[h, shard // 2, shard % 2] = total.astype(BF)
        if first:
            self.push_high(p, None)
        else:
            self.push_y(p, held.at[:, :, 1 - me.y])

    def add_high(self, p):
        me = self.at
        held = self.held[p]
        self.take_high(p)
        first = self.parts[p][4]
        for zz in range(me.depth):
            for yy in (0, 1) if first else (me.y,):
                value = held[me.hi, zz, yy].astype(F32)
                for k in range(me.high - 1):
                    more = self.high_in[p][k, zz, yy] if first else self.high_in[p][k, zz]
                    value += more.astype(F32)
                held[me.hi, zz, yy] = value.astype(BF)

    def second(self, p):
        me = self.at
        held = self.held[p]
        if self.parts[p][4]:
            self.add_high(p)
            self.push_y(p, held.at[me.hi, :, 1 - me.y])
        else:
            self.take_y(p)
            for h in range(me.high):
                for zz in range(me.depth):
                    value = held[h, zz, me.y].astype(F32) + self.y_in[p][h, zz].astype(F32)
                    held[h, zz, me.y] = value.astype(BF)
            self.push_high(p, me.y)

    def third(self, p):
        me = self.at
        held = self.held[p]
        if self.parts[p][4]:
            self.take_y(p)
            for zz in range(me.depth):
                value = held[me.hi, zz, me.y].astype(F32) + self.y_in[p][zz].astype(F32)
                held[me.hi, zz, me.y] = value.astype(BF)
        else:
            self.add_high(p)
        for k in range(1, me.depth):
            zz = lax.rem(me.z + k, me.depth)
            self.copies.push(
                held.at[me.hi, zz, me.y],
                self.z_in[p].at[me.depth - k - 1],
                self.sem(p, 3, k - 1),
                self.sem(p, 3, me.depth - k - 1),
                (zz * 2 + me.y, me.s),
            )

    def place_of(self, p, owner):
        part = self.parts[p]
        src, lo, up, by_rows, _, _ = part
        a, b = block_shape(part, self.at.n_dp, self.at.n_seq)
        which = lax.rem(owner, 2) * self.at.high + lax.div(owner, 2)
        if by_rows:
            return self.finals[src].at[:, pl.ds(pl.multiple_of(lo + which * b, 128), b)]
        return self.finals[src].at[pl.ds(pl.multiple_of(which * a, a), a), :]

    def final(self, p):
        me = self.at
        value = self.held[p][me.hi, me.z, me.y].astype(F32)
        for k in range(1, me.depth):
            zz = lax.rem(me.z + k, me.depth)
            self.copies.arrived(self.z_in[p].at[k - 1], self.sem(p, 3, k - 1), (zz * 2 + me.y, me.s))
            value += self.z_in[p][k - 1].astype(F32)
        low = value.astype(BF)
        here = self.place_of(p, me.s)
        here[...] = low
        value = low.astype(F32)
        return jnp.sum(jnp.sum(value * value, axis=0, keepdims=True), axis=1, keepdims=True)

    def publish(self, p):
        me = self.at
        here = self.place_of(p, me.s)
        for o in me.seq_others:
            self.copies.push(here, here, self.sem(p, 4), self.sem(p, 4), (me.d, o), alone=False)

    def share(self, p):
        part = self.parts[p]
        a, b = block_shape(part, self.at.n_dp, self.at.n_seq)
        n = self.at.n_seq - 1
        if part[3]:
            return self.finals[part[0]].at[:, 0 : n * b]
        return self.finals[part[0]].at[0 : n * a, :]

    def settle(self, p):
        me = self.at
        self.copies.arrived(self.share(p), self.sem(p, 4), (me.d, me.mate))
        self.copies.left(self.share(p), self.sem(p, 4), (me.d, me.mate))


class Named:
    def __init__(self, names, refs):
        for name, ref in zip(names, refs):
            setattr(self, name, ref)


INPUTS = ["x_far", "seg", "og_far", "wqkv_far", "wout_far", "wup_far", "wdown_far", "norm_own"]
OUTPUTS = ["out_far", "ginput_far", "sup_far", "smix_far", "sdown_far", "small"]
FETCHES = 8 + FF // D
PARTS = 7


def layer_scratch(z):
    tokens = (z.tokens, D)
    tall = (max(z.tokens, 2 * NKEY), D)
    return {
        "slots": pltpu.VMEM((z.n_dp, 8, 128), F32),
        "norm": pltpu.VMEM((8, D), F32),
        "fqkv": pltpu.VMEM((3, D, D), BF),
        "fout": pltpu.VMEM((D, D), BF),
        "fup": pltpu.VMEM((D, FF), BF),
        "fdown": pltpu.VMEM((FF // CHUNK, CHUNK, D), BF),
        "normed": pltpu.VMEM(tokens, BF),
        "q": pltpu.VMEM(tokens, BF),
        "kv": pltpu.VMEM(z.pairs, BF),
        "coarse": pltpu.VMEM(z.pairs, BF),
        "edge_own": pltpu.VMEM(z.edge, BF),
        "edge_near": pltpu.VMEM(z.edge, BF),
        "edge_back": pltpu.VMEM(z.edge, BF),
        "far_all": pltpu.VMEM(z.far, BF),
        "gfar": pltpu.VMEM(z.far, BF),
        "far_back": pltpu.VMEM(z.far, BF),
        "keys": pltpu.VMEM((NKEY, 2 * D), BF),
        "bias": pltpu.VMEM((NKEY, QB), F32),
        "mixed": pltpu.VMEM(tokens, BF),
        "totals": pltpu.VMEM((z.rows, z.blocks, PAIRS, 2 * QB), F32),
        "second_t": pltpu.VMEM((D, z.tokens), BF),
        "og_t": pltpu.VMEM((D, z.tokens), BF),
        "acc": pltpu.VMEM(tall, F32),
        "gsec": pltpu.VMEM(tall, F32),
        "hid": pltpu.VMEM(tall, BF),
        "gpre": pltpu.VMEM(tall, BF),
        "gmix": pltpu.VMEM((D, 4 * D), BF),
        "grow": pltpu.VMEM((8, D), F32),
        "small_seq": pltpu.VMEM((z.n_seq, 8, D), F32),
        "small_dp": pltpu.VMEM((z.n_dp, 8, D), F32),
        "square": pltpu.VMEM((8, 128), F32),
        "square_seq": pltpu.VMEM((z.n_seq, 8, 128), F32),
        "square_dp": pltpu.VMEM((z.n_dp, 8, 128), F32),
        "send": DMA((z.sems + PARTS,)),
        "recv": DMA((z.sems + PARTS * Gather.sems(z.n_dp, z.n_seq),)),
        "edge_send": DMA((z.edge_sems,)),
        "edge_recv": DMA((z.edge_sems,)),
        "back_send": DMA((z.edge_sems,)),
        "back_recv": DMA((z.edge_sems,)),
        "local_sem": DMA((FETCHES + 4 + z.tokens // min(z.local, 512),)),
        "sup": pltpu.VMEM((D // z.n_dp, FF), BF),
        "smix": pltpu.VMEM((D // z.n_dp, 4 * D), BF),
        "sdown": pltpu.VMEM((D, FF // z.n_dp), BF),
        "x": pltpu.VMEM(tokens, BF),
        "og": pltpu.VMEM(tokens, BF),
        "ginput": pltpu.VMEM(tokens, F32),
    }


def layer_kernel(z, names, *refs):
    count = len(INPUTS) + len(OUTPUTS) + len(names)
    r = Named(INPUTS + OUTPUTS + names, refs[:count])
    ext = refs[count : count + LEVELS]
    gext = refs[count + LEVELS : count + 2 * LEVELS]
    buffers = refs[count + 2 * LEVELS :]
    rows, local, tokens, seq_len = z.rows, z.local, z.tokens, z.seq_len
    n_dp, n_seq = z.n_dp, z.n_seq
    shard = D // n_dp
    down = FF // n_dp
    own_down = r.gsec.at[0:down, :]
    own_out = r.gsec.at[down : down + shard, :]
    own_up = [
        r.gsec.at[down + shard * (c + 1) : down + shard * (c + 2), :] for c in range(FF // D)
    ]
    moves = [(r.x_far, r.x), (r.og_far, r.og), (r.wdown_far, own_down), (r.wout_far, own_out)]
    moves += [(r.wup_far.at[:, c * D : c * D + D], to) for c, to in enumerate(own_up)]
    own_qkv = [r.acc.at[c * shard : c * shard + shard, :] for c in range(3)]
    moves += [(r.wqkv_far.at[c], to) for c, to in enumerate(own_qkv)]
    fetch = [
        pltpu.make_async_copy(here, there, r.local_sem.at[at])
        for at, (here, there) in enumerate(moves)
    ]
    for copy in fetch[-3:] + fetch[:-3]:
        copy.start()
    me = Place(n_dp, n_seq)
    me.greet()
    copies = Copies(r.send, r.recv)
    reduce_base = 3 * n_dp + 2 * n_seq
    gather_base = reduce_base + z.parts * Reduce.sems(n_dp, n_seq)
    gather = Gather(
        me,
        [
            (own_qkv, r.fqkv, (1, 2), shard, True),
            (own_qkv, r.fqkv, (2, 3), shard, True),
            (own_qkv, r.fqkv, (0, 1), shard, True),
            (own_up[: FF // D // 2], r.fup.at[:, 0 : FF // 2], None, shard, True),
            (own_up[FF // D // 2 :], r.fup.at[:, FF // 2 : FF], None, shard, False),
            (own_down, r.fdown, "blocks", down, True),
            (own_out, r.fout, None, shard, False),
        ],
        copies,
        gather_base,
        gather_base,
        r.fup,
    )
    K, V, Q, UPA, UPB, DOWN, OUT = range(PARTS)
    reduce = Reduce(
        me,
        (r.fup, r.fdown, r.gmix),
        (r.sup, r.sdown, r.smix),
        buffers,
        copies,
        reduce_base,
    )
    exchange = Exchange(
        me, False, r.edge_own, r.coarse, r.edge_near, r.far_all, r.edge_send, r.edge_recv
    )
    exchange_back = Exchange(
        me, True, r.edge_own, r.gfar, r.edge_back, r.far_back, r.back_send, r.back_recv
    )
    tile = min(local, 512)
    tiles = tokens // tile
    row_tiles = local // tile

    def tile_of(i):
        return pl.ds(pl.multiple_of(i * tile, tile), tile)


    r.slots[me.d] = jnp.zeros((8, 128), F32)
    r.slots[me.d, 0:4, 0:shard] = r.norm_own[...].astype(BF).astype(F32)
    for k, o in enumerate(me.dp_others):
        copies.push(r.slots.at[me.d], r.slots.at[me.d], 1 + k, me.d, (o, me.s))
    for copy in fetch[-3:]:
        copy.wait()
    gather.start(K)
    gather.start(V)
    gather.start(Q)
    mean_of = averaging(local)
    for o in me.dp_others:
        copies.arrived(r.slots.at[o], o, (o, me.s))
    total = jnp.zeros((8, D), F32)
    for at in range(n_dp):
        i = lax.broadcasted_iota(jnp.int32, (128, D), 0)
        j = lax.broadcasted_iota(jnp.int32, (128, D), 1)
        pick = jnp.where((j == i + at * shard) & (i < shard), 1.0, 0.0).astype(BF)
        total += mm(r.slots[at].astype(BF), pick, NN)
    r.norm[...] = total
    fetch[0].wait()
    fetch[1].wait()

    def normalize(i, carry):
        part = tile_of(i)
        hat, _ = norm_parts(r.x[part, :].astype(F32))
        r.normed[part, :] = (hat * r.norm[0:1, :] + r.norm[1:2, :]).astype(BF)
        r.og_t[:, part] = r.og[part, :].T
        return carry

    lax.fori_loop(0, tiles, normalize, 0)
    gather.relay_z(K)
    gather.relay_z(V)
    gather.relay_y(K)
    gather.relay_z(Q)
    for copy in fetch[4:-3]:
        copy.wait()
    gather.start(UPA)
    gather.relay_y(V)
    gather.relay_x(K)
    gather.start(UPB)
    gather.relay_y(Q)
    gather.relay_x(V)
    gather.settle(K)
    gather.settle(V)
    fetch[2].wait()
    gather.start(DOWN)
    for row in range(rows):

        def project_kv(i, carry):
            part = tile_of(i)
            normed = r.normed[tile_of(row * row_tiles + i), :]
            r.kv[row, part, 0:D] = mm(normed, r.fqkv[1], NN).astype(BF)
            r.kv[row, part, D : 2 * D] = mm(normed, r.fqkv[2], NN).astype(BF)
            return carry

        lax.fori_loop(0, row_tiles, project_kv, 0)
        r.coarse[row] = mm(mean_of, r.kv[row], NN).astype(BF)
        for lv in edge_levels(local):
            n = local >> lv
            to = slice(16 * lv, 16 * lv + 16)
            if lv == 0:
                r.edge_own[row, 0, to, :] = r.kv[row, 0:16, :]
                r.edge_own[row, 1, to, :] = r.kv[row, n - 16 : n, :]
            else:
                at = level_offset(local, lv)
                r.edge_own[row, 0, to, :] = r.coarse[row, at : at + 16, :]
                r.edge_own[row, 1, to, :] = r.coarse[row, at + n - 16 : at + n, :]
        exchange.start(row)
        if row == 0:
            gather.relay_x(Q)
            gather.relay_z(UPA)
            fetch[3].wait()
            gather.start(OUT)
    gather.settle(Q)

    def project_q(i, carry):
        part = tile_of(i)
        r.q[part, :] = mm(r.normed[part, :], r.fqkv[0], NN).astype(BF)
        return carry

    lax.fori_loop(0, tiles, project_q, 0)
    gather.relay_y(UPA)
    gather.relay_z(UPB)


    offset = me.s * local
    blocks = local // QB
    half = blocks // 2

    score_at = [
        (slice(p // 2 * NKEY, p // 2 * NKEY + NKEY), slice(p % 2 * 2 * QB, p % 2 * 2 * QB + 2 * QB))
        for p in range(PAIRS)
    ]
    lanes_of = [slice(128 * p, 128 * p + 128) for p in range(PAIRS)]
    vlanes_of = [slice(D + 128 * p, D + 128 * p + 128) for p in range(PAIRS)]

    def queries(part, pair):
        return lane_halves(r.q[part, lanes_of[pair]] * BF(DH**-0.5))

    def part_of(row, block):
        return pl.ds(pl.multiple_of(row * local + block * QB, QB), QB)

    for row in range(rows):
        exchange.arrive(row)
        build_ext(row, local, r.kv, r.coarse, r.edge_near, r.far_all, ext)
        starts = document_bounds(r.seg[row : row + 1, :], seq_len)

        def attend(block, carry):
            gather_keys(ext, block, offset, local, r.keys)
            fill_bias(starts, offset + block * QB, seq_len, r.bias)
            part = part_of(row, block)
            both = jnp.concatenate([r.bias[...], r.bias[...]], axis=1)
            for pair in range(PAIRS):
                r.acc[score_at[pair]] = mm(r.keys[:, lanes_of[pair]], queries(part, pair), NT) + both
            sums = []
            for pair in range(PAIRS):
                scores = r.acc[score_at[pair]]
                peak = jnp.max(scores, axis=0, keepdims=True)
                weights = jnp.exp(scores - peak)
                sums.append(jnp.sum(weights, axis=0, keepdims=True))
                r.totals[row, block, pair : pair + 1, :] = peak + jnp.log(sums[pair])
                r.hid[score_at[pair]] = weights.astype(BF)
            for pair in range(PAIRS):
                mixed_t = mm(r.keys[:, vlanes_of[pair]], r.hid[score_at[pair]], TN) / sums[pair]
                r.mixed[part, lanes_of[pair]] = own_halves(mixed_t).T.astype(BF)
            return carry

        lax.fori_loop(0, min(1, blocks), attend, 0)
        if row == 0:
            gather.relay_z(DOWN)
        lax.fori_loop(min(1, blocks), half, attend, 0)
        if row == 0:
            gather.relay_y(UPB)
            gather.relay_x(UPA)
            gather.relay_z(OUT)
        if row == rows - 1:
            gather.relay_y(OUT)
        lax.fori_loop(max(half, min(1, blocks)), blocks, attend, 0)
        if row == 0:
            gather.relay_y(DOWN)
    gather.settle(OUT)
    for row in range(rows):
        exchange.finish(row)


    def feed_first(i, carry):
        part = tile_of(i)
        resid = r.x[part, :].astype(F32) + mm(r.mixed[part, :], r.fout[...], NN)
        r.ginput[part, :] = resid
        r.acc[part, :] = resid
        hat, _ = norm_parts(resid)
        second = (hat * r.norm[2:3, :] + r.norm[3:4, :]).astype(BF)
        r.x[part, :] = second
        r.second_t[:, part] = second.T
        r.gsec[part, :] = jnp.zeros((tile, D), F32)
        return carry

    lax.fori_loop(0, tiles, feed_first, 0)
    gather.relay_x(DOWN)
    for p in (UPA, UPB, DOWN):
        gather.settle(p)
    gather.finish()
    copies.finish()

    def feed_chunk(f, carry):
        cols = pl.ds(pl.multiple_of(f * CHUNK, CHUNK), CHUNK)

        everything = slice(0, tokens)
        pre = mm(r.x[...], r.fup[:, cols], NN)
        square = pre * pre
        tangent = jnp.tanh(pre * (0.7978845608 + (0.7978845608 * 0.044715) * square))
        upper = 0.5 + 0.5 * tangent
        hidden = pre * upper
        slope = upper + (hidden * (1.0 - tangent)) * (
            0.7978845608 + (0.7978845608 * 3.0 * 0.044715) * square
        )
        hidden = hidden.astype(BF)
        grad_pre = (mm(r.og[...], r.fdown[f], NT) * slope).astype(BF)
        r.hid[everything, :] = hidden
        r.gpre[everything, :] = grad_pre
        r.acc[everything, :] += mm(hidden, r.fdown[f], NN)
        r.gsec[everything, :] += mm(grad_pre, r.fup[:, cols], NT)
        r.fdown[f] = mm(r.og_t[...], r.hid[everything, :], NN).astype(BF)
        r.fup[:, cols] = mm(r.second_t[...], r.gpre[everything, :], NN).astype(BF)
        return carry

    chunks = FF // CHUNK
    lax.fori_loop(0, chunks // 2, feed_chunk, 0)
    for p in reduce.of("first"):
        reduce.start(p)
    lax.fori_loop(chunks // 2, chunks - 1, feed_chunk, 0)
    for p in reduce.of("first"):
        reduce.combine(p)
    lax.fori_loop(chunks - 1, chunks, feed_chunk, 0)
    for p in reduce.of("up", "down"):
        reduce.start(p)
    again = pltpu.make_async_copy(r.x_far, r.x, r.local_sem.at[FETCHES - 1])
    again.start()
    r.grow[...] = jnp.zeros_like(r.grow)

    def feed_last(i, carry):
        part = tile_of(i)
        r.gpre[part, :] = r.acc[part, :].astype(BF)
        hat, inverse = norm_parts(r.ginput[part, :])
        grad = r.gsec[part, :]
        gres = r.og[part, :].astype(F32) + norm_back(grad, hat, inverse, r.norm[2:3, :])
        r.ginput[part, :] = gres
        r.og[part, :] = gres.astype(BF)
        r.grow[2:3, :] += jnp.sum(grad * hat, axis=0, keepdims=True)
        r.grow[3:4, :] += jnp.sum(grad, axis=0, keepdims=True)
        return carry

    lax.fori_loop(0, tiles, feed_last, 0)
    store_out = pltpu.make_async_copy(
        r.gpre.at[0:tokens, :], r.out_far, r.local_sem.at[FETCHES]
    )
    store_out.start()
    for p in reduce.of("first"):
        reduce.second(p)
    for p in reduce.of("up", "down"):
        reduce.combine(p)
    r.gmix[:, 3 * D : 4 * D] = mm(r.mixed[...], r.og[...], TN).astype(BF)
    for p in reduce.of("out"):
        reduce.start(p)

    def mixed_back(i, carry):
        part = tile_of(i)
        r.mixed[part, :] = mm(r.og[part, :], r.fout[...], NT).astype(BF)
        r.og_t[:, part] = r.normed[part, :].T
        return carry

    lax.fori_loop(0, tiles, mixed_back, 0)


    store_out.wait()

    square = jnp.zeros((1, 1), F32)
    for row in range(rows):
        build_ext(row, local, r.kv, r.coarse, r.edge_near, r.far_all, ext)
        starts = document_bounds(r.seg[row : row + 1, :], seq_len)
        for item in gext:
            item[...] = jnp.zeros_like(item)

        def attend_back(block, carry):
            gather_keys(ext, block, offset, local, r.keys)
            fill_bias(starts, offset + block * QB, seq_len, r.bias)
            part = part_of(row, block)
            both = jnp.concatenate([r.bias[...], r.bias[...]], axis=1)
            def grads(pair):
                return lane_halves(r.mixed[part, lanes_of[pair]])

            for pair in range(PAIRS):
                at = score_at[pair]
                r.acc[at] = mm(r.keys[:, lanes_of[pair]], queries(part, pair), NT) + both
                r.gsec[at] = mm(r.keys[:, vlanes_of[pair]], grads(pair), NT)
            for pair in range(PAIRS):
                at = score_at[pair]
                soft = jnp.exp(r.acc[at] - r.totals[row, block, pair : pair + 1, :])
                gsoft = r.gsec[at]
                row_total = jnp.sum(soft * gsoft, axis=0, keepdims=True)
                r.hid[at] = soft.astype(BF)
                r.gpre[at] = (soft * (gsoft - row_total)).astype(BF)
            for pair in range(PAIRS):
                at = score_at[pair]
                gkeys = mm(r.gpre[at], queries(part, pair), NN)
                gvalues = mm(r.hid[at], grads(pair), NN)
                for lv in range(LEVELS):
                    n, at_key = key_rows(lv), key_start(lv)
                    to = pl.ds(pl.multiple_of(window_start(lv, block, offset, local), 16), n)
                    gext[lv][to, lanes_of[pair]] += gkeys[at_key : at_key + n, :]
                    gext[lv][to, vlanes_of[pair]] += gvalues[at_key : at_key + n, :]
                gq_t = own_halves(mm(r.keys[:, lanes_of[pair]], r.gpre[at], TN)) * DH**-0.5
                r.og[part, lanes_of[pair]] = gq_t.T.astype(BF)
            return carry

        lax.fori_loop(0, half, attend_back, 0)
        if row == 0:
            for p in reduce.of("out"):
                reduce.combine(p)
            for p in reduce.of("first"):
                reduce.third(p)
            for p in reduce.of("up"):
                reduce.second(p)
        if row == rows - 1:
            for p in reduce.of("down", "out"):
                reduce.second(p)
            for p in reduce.of("up"):
                reduce.third(p)
        lax.fori_loop(half, blocks, attend_back, 0)
        if row == 0:
            for p in reduce.of("first"):
                square += reduce.final(p)
                reduce.publish(p)
        r.kv[row] = gext[0][16 : 16 + local, :].astype(BF)
        for lv in edge_levels(local):
            n = local >> lv
            to = slice(16 * lv, 16 * lv + 16)
            if lv > 0:
                at = level_offset(local, lv)
                r.coarse[row, at : at + n, :] = gext[lv][16 : 16 + n, :].astype(BF)
            r.edge_own[row, 0, to, :] = gext[lv][0:16, :].astype(BF)
            r.edge_own[row, 1, to, :] = gext[lv][16 + n : 32 + n, :].astype(BF)
        for owner in range(n_seq):
            pieces = []
            used = 0
            for lv in far_levels(local):
                n = local >> lv
                pieces.append(gext[lv][16 + owner * n : 16 + owner * n + n, :])
                used += n
            pieces.append(jnp.zeros((16 - used, 2 * D), F32))
            r.gfar[row, owner] = jnp.concatenate(pieces, axis=0).astype(BF)
        exchange_back.start(row)


    for p in reduce.of("out"):
        reduce.third(p)
    r.gmix[:, 0:D] = mm(r.og_t[...], r.og[...], NN).astype(BF)
    for p in reduce.of("q"):
        reduce.start(p)
    for p in reduce.of("down"):
        reduce.third(p)
    for p in reduce.of("q"):
        reduce.combine(p)

    def settle_inputs(i):
        part = tile_of(i)
        gnormed = (
            mm(r.og[part, :], r.fqkv[0], NT)
            + mm(r.hid[part, :], r.fqkv[1], NT)
            + mm(r.gpre[part, :], r.fqkv[2], NT)
        )
        hat, inverse = norm_parts(r.x[part, :].astype(F32))
        r.ginput[part, :] += norm_back(gnormed, hat, inverse, r.norm[0:1, :])
        r.grow[0:1, :] += jnp.sum(gnormed * hat, axis=0, keepdims=True)
        r.grow[1:2, :] += jnp.sum(gnormed, axis=0, keepdims=True)
        store = pltpu.make_async_copy(
            r.ginput.at[part, :], r.ginput_far.at[part, :], r.local_sem.at[FETCHES + 4 + i]
        )
        store.start()
        return store

    stores = []
    again.wait()
    spread_of = averaging(local)
    for row in range(rows):
        exchange_back.arrive(row)
        base = row * local
        for lv in edge_levels(local):
            n = local >> lv
            for way in range(2):
                more = r.edge_back[row, way, 16 * lv : 16 * lv + 16, :].astype(F32)
                low_row = 0 if way == 0 else n - 16
                if lv == 0:
                    sums = r.kv[row, low_row : low_row + 16, :].astype(F32) + more
                    r.kv[row, low_row : low_row + 16, :] = sums.astype(BF)
                else:
                    at = level_offset(local, lv) + low_row
                    sums = r.coarse[row, at : at + 16, :].astype(F32) + more
                    r.coarse[row, at : at + 16, :] = sums.astype(BF)
        total = r.far_back[row, 0].astype(F32)
        for owner in range(1, n_seq):
            total += r.far_back[row, owner].astype(F32)
        r.coarse[row, local - 16 : local, :] = total.astype(BF)
        for at in range(0, local, tile):
            span, where = slice(at, at + tile), slice(base + at, base + at + tile)
            spread = mm(spread_of[:, span], r.coarse[row], TN)
            pair = (r.kv[row, span, :].astype(F32) + spread).astype(BF)
            r.hid[where, :] = pair[:, 0:D]
            r.gpre[where, :] = pair[:, D : 2 * D]
        if row < rows - 1:
            stores += [settle_inputs(row * row_tiles + i) for i in range(row_tiles)]
    for p in reduce.of("q"):
        reduce.second(p)
    late = reduce.of("kv")
    r.gmix[:, D : 2 * D] = mm(r.og_t[...], r.hid[0:tokens, :], NN).astype(BF)
    if len(late) > 1:
        reduce.start(late[0])
    r.gmix[:, 2 * D : 3 * D] = mm(r.og_t[...], r.gpre[0:tokens, :], NN).astype(BF)
    reduce.start(late[-1])

    stores += [settle_inputs((rows - 1) * row_tiles + i) for i in range(row_tiles)]
    rows_total = SmallSum(me, copies, r.grow, r.small_seq, r.small_dp, n_dp)
    square_total = SmallSum(me, copies, r.square, r.square_seq, r.square_dp, 2 * n_dp + n_seq)
    for p in late:
        reduce.combine(p)
    rows_total.start()
    for p in reduce.of("q"):
        reduce.third(p)
    for p in late:
        reduce.second(p)
    for p in reduce.of("up"):
        square += reduce.final(p)
        reduce.publish(p)
    for p in late:
        reduce.third(p)
    for p in reduce.of("out", "down"):
        square += reduce.final(p)
        reduce.publish(p)
    rows_total.turn()
    for p in reduce.of("q"):
        square += reduce.final(p)
        reduce.publish(p)
    for p in late:
        square += reduce.final(p)
    r.square[...] = jnp.broadcast_to(square, (8, 128))
    square_total.start()
    for p in late:
        reduce.publish(p)
    square_total.turn()
    r.small[...] = rows_total.finish()
    for p in range(len(reduce.parts)):
        reduce.settle(p)
    for at, name in enumerate(("sup", "smix", "sdown")):
        store = pltpu.make_async_copy(
            getattr(r, name), getattr(r, name + "_far"), r.local_sem.at[FETCHES + 1 + at]
        )
        store.start()
        stores.append(store)
    total = square_total.finish()
    r.small[4:5, 0:128] = total[0:1, :]
    for row in range(rows):
        exchange_back.finish(row)
    for store in stores:
        store.wait()
    copies.finish()


DMA = pltpu.SemaphoreType.DMA


class Shapes:
    def __init__(self, inputs, segment_ids):
        self.n_dp, self.n_seq = lax.axis_size("dp"), lax.axis_size("seq")
        self.rows, self.local = inputs.shape[0], inputs.shape[1]
        self.seq_len = segment_ids.shape[1]
        self.tokens = self.rows * self.local
        self.blocks = self.local // QB
        edge = 16 * len(edge_levels(self.local))
        self.edge = (self.rows, 2, edge, 2 * D)
        self.far = (self.rows, self.n_seq, 16, 2 * D)
        ext = [(ext_rows(self.local, self.seq_len, lv), 2 * D) for lv in range(LEVELS)]
        self.ext_low = [pltpu.VMEM(shape, BF) for shape in ext]
        self.ext_wide = [pltpu.VMEM(shape, F32) for shape in ext]
        self.edge_sems = Exchange.sems(self.rows, self.n_seq)
        self.heads = (self.rows, self.local, D)
        self.parts = len(grad_parts(self.n_dp, self.n_seq))
        self.sems = 3 * self.n_dp + 2 * self.n_seq
        self.sems += self.parts * Reduce.sems(self.n_dp, self.n_seq)
        self.pairs = (self.rows, self.local, 2 * D)


def run_layer(z, inputs, segment_ids, out_grad, w_qkv, w_out, w_up, w_down, norm_params):
    flat = (z.tokens, D)
    named = layer_scratch(z)
    return pl.pallas_call(
        functools.partial(layer_kernel, z, list(named)),
        out_shape=[
            sds(flat, BF),
            sds(flat, F32),
            sds((D // z.n_dp, FF), BF),
            sds((D // z.n_dp, 4 * D), BF),
            sds((D, FF // z.n_dp), BF),
            sds((8, D), F32),
        ],
        in_specs=[ANY if name.endswith("_far") else VM for name in INPUTS],
        out_specs=[ANY if name.endswith("_far") else VM for name in OUTPUTS],
        scratch_shapes=[
            *named.values(),
            *z.ext_low,
            *z.ext_wide,
            *Reduce.scratch(z.n_dp, z.n_seq),
        ],
        compiler_params=params(0),
        name="layer",
    )(
        inputs.reshape(flat),
        segment_ids,
        out_grad.reshape(flat),
        w_qkv,
        w_out,
        w_up,
        w_down,
        norm_params,
    )


def run_adam(z, sums, masters, firsts, seconds, passed):
    shapes = [sds(w.shape, F32) for w in masters]
    norm_shape = sds(firsts[4].shape, F32)
    steps = 2 if D // z.n_dp % 32 == 0 else 1
    coarse = max(1, steps // (FF // z.n_dp // 128))
    down = max(128, FF // z.n_dp // steps)

    def rows_of(shape):
        if len(shape) == 3:
            return pl.BlockSpec((shape[0], shape[1] // steps, shape[2]), lambda i: (0, i, 0))
        return pl.BlockSpec((shape[0] // steps, shape[1]), lambda i: (i, 0))

    def whole(shape):
        return pl.BlockSpec(shape, lambda i: (0, 0))

    big = [rows_of(w.shape) for w in masters]
    big[3] = pl.BlockSpec((down, D), lambda i: (i // coarse, 0))
    norm_spec = whole(firsts[4].shape)
    down_spec = pl.BlockSpec((D, down), lambda i: (0, i // coarse))
    through = [rows_of(item.shape) for item in passed]
    sums_spec = [rows_of(sums[0].shape), rows_of(sums[1].shape), down_spec, whole((8, D))]
    return pl.pallas_call(
        functools.partial(adam_kernel, z.n_dp),
        grid=(steps,),
        out_shape=shapes
        + [norm_shape]
        + shapes
        + [norm_shape]
        + shapes
        + [norm_shape, sds((1, 1), F32)]
        + [sds(item.shape, item.dtype) for item in passed],
        in_specs=sums_spec + big + big + [norm_spec] + big + [norm_spec] + through,
        out_specs=(big + [norm_spec]) * 3 + [whole((1, 1))] + through,
        compiler_params=params(),
        name="adam",
    )(*sums, *masters, *firsts, *seconds, *passed)


def on_device(
    inputs,
    segment_ids,
    out_grad,
    w_qkv,
    w_out,
    w_up,
    w_down,
    norm_params,
    qkv_first,
    qkv_second,
    out_first,
    out_second,
    up_first,
    up_second,
    down_first,
    down_second,
    norm_first,
    norm_second,
):
    z = Shapes(inputs, segment_ids)
    masters = [w_qkv, w_out, w_up, w_down]
    firsts = [qkv_first, out_first, up_first, down_first, norm_first]
    seconds = [qkv_second, out_second, up_second, down_second, norm_second]
    outputs, input_grad, *sums = run_layer(
        z, inputs, segment_ids, out_grad, *masters, norm_params
    )
    updated = run_adam(z, sums, masters, firsts, seconds, (outputs, input_grad))
    return (
        updated[16].reshape(z.heads),
        updated[17].reshape(z.heads),
        updated[15].reshape(()),
        *updated[0:15],
    )


def solution(mesh):
    tokens = P("dp", "seq", None)
    rows, stack, lanes = P("dp", None), P(None, "dp", None), P(None, "dp")
    moments = (stack, stack, rows, rows, rows, rows, rows, rows, lanes, lanes)
    weights = (stack, rows, rows, rows)
    return jax.shard_map(
        on_device,
        mesh=mesh,
        in_specs=(tokens, rows, tokens, *weights, lanes, *moments),
        out_specs=(tokens, tokens, P(), *weights, lanes, *weights, lanes, *weights, lanes),
        check_vma=False,
    )
```

```python
import functools
import math

import jax
import jax.numpy as jnp
from jax import lax
from jax.experimental import pallas as pl
from jax.experimental.pallas import tpu as pltpu
from jax.sharding import PartitionSpec as P

D = 512
HEADS = 8
DH = 64
FF = 2048
LEVELS = 7
DOCS = 4
QB = 128
NKEY = 512
CHUNK = 512
LIMIT = 63
PAIRS = HEADS // 2

masked_score = -1e30
beta_one = 0.9
beta_two = 0.999
bias_first = 1.0 - 0.9**10
bias_second = 1.0 - 0.999**10
learn_rate = 0.1
weight_decay = 0.1
epsilon = 1e-08
clip_norm = 1.0

BF = jnp.bfloat16
F32 = jnp.float32
MESH = pl.DeviceIdType.MESH
VM = pl.BlockSpec(memory_space=pltpu.VMEM)
ANY = pl.BlockSpec(memory_space=pl.ANY)

NN = ((1,), (0,))
NT = ((1,), (1,))
TN = ((0,), (0,))


def mm(left, right, dims):
    return lax.dot_general(left, right, (dims, ((), ())), preferred_element_type=F32)


def params(cid=None):
    if cid is None:
        return pltpu.CompilerParams(vmem_limit_bytes=LIMIT * 2**20)
    return pltpu.CompilerParams(
        vmem_limit_bytes=LIMIT * 2**20, collective_id=cid, has_side_effects=True
    )


def sds(shape, dtype):
    return jax.ShapeDtypeStruct(shape, dtype)


def level_offset(local, level):
    return local - (local >> (level - 1))


def edge_levels(local):
    return [lv for lv in range(LEVELS) if (local >> lv) >= 16]


def far_levels(local):
    return [lv for lv in range(LEVELS) if (local >> lv) < 16]


def ext_rows(local, seq_len, level):
    return ((local >> level) if (local >> level) >= 16 else (seq_len >> level)) + 32


def key_rows(level):
    return max(QB >> level, 16) + 32


def key_start(level):
    return sum(key_rows(lv) for lv in range(level))


def window_start(level, block, offset, local):
    span = 16 << level
    if (local >> level) >= 16:
        if span <= QB:
            return block * (QB >> level)
        return (block * QB) // span * 16
    return (offset + block * QB) // span * 16


def averaging(local):
    row = lax.broadcasted_iota(jnp.int32, (local, local), 0)
    col = lax.broadcasted_iota(jnp.int32, (local, local), 1)
    total = jnp.zeros((local, local), F32)
    for lv in range(1, LEVELS):
        at = lax.shift_right_logical(col, lv) + level_offset(local, lv)
        total = jnp.where(at == row, 2.0**-lv, total)
    return total.astype(BF)


def norm_parts(values):
    center = jnp.mean(values, axis=-1, keepdims=True)
    centered = values - center
    spread = jnp.mean(centered * centered, axis=-1, keepdims=True)
    inverse = lax.rsqrt(spread + 1e-05)
    return centered * inverse, inverse


def norm_back(grad_in, normed, inverse, gain):
    scaled = grad_in * gain
    return inverse * (
        scaled
        - jnp.mean(scaled, axis=-1, keepdims=True)
        - normed * jnp.mean(scaled * normed, axis=-1, keepdims=True)
    )


def document_bounds(seg_row, seq_len):
    return [
        jnp.sum(jnp.where(seg_row < doc, 1.0, 0.0), axis=1, keepdims=True)
        for doc in range(1, DOCS)
    ]


def fill_bias(starts, first_query, seq_len, bias_ref):
    qpos = first_query + lax.broadcasted_iota(jnp.int32, (1, QB), 1)
    qf = qpos.astype(F32)
    low = jnp.zeros((1, QB), F32)
    high = jnp.full((1, QB), float(seq_len), F32)
    for start in starts:
        low = jnp.where(qf >= start, jnp.maximum(low, start), low)
        high = jnp.where(qf < start, jnp.minimum(high, start), high)
    for lv in range(LEVELS):
        span = 16 << lv
        rows = key_rows(lv)
        if span <= QB:
            key_first = first_query // (1 << lv) - 16
        else:
            key_first = first_query // span * 16 - 16
        index = key_first + lax.broadcasted_iota(jnp.int32, (rows, QB), 0)
        begin = (index * (1 << lv)).astype(F32)
        end = begin + float((1 << lv) - 1)
        block = lax.div(qpos, span)
        lo = jnp.maximum(low, ((block - 1) * span).astype(F32))
        hi = jnp.minimum(high, ((block + 2) * span).astype(F32))
        allowed = (begin >= lo) & (end < hi)
        if lv > 0:
            half = span // 2
            parent = lax.div(qpos, half)
            inner_lo = ((parent - 1) * half).astype(F32)
            inner_hi = ((parent + 2) * half).astype(F32)
            allowed = allowed & ((begin < inner_lo) | (begin >= inner_hi))
        bias_ref[key_start(lv) : key_start(lv) + rows, :] = jnp.where(
            allowed, lv * math.log(2.0), masked_score
        )


def build_ext(row, local, kv_ref, coarse_ref, edge_ref, far_ref, ext):
    count = far_ref.shape[1]
    for lv in range(LEVELS):
        rows = local >> lv
        if rows >= 16:
            ext[lv][0:16, :] = edge_ref[row, 0, 16 * lv : 16 * lv + 16, :]
            if lv == 0:
                ext[lv][16 : 16 + rows, :] = kv_ref[row]
            else:
                at = level_offset(local, lv)
                ext[lv][16 : 16 + rows, :] = coarse_ref[row, at : at + rows, :]
            ext[lv][16 + rows : 32 + rows, :] = edge_ref[row, 1, 16 * lv : 16 * lv + 16, :]
        else:
            at = level_offset(local, lv) - (local - 16)
            blank = jnp.zeros((16, 2 * D), F32)
            pieces = [blank]
            for owner in range(count):
                pieces.append(far_ref[row, owner].astype(F32)[at : at + rows, :])
            pieces.append(blank)
            ext[lv][...] = jnp.concatenate(pieces, axis=0).astype(BF)


def gather_keys(ext, block, offset, local, keys_ref):
    for lv in range(LEVELS):
        start = pl.multiple_of(window_start(lv, block, offset, local), 16)
        at = key_start(lv)
        keys_ref[at : at + key_rows(lv), :] = ext[lv][pl.ds(start, key_rows(lv)), :]


def lane_halves(values):
    lane = lax.broadcasted_iota(jnp.int32, values.shape, 1)
    zero = jnp.zeros_like(values)
    return jnp.concatenate(
        [jnp.where(lane < DH, values, zero), jnp.where(lane >= DH, values, zero)], axis=0
    )


def own_halves(pair_t):
    n = pair_t.shape[1] // 2
    sub = lax.broadcasted_iota(jnp.int32, (2 * DH, n), 0)
    return jnp.where(sub < DH, pair_t[:, :n], pair_t[:, n:])


def adam_kernel(n_dp, *refs):
    gup, gmix, gdown, small = refs[0:4]
    weights, firsts, seconds = refs[4:8], refs[8:13], refs[13:18]
    passed, outs, passed_out = refs[18:20], refs[20:36], refs[36:38]
    for here, there in zip(passed, passed_out):
        there[...] = here[...]

    new_w, norm_grad, new_m, new_s, grad_norm = (
        outs[0:4],
        outs[4],
        outs[5:10],
        outs[10:15],
        outs[15],
    )
    own = small[0:4, :]
    square = jnp.sum(jnp.sum(own * own, axis=0, keepdims=True), axis=1, keepdims=True)
    root = jnp.sqrt(square + small[4:5, 0:1])
    grad_norm[...] = root
    factor = jnp.minimum(1.0, clip_norm / root)

    def moments(clipped, first, second):
        return (
            beta_one * first + (1.0 - beta_one) * clipped,
            beta_two * second + (1.0 - beta_two) * clipped * clipped,
        )

    def update(weight, grad, first, second):
        mean, sq = moments(grad * factor, first, second)
        change = mean / bias_first / (jnp.sqrt(sq / bias_second) + epsilon) + weight_decay * weight
        return weight - learn_rate * change, mean, sq

    for c in range(3):
        w, m, s = update(
            weights[0][c], gmix[:, c * D : c * D + D].astype(F32), firsts[0][c], seconds[0][c]
        )
        new_w[0][c], new_m[0][c], new_s[0][c] = w, m, s
    for at, grad in ((1, gmix[:, 3 * D : 4 * D]), (2, gup[...]), (3, gdown[...])):
        grad = grad.astype(F32)
        if at == 3:
            grad = grad.T
        w, m, s = update(weights[at][...], grad, firsts[at][...], seconds[at][...])
        new_w[at][...], new_m[at][...], new_s[at][...] = w, m, s
    width = D // n_dp
    lane = lax.axis_index("dp") * width
    rolled = pltpu.roll(small[...], D - lane, 1)[0:4, 0:width]
    clipped = rolled * factor
    norm_grad[...] = clipped
    m, s = moments(clipped, firsts[4][...], seconds[4][...])
    new_m[4][...], new_s[4][...] = m, s


class Copies:
    def __init__(self, send, recv):
        self.send, self.recv = send, recv
        self.started = []

    def push(self, src, dst, send_at, recv_at, device, alone=True):
        copy = pltpu.make_async_remote_copy(
            src_ref=src,
            dst_ref=dst,
            send_sem=self.send.at[send_at],
            recv_sem=self.recv.at[recv_at],
            device_id=device,
            device_id_type=MESH,
        )
        copy.start()
        if alone:
            self.started.append(copy)

    def arrived(self, dst, recv_at, device):
        pltpu.make_async_remote_copy(
            src_ref=dst,
            dst_ref=dst,
            send_sem=self.send.at[0],
            recv_sem=self.recv.at[recv_at],
            device_id=device,
            device_id_type=MESH,
        ).wait_recv()

    def left(self, src, send_at, device):
        pltpu.make_async_remote_copy(
            src_ref=src,
            dst_ref=src,
            send_sem=self.send.at[send_at],
            recv_sem=self.recv.at[0],
            device_id=device,
            device_id_type=MESH,
        ).wait_send()

    def finish(self):
        for copy in self.started:
            copy.wait_send()
        self.started = []


def greet(peers):
    barrier = pltpu.get_barrier_semaphore()
    for peer in peers:
        pl.semaphore_signal(barrier, inc=1, device_id=peer, device_id_type=MESH)
    pl.semaphore_wait(barrier, len(peers))


class Place:
    def __init__(self, n_dp, n_seq):
        self.n_dp, self.n_seq = n_dp, n_seq
        self.d, self.s = lax.axis_index("dp"), lax.axis_index("seq")
        self.z, self.y = lax.div(self.d, 2), lax.rem(self.d, 2)
        self.hi, self.core = lax.div(self.s, 2), lax.rem(self.s, 2)
        self.depth, self.high = n_dp // 2, n_seq // 2
        self.mate = self.s + 1 - 2 * self.core
        self.flip = self.d + 1 - 2 * self.y
        self.seq_others = [lax.rem(self.s + k, n_seq) for k in range(1, n_seq)]
        self.dp_others = [lax.rem(self.d + k, n_dp) for k in range(1, n_dp)]

    def greet(self):
        greet([(self.d, o) for o in self.seq_others] + [(o, self.s) for o in self.dp_others])


class Gather:
    def __init__(self, place, parts, copies, base, send_base, measure):
        self.at, self.parts, self.copies, self.base = place, parts, copies, base
        self.send_base, self.measure = send_base, measure
        self.stride = self.sems(place.n_dp, place.n_seq)

    @staticmethod
    def sems(n_dp, n_seq):
        return 2 * (n_dp // 2) + 2

    def split(self, p):
        high = self.at.high
        return self.parts[p][4] and high > 1 and self.parts[p][3] % (32 * high) == 0

    def piece(self, p, shard, core, hi):
        _, whole, lead, rows, _ = self.parts[p]
        n = rows // 2
        start = shard * rows + core * n
        if self.split(p):
            n = n // self.at.high
            start = start + hi * n
        if lead is None:
            return whole.at[pl.ds(pl.multiple_of(start, n), n), :]
        if lead == "blocks":
            row = pl.multiple_of(lax.rem(start, CHUNK), n)
            return whole.at[lax.div(start, CHUNK), pl.ds(row, n), :]
        return whole.at[lead[0] : lead[1], pl.ds(pl.multiple_of(start, n), n), :]

    def sem(self, p, stage, index=0):
        at = self.base + p * self.stride
        sizes = (self.at.depth, self.at.depth, 1)
        return at + sum(sizes[:stage]) + index

    def push(self, p, here, recv_at, device):
        self.copies.push(here, here, self.send_base + p, recv_at, device, alone=False)

    def share(self, p, rows):
        _, whole, lead, _, _ = self.parts[p]
        if lead is None:
            return whole.at[0:rows, :]
        if lead == "blocks":
            return self.measure.at[0 : rows * D // FF, :]
        return whole.at[lead[0] : lead[1], 0:rows, :]

    def load(self, p):
        own, whole, lead, rows, _ = self.parts[p]
        start = pl.multiple_of(self.at.d * rows, rows)
        if isinstance(lead, tuple):
            for c in range(*lead):
                whole[c, pl.ds(start, rows), :] = own[c][...].astype(BF)
        elif isinstance(own, list):
            for c, item in enumerate(own):
                whole.at[pl.ds(start, rows), c * D : c * D + D][...] = item[...].astype(BF)
        elif lead is None:
            whole[pl.ds(start, rows), :] = own[...].astype(BF)
        elif lead == "blocks":
            row = pl.multiple_of(lax.rem(start, CHUNK), rows)
            whole[lax.div(start, CHUNK), pl.ds(row, rows), :] = own[...].astype(BF)

    def start(self, p):
        me = self.at
        self.load(p)
        mine = self.piece(p, me.d, me.core, me.hi)
        for k in range(1, me.depth):
            other = lax.rem(me.z + k, me.depth) * 2 + me.y
            self.push(p, mine, self.sem(p, 0, me.z), (other, me.s))
        self.push(p, mine, self.sem(p, 1, me.z), (me.flip, me.s))

    def onward(self, p, shard):
        me = self.at
        here = self.piece(p, shard, me.core, me.hi)
        if self.split(p):
            for kh in range(1, me.high):
                other = lax.rem(me.hi + kh, me.high) * 2 + me.core
                self.push(p, here, self.sem(p, 2), (me.d, other))
        self.push(p, here, self.sem(p, 3), (me.d, me.mate))

    def relay_z(self, p):
        me = self.at
        for k in range(1, me.depth):
            zz = lax.rem(me.z + k, me.depth)
            shard = zz * 2 + me.y
            here = self.piece(p, shard, me.core, me.hi)
            self.copies.arrived(here, self.sem(p, 0, zz), (shard, me.s))
            self.push(p, here, self.sem(p, 1, zz), (me.flip, me.s))
            self.onward(p, shard)

    def relay_y(self, p):
        me = self.at
        for k in range(me.depth):
            zz = lax.rem(me.z + k, me.depth)
            shard = zz * 2 + 1 - me.y
            here = self.piece(p, shard, me.core, me.hi)
            self.copies.arrived(here, self.sem(p, 1, zz), (me.flip, me.s))
            self.onward(p, shard)

    def relay_x(self, p):
        me = self.at
        if not self.split(p):
            return
        rows = self.parts[p][3] // (2 * me.high) * (me.n_dp - 1) * (me.high - 1)
        mirror = lax.rem(me.hi + 1, me.high) * 2 + me.core
        self.copies.arrived(self.share(p, rows), self.sem(p, 2), (me.d, mirror))
        for kh in range(1, me.high):
            h = lax.rem(me.hi + kh, me.high)
            for k in range(1, me.n_dp):
                shard = lax.rem(me.d + k, me.n_dp)
                here = self.piece(p, shard, me.core, h)
                self.push(p, here, self.sem(p, 3), (me.d, me.mate))

    def settle(self, p):
        me = self.at
        rows = self.parts[p][3] // 2 * (me.n_dp - 1)
        self.copies.arrived(self.share(p, rows), self.sem(p, 3), (me.d, me.mate))

    def finish(self):
        me = self.at
        for p, part in enumerate(self.parts):
            ref = self.share(p, part[3] * (me.n_dp - 1))
            self.copies.left(ref, self.send_base + p, (me.d, me.mate))


class Exchange:
    def __init__(self, place, personal, edge_in, far_in, edge_out, far_out, send, recv):
        self.at, self.personal = place, personal
        self.edge_in, self.far_in, self.edge_out, self.far_out = edge_in, far_in, edge_out, far_out
        self.send, self.recv = send, recv

    @staticmethod
    def sems(rows, n_seq):
        return rows * (2 + n_seq)

    def edge(self, row, way, device):
        base = row * (2 + self.at.n_seq)
        return pltpu.make_async_remote_copy(
            src_ref=self.edge_in.at[row, way],
            dst_ref=self.edge_out.at[row, 1 - way],
            send_sem=self.send.at[base + way],
            recv_sem=self.recv.at[base + 1 - way],
            device_id=(self.at.d, device),
            device_id_type=MESH,
        )

    def far_rows(self, row, other):
        if self.personal:
            return self.far_in.at[row, other]
        local = self.far_in.shape[1]
        return self.far_in.at[row, local - 16 : local, :]

    def far(self, row, k, other):
        base = row * (2 + self.at.n_seq) + 2
        return pltpu.make_async_remote_copy(
            src_ref=self.far_rows(row, other),
            dst_ref=self.far_out.at[row, self.at.s],
            send_sem=self.send.at[base + k],
            recv_sem=self.recv.at[base + self.at.s],
            device_id=(self.at.d, other),
            device_id_type=MESH,
        )

    def start(self, row):
        s, n_seq = self.at.s, self.at.n_seq

        @pl.when(s > 0)
        def _():
            self.edge(row, 0, s - 1).start()

        @pl.when(s < n_seq - 1)
        def _():
            self.edge(row, 1, s + 1).start()

        for k, other in enumerate(self.at.seq_others):
            self.far(row, k, other).start()
        self.far_out[row, s] = self.far_rows(row, s)[...]

    def arrive(self, row):
        s, n_seq = self.at.s, self.at.n_seq
        blank = jnp.zeros(self.edge_out.shape[2:], BF)

        @pl.when(s > 0)
        def _():
            self.edge(row, 1, s - 1).wait_recv()

        @pl.when(s == 0)
        def _():
            self.edge_out[row, 0] = blank

        @pl.when(s < n_seq - 1)
        def _():
            self.edge(row, 0, s + 1).wait_recv()

        @pl.when(s == n_seq - 1)
        def _():
            self.edge_out[row, 1] = blank

        base = row * (2 + n_seq) + 2
        for other in self.at.seq_others:
            here = self.far_out.at[row, other]
            pltpu.make_async_remote_copy(
                src_ref=here,
                dst_ref=here,
                send_sem=self.send.at[base],
                recv_sem=self.recv.at[base + other],
                device_id=(self.at.d, other),
                device_id_type=MESH,
            ).wait_recv()

    def finish(self, row):
        s, n_seq = self.at.s, self.at.n_seq

        @pl.when(s > 0)
        def _():
            self.edge(row, 0, s - 1).wait_send()

        @pl.when(s < n_seq - 1)
        def _():
            self.edge(row, 1, s + 1).wait_send()

        for k, other in enumerate(self.at.seq_others):
            self.far(row, k, other).wait_send()


class SmallSum:
    sems = 2

    def __init__(self, place, copies, own, seq_in, dp_in, base):
        self.at, self.copies, self.own = place, copies, own
        self.seq_in, self.dp_in, self.base = seq_in, dp_in, base

    def start(self):
        me = self.at
        self.seq_in[me.s] = self.own[...]
        for o in me.seq_others:
            here = self.seq_in.at[me.s]
            self.copies.push(self.own, here, self.base, self.base, (me.d, o), alone=False)

    def turn(self):
        me = self.at
        rest = self.seq_in.at[0 : me.n_seq - 1]
        self.copies.arrived(rest, self.base, (me.d, me.mate))
        total = self.seq_in[0]
        for o in range(1, me.n_seq):
            total += self.seq_in[o]
        self.dp_in[me.d] = total
        for o in me.dp_others:
            here = self.dp_in.at[me.d]
            self.copies.push(here, here, self.base + 1, self.base + 1, (o, me.s), alone=False)

    def finish(self):
        me = self.at
        rest = self.dp_in.at[0 : me.n_dp - 1]
        self.copies.arrived(rest, self.base + 1, (me.flip, me.s))
        total = self.dp_in[0]
        for o in range(1, me.n_dp):
            total += self.dp_in[o]
        self.copies.left(self.seq_in.at[0 : me.n_seq - 1], self.base, (me.d, me.mate))
        self.copies.left(rest, self.base + 1, (me.flip, me.s))
        return total


def grad_parts(n_dp, n_seq):
    if D // n_seq % 128:
        return [
            (0, 0, FF, True, True, "up"),
            (1, 0, FF, False, False, "down"),
            (2, 0, 4 * D, True, True, "kv"),
        ]
    return [
        (0, 0, FF // 2, True, True, "first"),
        (0, FF // 2, FF, True, True, "up"),
        (1, 0, FF, False, False, "down"),
        (2, 3 * D, 4 * D, True, True, "out"),
        (2, 0, D, True, False, "q"),
        (2, D, 2 * D, True, True, "kv"),
        (2, 2 * D, 3 * D, True, False, "kv"),
    ]


def block_shape(part, n_dp, n_seq):
    _, lo, hi, by_rows, _, _ = part
    if by_rows:
        return (D // n_dp, (hi - lo) // n_seq)
    return (D // n_seq, (hi - lo) // n_dp)


class Reduce:
    def __init__(self, place, sources, finals, buffers, copies, base):
        self.at, self.sources, self.finals = place, sources, finals
        self.parts = grad_parts(place.n_dp, place.n_seq)
        n = len(self.parts)
        groups = [buffers[i * n : i * n + n] for i in range(5)]
        self.core_in, self.held, self.high_in, self.y_in, self.z_in = groups
        self.copies, self.base = copies, base
        self.stride = self.sems(place.n_dp, place.n_seq)

    @staticmethod
    def sems(n_dp, n_seq):
        return 2 + (n_seq // 2 - 1) + (n_dp // 2 - 1) + 1

    @staticmethod
    def scratch(n_dp, n_seq):
        high, depth = n_seq // 2, n_dp // 2
        groups = [[], [], [], [], []]
        for part in grad_parts(n_dp, n_seq):
            _, lo, up, by_rows, first, _ = part
            a, b = block_shape(part, n_dp, n_seq)
            shapes = [
                (D, (up - lo) // 2) if by_rows else (FF // CHUNK, D // 2, CHUNK),
                (high, depth, 2, a, b),
                (high - 1, depth, 2, a, b) if first else (high - 1, depth, a, b),
                (depth, a, b) if first else (high, depth, a, b),
                (depth - 1, a, b),
            ]
            for group, shape in zip(groups, shapes):
                group.append(pltpu.VMEM(shape, BF))
        return [item for group in groups for item in group]

    def of(self, *stages):
        return [p for p, part in enumerate(self.parts) if part[5] in stages]

    def sem(self, p, stage, index=0):
        sizes = (1, 1, self.at.high - 1, self.at.depth - 1)
        return self.base + p * self.stride + sum(sizes[:stage]) + index

    def start(self, p):
        me = self.at
        src, lo, up, by_rows, _, _ = self.parts[p]
        ref = self.sources[src]
        which = 1 - me.core
        if by_rows:
            w = (up - lo) // 2
            half = ref.at[:, pl.ds(pl.multiple_of(lo + which * w, 128), w)]
        else:
            w = D // 2
            half = ref.at[:, pl.ds(pl.multiple_of(which * w, w), w), :]
        self.copies.push(half, self.core_in[p], self.sem(p, 0), self.sem(p, 0), (me.d, me.mate))

    def push_y(self, p, held):
        me = self.at
        self.copies.push(held, self.y_in[p], self.sem(p, 1), self.sem(p, 1), (me.flip, me.s))

    def take_y(self, p):
        me = self.at
        self.copies.arrived(self.y_in[p], self.sem(p, 1), (me.flip, me.s))


    def push_high(self, p, y):
        me = self.at
        for k in range(1, me.high):
            h = lax.rem(me.hi + k, me.high)
            src = self.held[p].at[h] if y is None else self.held[p].at[h, :, y]
            self.copies.push(
                src,
                self.high_in[p].at[me.high - k - 1],
                self.sem(p, 2, k - 1),
                self.sem(p, 2, me.high - k - 1),
                (me.d, h * 2 + me.core),
            )

    def take_high(self, p):
        me = self.at
        for k in range(1, me.high):
            h = lax.rem(me.hi + k, me.high)
            self.copies.arrived(
                self.high_in[p].at[k - 1], self.sem(p, 2, k - 1), (me.d, h * 2 + me.core)
            )

    def combine(self, p):
        me = self.at
        part = self.parts[p]
        src, lo, up, by_rows, first, _ = part
        a, b = block_shape(part, me.n_dp, me.n_seq)
        self.copies.arrived(self.core_in[p], self.sem(p, 0), (me.d, me.mate))
        theirs, held, source = self.core_in[p], self.held[p], self.sources[src]
        for h in range(me.high):
            for shard in range(me.n_dp):
                which = me.core * me.high + h
                if by_rows:
                    r = slice(shard * a, shard * a + a)
                    left = source[r, pl.ds(pl.multiple_of(lo + which * b, 128), b)]
                    right = theirs[r, h * b : h * b + b]
                else:
                    block, lane = shard * b // CHUNK, shard * b % CHUNK
                    lanes = slice(lane, lane + b)
                    left = source[block, pl.ds(pl.multiple_of(which * a, a), a), lanes]
                    right = theirs[block, h * a : h * a + a, lanes]
                total = left.astype(F32) + right.astype(F32)
                held[h, shard // 2, shard % 2] = total.astype(BF)
        if first:
            self.push_high(p, None)
        else:
            self.push_y(p, held.at[:, :, 1 - me.y])

    def add_high(self, p):
        me = self.at
        held = self.held[p]
        self.take_high(p)
        first = self.parts[p][4]
        for zz in range(me.depth):
            for yy in (0, 1) if first else (me.y,):
                value = held[me.hi, zz, yy].astype(F32)
                for k in range(me.high - 1):
                    more = self.high_in[p][k, zz, yy] if first else self.high_in[p][k, zz]
                    value += more.astype(F32)
                held[me.hi, zz, yy] = value.astype(BF)

    def second(self, p):
        me = self.at
        held = self.held[p]
        if self.parts[p][4]:
            self.add_high(p)
            self.push_y(p, held.at[me.hi, :, 1 - me.y])
        else:
            self.take_y(p)
            for h in range(me.high):
                for zz in range(me.depth):
                    value = held[h, zz, me.y].astype(F32) + self.y_in[p][h, zz].astype(F32)
                    held[h, zz, me.y] = value.astype(BF)
            self.push_high(p, me.y)

    def third(self, p):
        me = self.at
        held = self.held[p]
        if self.parts[p][4]:
            self.take_y(p)
            for zz in range(me.depth):
                value = held[me.hi, zz, me.y].astype(F32) + self.y_in[p][zz].astype(F32)
                held[me.hi, zz, me.y] = value.astype(BF)
        else:
            self.add_high(p)
        for k in range(1, me.depth):
            zz = lax.rem(me.z + k, me.depth)
            self.copies.push(
                held.at[me.hi, zz, me.y],
                self.z_in[p].at[me.depth - k - 1],
                self.sem(p, 3, k - 1),
                self.sem(p, 3, me.depth - k - 1),
                (zz * 2 + me.y, me.s),
            )

    def place_of(self, p, owner):
        part = self.parts[p]
        src, lo, up, by_rows, _, _ = part
        a, b = block_shape(part, self.at.n_dp, self.at.n_seq)
        which = lax.rem(owner, 2) * self.at.high + lax.div(owner, 2)
        if by_rows:
            return self.finals[src].at[:, pl.ds(pl.multiple_of(lo + which * b, 128), b)]
        return self.finals[src].at[pl.ds(pl.multiple_of(which * a, a), a), :]

    def final(self, p):
        me = self.at
        value = self.held[p][me.hi, me.z, me.y].astype(F32)
        for k in range(1, me.depth):
            zz = lax.rem(me.z + k, me.depth)
            self.copies.arrived(self.z_in[p].at[k - 1], self.sem(p, 3, k - 1), (zz * 2 + me.y, me.s))
            value += self.z_in[p][k - 1].astype(F32)
        low = value.astype(BF)
        here = self.place_of(p, me.s)
        here[...] = low
        value = low.astype(F32)
        return jnp.sum(jnp.sum(value * value, axis=0, keepdims=True), axis=1, keepdims=True)

    def publish(self, p):
        me = self.at
        here = self.place_of(p, me.s)
        for o in me.seq_others:
            self.copies.push(here, here, self.sem(p, 4), self.sem(p, 4), (me.d, o), alone=False)

    def share(self, p):
        part = self.parts[p]
        a, b = block_shape(part, self.at.n_dp, self.at.n_seq)
        n = self.at.n_seq - 1
        if part[3]:
            return self.finals[part[0]].at[:, 0 : n * b]
        return self.finals[part[0]].at[0 : n * a, :]

    def settle(self, p):
        me = self.at
        self.copies.arrived(self.share(p), self.sem(p, 4), (me.d, me.mate))
        self.copies.left(self.share(p), self.sem(p, 4), (me.d, me.mate))


class Named:
    def __init__(self, names, refs):
        for name, ref in zip(names, refs):
            setattr(self, name, ref)


INPUTS = ["x_far", "seg", "og_far", "wqkv_far", "wout_far", "wup_far", "wdown_far", "norm_own"]
OUTPUTS = ["out_far", "ginput_far", "sup_far", "smix_far", "sdown_far", "small"]
FETCHES = 8 + FF // D
PARTS = 7


def layer_scratch(z):
    tokens = (z.tokens, D)
    tall = (max(z.tokens, 2 * NKEY), D)
    return {
        "slots": pltpu.VMEM((z.n_dp, 8, 128), F32),
        "norm": pltpu.VMEM((8, D), F32),
        "fqkv": pltpu.VMEM((3, D, D), BF),
        "fout": pltpu.VMEM((D, D), BF),
        "fup": pltpu.VMEM((D, FF), BF),
        "fdown": pltpu.VMEM((FF // CHUNK, CHUNK, D), BF),
        "normed": pltpu.VMEM(tokens, BF),
        "q": pltpu.VMEM(tokens, BF),
        "kv": pltpu.VMEM(z.pairs, BF),
        "coarse": pltpu.VMEM(z.pairs, BF),
        "edge_own": pltpu.VMEM(z.edge, BF),
        "edge_near": pltpu.VMEM(z.edge, BF),
        "edge_back": pltpu.VMEM(z.edge, BF),
        "far_all": pltpu.VMEM(z.far, BF),
        "gfar": pltpu.VMEM(z.far, BF),
        "far_back": pltpu.VMEM(z.far, BF),
        "keys": pltpu.VMEM((NKEY, 2 * D), BF),
        "bias": pltpu.VMEM((NKEY, QB), F32),
        "mixed": pltpu.VMEM(tokens, BF),
        "totals": pltpu.VMEM((z.rows, z.blocks, PAIRS, 2 * QB), F32),
        "second_t": pltpu.VMEM((D, z.tokens), BF),
        "og_t": pltpu.VMEM((D, z.tokens), BF),
        "acc": pltpu.VMEM(tall, F32),
        "gsec": pltpu.VMEM(tall, F32),
        "hid": pltpu.VMEM(tall, BF),
        "gpre": pltpu.VMEM(tall, BF),
        "gmix": pltpu.VMEM((D, 4 * D), BF),
        "grow": pltpu.VMEM((8, D), F32),
        "small_seq": pltpu.VMEM((z.n_seq, 8, D), F32),
        "small_dp": pltpu.VMEM((z.n_dp, 8, D), F32),
        "square": pltpu.VMEM((8, 128), F32),
        "square_seq": pltpu.VMEM((z.n_seq, 8, 128), F32),
        "square_dp": pltpu.VMEM((z.n_dp, 8, 128), F32),
        "send": DMA((z.sems + PARTS,)),
        "recv": DMA((z.sems + PARTS * Gather.sems(z.n_dp, z.n_seq),)),
        "edge_send": DMA((z.edge_sems,)),
        "edge_recv": DMA((z.edge_sems,)),
        "back_send": DMA((z.edge_sems,)),
        "back_recv": DMA((z.edge_sems,)),
        "local_sem": DMA((FETCHES + 4 + z.tokens // min(z.local, 512),)),
        "sup": pltpu.VMEM((D // z.n_dp, FF), BF),
        "smix": pltpu.VMEM((D // z.n_dp, 4 * D), BF),
        "sdown": pltpu.VMEM((D, FF // z.n_dp), BF),
        "x": pltpu.VMEM(tokens, BF),
        "og": pltpu.VMEM(tokens, BF),
        "ginput": pltpu.VMEM(tokens, F32),
    }


def layer_kernel(z, names, *refs):
    count = len(INPUTS) + len(OUTPUTS) + len(names)
    r = Named(INPUTS + OUTPUTS + names, refs[:count])
    ext = refs[count : count + LEVELS]
    gext = refs[count + LEVELS : count + 2 * LEVELS]
    buffers = refs[count + 2 * LEVELS :]
    rows, local, tokens, seq_len = z.rows, z.local, z.tokens, z.seq_len
    n_dp, n_seq = z.n_dp, z.n_seq
    shard = D // n_dp
    down = FF // n_dp
    own_down = r.gsec.at[0:down, :]
    own_out = r.gsec.at[down : down + shard, :]
    own_up = [
        r.gsec.at[down + shard * (c + 1) : down + shard * (c + 2), :] for c in range(FF // D)
    ]
    moves = [(r.x_far, r.x), (r.og_far, r.og), (r.wdown_far, own_down), (r.wout_far, own_out)]
    moves += [(r.wup_far.at[:, c * D : c * D + D], to) for c, to in enumerate(own_up)]
    own_qkv = [r.acc.at[c * shard : c * shard + shard, :] for c in range(3)]
    moves += [(r.wqkv_far.at[c], to) for c, to in enumerate(own_qkv)]
    fetch = [
        pltpu.make_async_copy(here, there, r.local_sem.at[at])
        for at, (here, there) in enumerate(moves)
    ]
    for copy in fetch[-3:] + fetch[:-3]:
        copy.start()
    me = Place(n_dp, n_seq)
    me.greet()
    copies = Copies(r.send, r.recv)
    reduce_base = n_dp + 2 * SmallSum.sems
    gather_base = reduce_base + z.parts * Reduce.sems(n_dp, n_seq)
    gather = Gather(
        me,
        [
            (own_qkv, r.fqkv, (1, 2), shard, True),
            (own_qkv, r.fqkv, (2, 3), shard, True),
            (own_qkv, r.fqkv, (0, 1), shard, True),
            (own_up[: FF // D // 2], r.fup.at[:, 0 : FF // 2], None, shard, True),
            (own_up[FF // D // 2 :], r.fup.at[:, FF // 2 : FF], None, shard, False),
            (own_down, r.fdown, "blocks", down, True),
            (own_out, r.fout, None, shard, False),
        ],
        copies,
        gather_base,
        gather_base,
        r.fup,
    )
    K, V, Q, UPA, UPB, DOWN, OUT = range(PARTS)
    reduce = Reduce(
        me,
        (r.fup, r.fdown, r.gmix),
        (r.sup, r.sdown, r.smix),
        buffers,
        copies,
        reduce_base,
    )
    exchange = Exchange(
        me, False, r.edge_own, r.coarse, r.edge_near, r.far_all, r.edge_send, r.edge_recv
    )
    exchange_back = Exchange(
        me, True, r.edge_own, r.gfar, r.edge_back, r.far_back, r.back_send, r.back_recv
    )
    tile = min(local, 512)
    tiles = tokens // tile
    row_tiles = local // tile

    def tile_of(i):
        return pl.ds(pl.multiple_of(i * tile, tile), tile)


    r.slots[me.d] = jnp.zeros((8, 128), F32)
    r.slots[me.d, 0:4, 0:shard] = r.norm_own[...].astype(BF).astype(F32)
    for k, o in enumerate(me.dp_others):
        copies.push(r.slots.at[me.d], r.slots.at[me.d], 1 + k, me.d, (o, me.s))
    for copy in fetch[-3:]:
        copy.wait()
    gather.start(K)
    gather.start(V)
    gather.start(Q)
    mean_of = averaging(local)
    for o in me.dp_others:
        copies.arrived(r.slots.at[o], o, (o, me.s))
    total = jnp.zeros((8, D), F32)
    for at in range(n_dp):
        i = lax.broadcasted_iota(jnp.int32, (128, D), 0)
        j = lax.broadcasted_iota(jnp.int32, (128, D), 1)
        pick = jnp.where((j == i + at * shard) & (i < shard), 1.0, 0.0).astype(BF)
        total += mm(r.slots[at].astype(BF), pick, NN)
    r.norm[...] = total
    fetch[0].wait()
    fetch[1].wait()

    def normalize(i, carry):
        part = tile_of(i)
        hat, _ = norm_parts(r.x[part, :].astype(F32))
        r.normed[part, :] = (hat * r.norm[0:1, :] + r.norm[1:2, :]).astype(BF)
        r.og_t[:, part] = r.og[part, :].T
        return carry

    lax.fori_loop(0, tiles, normalize, 0)
    gather.relay_z(K)
    gather.relay_z(V)
    gather.relay_y(K)
    gather.relay_z(Q)
    for copy in fetch[4:-3]:
        copy.wait()
    gather.start(UPA)
    gather.relay_y(V)
    gather.relay_x(K)
    gather.start(UPB)
    gather.relay_y(Q)
    gather.relay_x(V)
    gather.settle(K)
    gather.settle(V)
    fetch[2].wait()
    gather.start(DOWN)
    for row in range(rows):

        def project_kv(i, carry):
            part = tile_of(i)
            normed = r.normed[tile_of(row * row_tiles + i), :]
            r.kv[row, part, 0:D] = mm(normed, r.fqkv[1], NN).astype(BF)
            r.kv[row, part, D : 2 * D] = mm(normed, r.fqkv[2], NN).astype(BF)
            return carry

        lax.fori_loop(0, row_tiles, project_kv, 0)
        r.coarse[row] = mm(mean_of, r.kv[row], NN).astype(BF)
        for lv in edge_levels(local):
            n = local >> lv
            to = slice(16 * lv, 16 * lv + 16)
            if lv == 0:
                r.edge_own[row, 0, to, :] = r.kv[row, 0:16, :]
                r.edge_own[row, 1, to, :] = r.kv[row, n - 16 : n, :]
            else:
                at = level_offset(local, lv)
                r.edge_own[row, 0, to, :] = r.coarse[row, at : at + 16, :]
                r.edge_own[row, 1, to, :] = r.coarse[row, at + n - 16 : at + n, :]
        exchange.start(row)
        if row == 0:
            gather.relay_x(Q)
            gather.relay_z(UPA)
            fetch[3].wait()
            gather.start(OUT)
    gather.settle(Q)

    def project_q(i, carry):
        part = tile_of(i)
        r.q[part, :] = mm(r.normed[part, :], r.fqkv[0], NN).astype(BF)
        return carry

    lax.fori_loop(0, tiles, project_q, 0)
    gather.relay_y(UPA)
    gather.relay_z(UPB)


    offset = me.s * local
    blocks = local // QB
    half = blocks // 2

    score_at = [
        (slice(p // 2 * NKEY, p // 2 * NKEY + NKEY), slice(p % 2 * 2 * QB, p % 2 * 2 * QB + 2 * QB))
        for p in range(PAIRS)
    ]
    lanes_of = [slice(128 * p, 128 * p + 128) for p in range(PAIRS)]
    vlanes_of = [slice(D + 128 * p, D + 128 * p + 128) for p in range(PAIRS)]

    def queries(part, pair):
        return lane_halves(r.q[part, lanes_of[pair]] * BF(DH**-0.5))

    def part_of(row, block):
        return pl.ds(pl.multiple_of(row * local + block * QB, QB), QB)

    for row in range(rows):
        exchange.arrive(row)
        build_ext(row, local, r.kv, r.coarse, r.edge_near, r.far_all, ext)
        starts = document_bounds(r.seg[row : row + 1, :], seq_len)

        def attend(block, carry):
            gather_keys(ext, block, offset, local, r.keys)
            fill_bias(starts, offset + block * QB, seq_len, r.bias)
            part = part_of(row, block)
            both = jnp.concatenate([r.bias[...], r.bias[...]], axis=1)
            for pair in range(PAIRS):
                r.acc[score_at[pair]] = mm(r.keys[:, lanes_of[pair]], queries(part, pair), NT) + both
            sums = []
            for pair in range(PAIRS):
                scores = r.acc[score_at[pair]]
                peak = jnp.max(scores, axis=0, keepdims=True)
                weights = jnp.exp(scores - peak)
                sums.append(jnp.sum(weights, axis=0, keepdims=True))
                r.totals[row, block, pair : pair + 1, :] = peak + jnp.log(sums[pair])
                r.hid[score_at[pair]] = weights.astype(BF)
            for pair in range(PAIRS):
                mixed_t = mm(r.keys[:, vlanes_of[pair]], r.hid[score_at[pair]], TN) / sums[pair]
                r.mixed[part, lanes_of[pair]] = own_halves(mixed_t).T.astype(BF)
            return carry

        lax.fori_loop(0, min(1, blocks), attend, 0)
        if row == 0:
            gather.relay_z(DOWN)
        lax.fori_loop(min(1, blocks), half, attend, 0)
        if row == 0:
            gather.relay_y(UPB)
        if row == rows - 1:
            gather.relay_y(OUT)
        lax.fori_loop(max(half, min(1, blocks)), blocks, attend, 0)
        if row == 0:
            gather.relay_y(DOWN)
            gather.relay_z(OUT)
            gather.relay_x(UPA)
    gather.settle(OUT)
    for row in range(rows):
        exchange.finish(row)


    def feed_first(i, carry):
        part = tile_of(i)
        resid = r.x[part, :].astype(F32) + mm(r.mixed[part, :], r.fout[...], NN)
        r.ginput[part, :] = resid
        r.acc[part, :] = resid
        hat, _ = norm_parts(resid)
        second = (hat * r.norm[2:3, :] + r.norm[3:4, :]).astype(BF)
        r.x[part, :] = second
        r.second_t[:, part] = second.T
        r.gsec[part, :] = jnp.zeros((tile, D), F32)
        return carry

    gather.relay_x(DOWN)
    lax.fori_loop(0, tiles, feed_first, 0)
    for p in (UPA, UPB, DOWN):
        gather.settle(p)
    gather.finish()
    copies.finish()

    def feed_chunk(f, carry):
        cols = pl.ds(pl.multiple_of(f * CHUNK, CHUNK), CHUNK)

        everything = slice(0, tokens)
        pre = mm(r.x[...], r.fup[:, cols], NN)
        square = pre * pre
        tangent = jnp.tanh(pre * (0.7978845608 + (0.7978845608 * 0.044715) * square))
        upper = 0.5 + 0.5 * tangent
        hidden = pre * upper
        slope = upper + (hidden * (1.0 - tangent)) * (
            0.7978845608 + (0.7978845608 * 3.0 * 0.044715) * square
        )
        hidden = hidden.astype(BF)
        grad_pre = (mm(r.og[...], r.fdown[f], NT) * slope).astype(BF)
        r.hid[everything, :] = hidden
        r.gpre[everything, :] = grad_pre
        r.acc[everything, :] += mm(hidden, r.fdown[f], NN)
        r.gsec[everything, :] += mm(grad_pre, r.fup[:, cols], NT)
        r.fdown[f] = mm(r.og_t[...], r.hid[everything, :], NN).astype(BF)
        r.fup[:, cols] = mm(r.second_t[...], r.gpre[everything, :], NN).astype(BF)
        return carry

    chunks = FF // CHUNK
    lax.fori_loop(0, chunks // 2, feed_chunk, 0)
    for p in reduce.of("first"):
        reduce.start(p)
    lax.fori_loop(chunks // 2, chunks - 1, feed_chunk, 0)
    for p in reduce.of("first"):
        reduce.combine(p)
    lax.fori_loop(chunks - 1, chunks, feed_chunk, 0)
    for p in reduce.of("up", "down"):
        reduce.start(p)
    again = pltpu.make_async_copy(r.x_far, r.x, r.local_sem.at[FETCHES - 1])
    again.start()
    r.grow[...] = jnp.zeros_like(r.grow)

    def feed_last(i, carry):
        part = tile_of(i)
        r.gpre[part, :] = r.acc[part, :].astype(BF)
        hat, inverse = norm_parts(r.ginput[part, :])
        grad = r.gsec[part, :]
        gres = r.og[part, :].astype(F32) + norm_back(grad, hat, inverse, r.norm[2:3, :])
        r.ginput[part, :] = gres
        r.og[part, :] = gres.astype(BF)
        r.grow[2:3, :] += jnp.sum(grad * hat, axis=0, keepdims=True)
        r.grow[3:4, :] += jnp.sum(grad, axis=0, keepdims=True)
        return carry

    lax.fori_loop(0, tiles, feed_last, 0)
    store_out = pltpu.make_async_copy(
        r.gpre.at[0:tokens, :], r.out_far, r.local_sem.at[FETCHES]
    )
    store_out.start()
    for p in reduce.of("first"):
        reduce.second(p)
    for p in reduce.of("up", "down"):
        reduce.combine(p)
    r.gmix[:, 3 * D : 4 * D] = mm(r.mixed[...], r.og[...], TN).astype(BF)
    for p in reduce.of("out"):
        reduce.start(p)

    def mixed_back(i, carry):
        part = tile_of(i)
        r.mixed[part, :] = mm(r.og[part, :], r.fout[...], NT).astype(BF)
        r.og_t[:, part] = r.normed[part, :].T
        return carry

    lax.fori_loop(0, tiles, mixed_back, 0)


    store_out.wait()

    square = jnp.zeros((1, 1), F32)
    for row in range(rows):
        build_ext(row, local, r.kv, r.coarse, r.edge_near, r.far_all, ext)
        starts = document_bounds(r.seg[row : row + 1, :], seq_len)
        for item in gext:
            item[...] = jnp.zeros_like(item)

        def attend_back(block, carry):
            gather_keys(ext, block, offset, local, r.keys)
            fill_bias(starts, offset + block * QB, seq_len, r.bias)
            part = part_of(row, block)
            both = jnp.concatenate([r.bias[...], r.bias[...]], axis=1)
            def grads(pair):
                return lane_halves(r.mixed[part, lanes_of[pair]])

            for pair in range(PAIRS):
                at = score_at[pair]
                r.acc[at] = mm(r.keys[:, lanes_of[pair]], queries(part, pair), NT) + both
                r.gsec[at] = mm(r.keys[:, vlanes_of[pair]], grads(pair), NT)
            for pair in range(PAIRS):
                at = score_at[pair]
                soft = jnp.exp(r.acc[at] - r.totals[row, block, pair : pair + 1, :])
                gsoft = r.gsec[at]
                row_total = jnp.sum(soft * gsoft, axis=0, keepdims=True)
                r.hid[at] = soft.astype(BF)
                r.gpre[at] = (soft * (gsoft - row_total)).astype(BF)
            for pair in range(PAIRS):
                at = score_at[pair]
                gkeys = mm(r.gpre[at], queries(part, pair), NN)
                gvalues = mm(r.hid[at], grads(pair), NN)
                for lv in range(LEVELS):
                    n, at_key = key_rows(lv), key_start(lv)
                    to = pl.ds(pl.multiple_of(window_start(lv, block, offset, local), 16), n)
                    gext[lv][to, lanes_of[pair]] += gkeys[at_key : at_key + n, :]
                    gext[lv][to, vlanes_of[pair]] += gvalues[at_key : at_key + n, :]
                gq_t = own_halves(mm(r.keys[:, lanes_of[pair]], r.gpre[at], TN)) * DH**-0.5
                r.og[part, lanes_of[pair]] = gq_t.T.astype(BF)
            return carry

        lax.fori_loop(0, half, attend_back, 0)
        if row == 0:
            for p in reduce.of("out"):
                reduce.combine(p)
            for p in reduce.of("first"):
                reduce.third(p)
            for p in reduce.of("up"):
                reduce.second(p)
        if row == rows - 1:
            for p in reduce.of("down", "out"):
                reduce.second(p)
            for p in reduce.of("up"):
                reduce.third(p)
        lax.fori_loop(half, blocks, attend_back, 0)
        if row == 0:
            for p in reduce.of("first"):
                square += reduce.final(p)
                reduce.publish(p)
        r.kv[row] = gext[0][16 : 16 + local, :].astype(BF)
        for lv in edge_levels(local):
            n = local >> lv
            to = slice(16 * lv, 16 * lv + 16)
            if lv > 0:
                at = level_offset(local, lv)
                r.coarse[row, at : at + n, :] = gext[lv][16 : 16 + n, :].astype(BF)
            r.edge_own[row, 0, to, :] = gext[lv][0:16, :].astype(BF)
            r.edge_own[row, 1, to, :] = gext[lv][16 + n : 32 + n, :].astype(BF)
        for owner in range(n_seq):
            pieces = []
            used = 0
            for lv in far_levels(local):
                n = local >> lv
                pieces.append(gext[lv][16 + owner * n : 16 + owner * n + n, :])
                used += n
            pieces.append(jnp.zeros((16 - used, 2 * D), F32))
            r.gfar[row, owner] = jnp.concatenate(pieces, axis=0).astype(BF)
        exchange_back.start(row)


    for p in reduce.of("out"):
        reduce.third(p)
    r.gmix[:, 0:D] = mm(r.og_t[...], r.og[...], NN).astype(BF)
    for p in reduce.of("q"):
        reduce.start(p)
    for p in reduce.of("down"):
        reduce.third(p)
    for p in reduce.of("q"):
        reduce.combine(p)

    def settle_inputs(i):
        part = tile_of(i)
        gnormed = (
            mm(r.og[part, :], r.fqkv[0], NT)
            + mm(r.hid[part, :], r.fqkv[1], NT)
            + mm(r.gpre[part, :], r.fqkv[2], NT)
        )
        hat, inverse = norm_parts(r.x[part, :].astype(F32))
        r.ginput[part, :] += norm_back(gnormed, hat, inverse, r.norm[0:1, :])
        r.grow[0:1, :] += jnp.sum(gnormed * hat, axis=0, keepdims=True)
        r.grow[1:2, :] += jnp.sum(gnormed, axis=0, keepdims=True)
        store = pltpu.make_async_copy(
            r.ginput.at[part, :], r.ginput_far.at[part, :], r.local_sem.at[FETCHES + 4 + i]
        )
        store.start()
        return store

    stores = []
    again.wait()
    spread_of = averaging(local)
    for row in range(rows):
        exchange_back.arrive(row)
        base = row * local
        for lv in edge_levels(local):
            n = local >> lv
            for way in range(2):
                more = r.edge_back[row, way, 16 * lv : 16 * lv + 16, :].astype(F32)
                low_row = 0 if way == 0 else n - 16
                if lv == 0:
                    sums = r.kv[row, low_row : low_row + 16, :].astype(F32) + more
                    r.kv[row, low_row : low_row + 16, :] = sums.astype(BF)
                else:
                    at = level_offset(local, lv) + low_row
                    sums = r.coarse[row, at : at + 16, :].astype(F32) + more
                    r.coarse[row, at : at + 16, :] = sums.astype(BF)
        total = r.far_back[row, 0].astype(F32)
        for owner in range(1, n_seq):
            total += r.far_back[row, owner].astype(F32)
        r.coarse[row, local - 16 : local, :] = total.astype(BF)
        for at in range(0, local, tile):
            span, where = slice(at, at + tile), slice(base + at, base + at + tile)
            spread = mm(spread_of[:, span], r.coarse[row], TN)
            pair = (r.kv[row, span, :].astype(F32) + spread).astype(BF)
            r.hid[where, :] = pair[:, 0:D]
            r.gpre[where, :] = pair[:, D : 2 * D]
        if row < rows - 1:
            stores += [settle_inputs(row * row_tiles + i) for i in range(row_tiles)]
    for p in reduce.of("q"):
        reduce.second(p)
    late = reduce.of("kv")
    r.gmix[:, D : 2 * D] = mm(r.og_t[...], r.hid[0:tokens, :], NN).astype(BF)
    if len(late) > 1:
        reduce.start(late[0])
    r.gmix[:, 2 * D : 3 * D] = mm(r.og_t[...], r.gpre[0:tokens, :], NN).astype(BF)
    reduce.start(late[-1])

    stores += [settle_inputs((rows - 1) * row_tiles + i) for i in range(row_tiles)]
    rows_total = SmallSum(me, copies, r.grow, r.small_seq, r.small_dp, n_dp)
    square_total = SmallSum(me, copies, r.square, r.square_seq, r.square_dp, n_dp + 2)
    for p in late:
        reduce.combine(p)
    rows_total.start()
    for p in reduce.of("q"):
        reduce.third(p)
    for p in late:
        reduce.second(p)
    for p in reduce.of("up"):
        square += reduce.final(p)
        reduce.publish(p)
    for p in late:
        reduce.third(p)
    for p in reduce.of("out", "down"):
        square += reduce.final(p)
        reduce.publish(p)
    rows_total.turn()
    for p in reduce.of("q"):
        square += reduce.final(p)
        reduce.publish(p)
    for p in late:
        square += reduce.final(p)
    r.square[...] = jnp.broadcast_to(square, (8, 128))
    square_total.start()
    for p in late:
        reduce.publish(p)
    square_total.turn()
    r.small[...] = rows_total.finish()
    for p in range(len(reduce.parts)):
        reduce.settle(p)
    for at, name in enumerate(("sup", "smix", "sdown")):
        store = pltpu.make_async_copy(
            getattr(r, name), getattr(r, name + "_far"), r.local_sem.at[FETCHES + 1 + at]
        )
        store.start()
        stores.append(store)
    total = square_total.finish()
    r.small[4:5, 0:128] = total[0:1, :]
    for row in range(rows):
        exchange_back.finish(row)
    for store in stores:
        store.wait()
    copies.finish()


DMA = pltpu.SemaphoreType.DMA


class Shapes:
    def __init__(self, inputs, segment_ids):
        self.n_dp, self.n_seq = lax.axis_size("dp"), lax.axis_size("seq")
        self.rows, self.local = inputs.shape[0], inputs.shape[1]
        self.seq_len = segment_ids.shape[1]
        self.tokens = self.rows * self.local
        self.blocks = self.local // QB
        edge = 16 * len(edge_levels(self.local))
        self.edge = (self.rows, 2, edge, 2 * D)
        self.far = (self.rows, self.n_seq, 16, 2 * D)
        ext = [(ext_rows(self.local, self.seq_len, lv), 2 * D) for lv in range(LEVELS)]
        self.ext_low = [pltpu.VMEM(shape, BF) for shape in ext]
        self.ext_wide = [pltpu.VMEM(shape, F32) for shape in ext]
        self.edge_sems = Exchange.sems(self.rows, self.n_seq)
        self.heads = (self.rows, self.local, D)
        self.parts = len(grad_parts(self.n_dp, self.n_seq))
        self.sems = self.n_dp + 2 * SmallSum.sems
        self.sems += self.parts * Reduce.sems(self.n_dp, self.n_seq)
        self.pairs = (self.rows, self.local, 2 * D)


def run_layer(z, inputs, segment_ids, out_grad, w_qkv, w_out, w_up, w_down, norm_params):
    flat = (z.tokens, D)
    named = layer_scratch(z)
    return pl.pallas_call(
        functools.partial(layer_kernel, z, list(named)),
        out_shape=[
            sds(flat, BF),
            sds(flat, F32),
            sds((D // z.n_dp, FF), BF),
            sds((D // z.n_dp, 4 * D), BF),
            sds((D, FF // z.n_dp), BF),
            sds((8, D), F32),
        ],
        in_specs=[ANY if name.endswith("_far") else VM for name in INPUTS],
        out_specs=[ANY if name.endswith("_far") else VM for name in OUTPUTS],
        scratch_shapes=[
            *named.values(),
            *z.ext_low,
            *z.ext_wide,
            *Reduce.scratch(z.n_dp, z.n_seq),
        ],
        compiler_params=params(0),
        name="layer",
    )(
        inputs.reshape(flat),
        segment_ids,
        out_grad.reshape(flat),
        w_qkv,
        w_out,
        w_up,
        w_down,
        norm_params,
    )


def run_adam(z, sums, masters, firsts, seconds, passed):
    shapes = [sds(w.shape, F32) for w in masters]
    norm_shape = sds(firsts[4].shape, F32)
    steps = 2 if D // z.n_dp % 32 == 0 else 1
    coarse = max(1, steps // (FF // z.n_dp // 128))
    down = max(128, FF // z.n_dp // steps)

    def rows_of(shape):
        if len(shape) == 3:
            return pl.BlockSpec((shape[0], shape[1] // steps, shape[2]), lambda i: (0, i, 0))
        return pl.BlockSpec((shape[0] // steps, shape[1]), lambda i: (i, 0))

    def whole(shape):
        return pl.BlockSpec(shape, lambda i: (0, 0))

    big = [rows_of(w.shape) for w in masters]
    big[3] = pl.BlockSpec((down, D), lambda i: (i // coarse, 0))
    norm_spec = whole(firsts[4].shape)
    down_spec = pl.BlockSpec((D, down), lambda i: (0, i // coarse))
    through = [rows_of(item.shape) for item in passed]
    sums_spec = [rows_of(sums[0].shape), rows_of(sums[1].shape), down_spec, whole((8, D))]
    return pl.pallas_call(
        functools.partial(adam_kernel, z.n_dp),
        grid=(steps,),
        out_shape=shapes
        + [norm_shape]
        + shapes
        + [norm_shape]
        + shapes
        + [norm_shape, sds((1, 1), F32)]
        + [sds(item.shape, item.dtype) for item in passed],
        in_specs=sums_spec + big + big + [norm_spec] + big + [norm_spec] + through,
        out_specs=(big + [norm_spec]) * 3 + [whole((1, 1))] + through,
        compiler_params=params(),
        name="adam",
    )(*sums, *masters, *firsts, *seconds, *passed)


def on_device(
    inputs,
    segment_ids,
    out_grad,
    w_qkv,
    w_out,
    w_up,
    w_down,
    norm_params,
    qkv_first,
    qkv_second,
    out_first,
    out_second,
    up_first,
    up_second,
    down_first,
    down_second,
    norm_first,
    norm_second,
):
    z = Shapes(inputs, segment_ids)
    masters = [w_qkv, w_out, w_up, w_down]
    firsts = [qkv_first, out_first, up_first, down_first, norm_first]
    seconds = [qkv_second, out_second, up_second, down_second, norm_second]
    outputs, input_grad, *sums = run_layer(
        z, inputs, segment_ids, out_grad, *masters, norm_params
    )
    updated = run_adam(z, sums, masters, firsts, seconds, (outputs, input_grad))
    return (
        updated[16].reshape(z.heads),
        updated[17].reshape(z.heads),
        updated[15].reshape(()),
        *updated[0:15],
    )


def solution(mesh):
    tokens = P("dp", "seq", None)
    rows, stack, lanes = P("dp", None), P(None, "dp", None), P(None, "dp")
    moments = (stack, stack, rows, rows, rows, rows, rows, rows, lanes, lanes)
    weights = (stack, rows, rows, rows)
    return jax.shard_map(
        on_device,
        mesh=mesh,
        in_specs=(tokens, rows, tokens, *weights, lanes, *moments),
        out_specs=(tokens, tokens, P(), *weights, lanes, *weights, lanes, *weights, lanes),
        check_vma=False,
    )
```

```python
import functools
import math

import jax
import jax.numpy as jnp
from jax import lax
from jax.experimental import pallas as pl
from jax.experimental.pallas import tpu as pltpu
from jax.sharding import PartitionSpec as P

D = 512
HEADS = 8
DH = 64
FF = 2048
LEVELS = 7
DOCS = 4
QB = 128
NKEY = 512
CHUNK = 512
LIMIT = 63
PAIRS = HEADS // 2

masked_score = -1e30
beta_one = 0.9
beta_two = 0.999
bias_first = 1.0 - 0.9**10
bias_second = 1.0 - 0.999**10
learn_rate = 0.1
weight_decay = 0.1
epsilon = 1e-08
clip_norm = 1.0

BF = jnp.bfloat16
F32 = jnp.float32
MESH = pl.DeviceIdType.MESH
VM = pl.BlockSpec(memory_space=pltpu.VMEM)
ANY = pl.BlockSpec(memory_space=pl.ANY)

NN = ((1,), (0,))
NT = ((1,), (1,))
TN = ((0,), (0,))


def mm(left, right, dims):
    return lax.dot_general(left, right, (dims, ((), ())), preferred_element_type=F32)


def params(cid=None):
    if cid is None:
        return pltpu.CompilerParams(vmem_limit_bytes=LIMIT * 2**20)
    return pltpu.CompilerParams(
        vmem_limit_bytes=LIMIT * 2**20, collective_id=cid, has_side_effects=True
    )


def sds(shape, dtype):
    return jax.ShapeDtypeStruct(shape, dtype)


def level_offset(local, level):
    return local - (local >> (level - 1))


def edge_levels(local):
    return [lv for lv in range(LEVELS) if (local >> lv) >= 16]


def far_levels(local):
    return [lv for lv in range(LEVELS) if (local >> lv) < 16]


def ext_rows(local, seq_len, level):
    return ((local >> level) if (local >> level) >= 16 else (seq_len >> level)) + 32


def key_rows(level):
    return max(QB >> level, 16) + 32


def key_start(level):
    return sum(key_rows(lv) for lv in range(level))


def window_start(level, block, offset, local):
    span = 16 << level
    if (local >> level) >= 16:
        if span <= QB:
            return block * (QB >> level)
        return (block * QB) // span * 16
    return (offset + block * QB) // span * 16


def averaging(local):
    row = lax.broadcasted_iota(jnp.int32, (local, local), 0)
    col = lax.broadcasted_iota(jnp.int32, (local, local), 1)
    total = jnp.zeros((local, local), F32)
    for lv in range(1, LEVELS):
        at = lax.shift_right_logical(col, lv) + level_offset(local, lv)
        total = jnp.where(at == row, 2.0**-lv, total)
    return total.astype(BF)


def norm_parts(values):
    center = jnp.mean(values, axis=-1, keepdims=True)
    centered = values - center
    spread = jnp.mean(centered * centered, axis=-1, keepdims=True)
    inverse = lax.rsqrt(spread + 1e-05)
    return centered * inverse, inverse


def norm_back(grad_in, normed, inverse, gain):
    scaled = grad_in * gain
    return inverse * (
        scaled
        - jnp.mean(scaled, axis=-1, keepdims=True)
        - normed * jnp.mean(scaled * normed, axis=-1, keepdims=True)
    )


def document_bounds(seg_row, seq_len):
    return [
        jnp.sum(jnp.where(seg_row < doc, 1.0, 0.0), axis=1, keepdims=True)
        for doc in range(1, DOCS)
    ]


def fill_bias(starts, first_query, seq_len, bias_ref):
    qpos = first_query + lax.broadcasted_iota(jnp.int32, (1, QB), 1)
    qf = qpos.astype(F32)
    low = jnp.zeros((1, QB), F32)
    high = jnp.full((1, QB), float(seq_len), F32)
    for start in starts:
        low = jnp.where(qf >= start, jnp.maximum(low, start), low)
        high = jnp.where(qf < start, jnp.minimum(high, start), high)
    for lv in range(LEVELS):
        span = 16 << lv
        rows = key_rows(lv)
        if span <= QB:
            key_first = first_query // (1 << lv) - 16
        else:
            key_first = first_query // span * 16 - 16
        index = key_first + lax.broadcasted_iota(jnp.int32, (rows, QB), 0)
        begin = (index * (1 << lv)).astype(F32)
        end = begin + float((1 << lv) - 1)
        block = lax.div(qpos, span)
        lo = jnp.maximum(low, ((block - 1) * span).astype(F32))
        hi = jnp.minimum(high, ((block + 2) * span).astype(F32))
        allowed = (begin >= lo) & (end < hi)
        if lv > 0:
            half = span // 2
            parent = lax.div(qpos, half)
            inner_lo = ((parent - 1) * half).astype(F32)
            inner_hi = ((parent + 2) * half).astype(F32)
            allowed = allowed & ((begin < inner_lo) | (begin >= inner_hi))
        bias_ref[key_start(lv) : key_start(lv) + rows, :] = jnp.where(
            allowed, lv * math.log(2.0), masked_score
        )


def build_ext(row, local, kv_ref, coarse_ref, edge_ref, far_ref, ext):
    count = far_ref.shape[1]
    for lv in range(LEVELS):
        rows = local >> lv
        if rows >= 16:
            ext[lv][0:16, :] = edge_ref[row, 0, 16 * lv : 16 * lv + 16, :]
            if lv == 0:
                ext[lv][16 : 16 + rows, :] = kv_ref[row]
            else:
                at = level_offset(local, lv)
                ext[lv][16 : 16 + rows, :] = coarse_ref[row, at : at + rows, :]
            ext[lv][16 + rows : 32 + rows, :] = edge_ref[row, 1, 16 * lv : 16 * lv + 16, :]
        else:
            at = level_offset(local, lv) - (local - 16)
            blank = jnp.zeros((16, 2 * D), F32)
            pieces = [blank]
            for owner in range(count):
                pieces.append(far_ref[row, owner].astype(F32)[at : at + rows, :])
            pieces.append(blank)
            ext[lv][...] = jnp.concatenate(pieces, axis=0).astype(BF)


def gather_keys(ext, block, offset, local, keys_ref):
    for lv in range(LEVELS):
        start = pl.multiple_of(window_start(lv, block, offset, local), 16)
        at = key_start(lv)
        keys_ref[at : at + key_rows(lv), :] = ext[lv][pl.ds(start, key_rows(lv)), :]


def lane_halves(values):
    lane = lax.broadcasted_iota(jnp.int32, values.shape, 1)
    zero = jnp.zeros_like(values)
    return jnp.concatenate(
        [jnp.where(lane < DH, values, zero), jnp.where(lane >= DH, values, zero)], axis=0
    )


def own_halves(pair_t):
    n = pair_t.shape[1] // 2
    sub = lax.broadcasted_iota(jnp.int32, (2 * DH, n), 0)
    return jnp.where(sub < DH, pair_t[:, :n], pair_t[:, n:])


def adam_kernel(n_dp, *refs):
    gup, gmix, gdown, small = refs[0:4]
    weights, firsts, seconds = refs[4:8], refs[8:13], refs[13:18]
    passed, outs, passed_out = refs[18:20], refs[20:36], refs[36:38]
    for here, there in zip(passed, passed_out):
        there[...] = here[...]

    new_w, norm_grad, new_m, new_s, grad_norm = (
        outs[0:4],
        outs[4],
        outs[5:10],
        outs[10:15],
        outs[15],
    )
    own = small[0:4, :]
    square = jnp.sum(jnp.sum(own * own, axis=0, keepdims=True), axis=1, keepdims=True)
    root = jnp.sqrt(square + small[4:5, 0:1])
    grad_norm[...] = root
    factor = jnp.minimum(1.0, clip_norm / root)

    def moments(clipped, first, second):
        return (
            beta_one * first + (1.0 - beta_one) * clipped,
            beta_two * second + (1.0 - beta_two) * clipped * clipped,
        )

    def update(weight, grad, first, second):
        mean, sq = moments(grad * factor, first, second)
        change = mean / bias_first / (jnp.sqrt(sq / bias_second) + epsilon) + weight_decay * weight
        return weight - learn_rate * change, mean, sq

    for c in range(3):
        w, m, s = update(
            weights[0][c], gmix[:, c * D : c * D + D].astype(F32), firsts[0][c], seconds[0][c]
        )
        new_w[0][c], new_m[0][c], new_s[0][c] = w, m, s
    for at, grad in ((1, gmix[:, 3 * D : 4 * D]), (2, gup[...]), (3, gdown[...])):
        grad = grad.astype(F32)
        if at == 3:
            grad = grad.T
        w, m, s = update(weights[at][...], grad, firsts[at][...], seconds[at][...])
        new_w[at][...], new_m[at][...], new_s[at][...] = w, m, s
    width = D // n_dp
    lane = lax.axis_index("dp") * width
    rolled = pltpu.roll(small[...], D - lane, 1)[0:4, 0:width]
    clipped = rolled * factor
    norm_grad[...] = clipped
    m, s = moments(clipped, firsts[4][...], seconds[4][...])
    new_m[4][...], new_s[4][...] = m, s


class Copies:
    def __init__(self, send, recv):
        self.send, self.recv = send, recv
        self.started = []

    def push(self, src, dst, send_at, recv_at, device, alone=True):
        copy = pltpu.make_async_remote_copy(
            src_ref=src,
            dst_ref=dst,
            send_sem=self.send.at[send_at],
            recv_sem=self.recv.at[recv_at],
            device_id=device,
            device_id_type=MESH,
        )
        copy.start()
        if alone:
            self.started.append(copy)

    def arrived(self, dst, recv_at, device):
        pltpu.make_async_remote_copy(
            src_ref=dst,
            dst_ref=dst,
            send_sem=self.send.at[0],
            recv_sem=self.recv.at[recv_at],
            device_id=device,
            device_id_type=MESH,
        ).wait_recv()

    def left(self, src, send_at, device):
        pltpu.make_async_remote_copy(
            src_ref=src,
            dst_ref=src,
            send_sem=self.send.at[send_at],
            recv_sem=self.recv.at[0],
            device_id=device,
            device_id_type=MESH,
        ).wait_send()

    def finish(self):
        for copy in self.started:
            copy.wait_send()
        self.started = []


def greet(peers):
    barrier = pltpu.get_barrier_semaphore()
    for peer in peers:
        pl.semaphore_signal(barrier, inc=1, device_id=peer, device_id_type=MESH)
    pl.semaphore_wait(barrier, len(peers))


class Place:
    def __init__(self, n_dp, n_seq):
        self.n_dp, self.n_seq = n_dp, n_seq
        self.d, self.s = lax.axis_index("dp"), lax.axis_index("seq")
        self.z, self.y = lax.div(self.d, 2), lax.rem(self.d, 2)
        self.hi, self.core = lax.div(self.s, 2), lax.rem(self.s, 2)
        self.depth, self.high = n_dp // 2, n_seq // 2
        self.mate = self.s + 1 - 2 * self.core
        self.flip = self.d + 1 - 2 * self.y
        self.seq_others = [lax.rem(self.s + k, n_seq) for k in range(1, n_seq)]
        self.dp_others = [lax.rem(self.d + k, n_dp) for k in range(1, n_dp)]

    def greet(self):
        greet([(self.d, o) for o in self.seq_others] + [(o, self.s) for o in self.dp_others])


class Gather:
    def __init__(self, place, parts, copies, base, send_base, measure):
        self.at, self.parts, self.copies, self.base = place, parts, copies, base
        self.send_base, self.measure = send_base, measure
        self.stride = self.sems(place.n_dp, place.n_seq)

    @staticmethod
    def sems(n_dp, n_seq):
        return 2 * (n_dp // 2) + 2

    def split(self, p):
        high = self.at.high
        return self.parts[p][4] and high > 1 and self.parts[p][3] % (32 * high) == 0

    def piece(self, p, shard, core, hi):
        _, whole, lead, rows, _ = self.parts[p]
        n = rows // 2
        start = shard * rows + core * n
        if self.split(p):
            n = n // self.at.high
            start = start + hi * n
        if lead is None:
            return whole.at[pl.ds(pl.multiple_of(start, n), n), :]
        if lead == "blocks":
            row = pl.multiple_of(lax.rem(start, CHUNK), n)
            return whole.at[lax.div(start, CHUNK), pl.ds(row, n), :]
        return whole.at[lead[0] : lead[1], pl.ds(pl.multiple_of(start, n), n), :]

    def sem(self, p, stage, index=0):
        at = self.base + p * self.stride
        sizes = (self.at.depth, self.at.depth, 1)
        return at + sum(sizes[:stage]) + index

    def push(self, p, here, recv_at, device):
        self.copies.push(here, here, self.send_base + p, recv_at, device, alone=False)

    def share(self, p, rows):
        _, whole, lead, _, _ = self.parts[p]
        if lead is None:
            return whole.at[0:rows, :]
        if lead == "blocks":
            return self.measure.at[0 : rows * D // FF, :]
        return whole.at[lead[0] : lead[1], 0:rows, :]

    def load(self, p):
        own, whole, lead, rows, _ = self.parts[p]
        start = pl.multiple_of(self.at.d * rows, rows)
        if isinstance(lead, tuple):
            for c in range(*lead):
                whole[c, pl.ds(start, rows), :] = own[c][...].astype(BF)
        elif isinstance(own, list):
            for c, item in enumerate(own):
                whole.at[pl.ds(start, rows), c * D : c * D + D][...] = item[...].astype(BF)
        elif lead is None:
            whole[pl.ds(start, rows), :] = own[...].astype(BF)
        elif lead == "blocks":
            row = pl.multiple_of(lax.rem(start, CHUNK), rows)
            whole[lax.div(start, CHUNK), pl.ds(row, rows), :] = own[...].astype(BF)

    def start(self, p):
        me = self.at
        self.load(p)
        mine = self.piece(p, me.d, me.core, me.hi)
        for k in range(1, me.depth):
            other = lax.rem(me.z + k, me.depth) * 2 + me.y
            self.push(p, mine, self.sem(p, 0, me.z), (other, me.s))
        self.push(p, mine, self.sem(p, 1, me.z), (me.flip, me.s))

    def onward(self, p, shard):
        me = self.at
        here = self.piece(p, shard, me.core, me.hi)
        if self.split(p):
            for kh in range(1, me.high):
                other = lax.rem(me.hi + kh, me.high) * 2 + me.core
                self.push(p, here, self.sem(p, 2), (me.d, other))
        self.push(p, here, self.sem(p, 3), (me.d, me.mate))

    def relay_z(self, p):
        me = self.at
        for k in range(1, me.depth):
            zz = lax.rem(me.z + k, me.depth)
            shard = zz * 2 + me.y
            here = self.piece(p, shard, me.core, me.hi)
            self.copies.arrived(here, self.sem(p, 0, zz), (shard, me.s))
            self.push(p, here, self.sem(p, 1, zz), (me.flip, me.s))
            self.onward(p, shard)

    def relay_y(self, p):
        me = self.at
        for k in range(me.depth):
            zz = lax.rem(me.z + k, me.depth)
            shard = zz * 2 + 1 - me.y
            here = self.piece(p, shard, me.core, me.hi)
            self.copies.arrived(here, self.sem(p, 1, zz), (me.flip, me.s))
            self.onward(p, shard)

    def relay_x(self, p):
        me = self.at
        if not self.split(p):
            return
        rows = self.parts[p][3] // (2 * me.high) * (me.n_dp - 1) * (me.high - 1)
        mirror = lax.rem(me.hi + 1, me.high) * 2 + me.core
        self.copies.arrived(self.share(p, rows), self.sem(p, 2), (me.d, mirror))
        for kh in range(1, me.high):
            h = lax.rem(me.hi + kh, me.high)
            for k in range(1, me.n_dp):
                shard = lax.rem(me.d + k, me.n_dp)
                here = self.piece(p, shard, me.core, h)
                self.push(p, here, self.sem(p, 3), (me.d, me.mate))

    def settle(self, p):
        me = self.at
        rows = self.parts[p][3] // 2 * (me.n_dp - 1)
        self.copies.arrived(self.share(p, rows), self.sem(p, 3), (me.d, me.mate))

    def finish(self):
        me = self.at
        for p, part in enumerate(self.parts):
            ref = self.share(p, part[3] * (me.n_dp - 1))
            self.copies.left(ref, self.send_base + p, (me.d, me.mate))


class Exchange:
    def __init__(self, place, personal, edge_in, far_in, edge_out, far_out, send, recv):
        self.at, self.personal = place, personal
        self.edge_in, self.far_in, self.edge_out, self.far_out = edge_in, far_in, edge_out, far_out
        self.send, self.recv = send, recv

    @staticmethod
    def sems(rows, n_seq):
        return rows * (2 + n_seq)

    def edge(self, row, way, device):
        base = row * (2 + self.at.n_seq)
        return pltpu.make_async_remote_copy(
            src_ref=self.edge_in.at[row, way],
            dst_ref=self.edge_out.at[row, 1 - way],
            send_sem=self.send.at[base + way],
            recv_sem=self.recv.at[base + 1 - way],
            device_id=(self.at.d, device),
            device_id_type=MESH,
        )

    def far_rows(self, row, other):
        if self.personal:
            return self.far_in.at[row, other]
        local = self.far_in.shape[1]
        return self.far_in.at[row, local - 16 : local, :]

    def far(self, row, k, other):
        base = row * (2 + self.at.n_seq) + 2
        return pltpu.make_async_remote_copy(
            src_ref=self.far_rows(row, other),
            dst_ref=self.far_out.at[row, self.at.s],
            send_sem=self.send.at[base + k],
            recv_sem=self.recv.at[base + self.at.s],
            device_id=(self.at.d, other),
            device_id_type=MESH,
        )

    def start(self, row):
        s, n_seq = self.at.s, self.at.n_seq

        @pl.when(s > 0)
        def _():
            self.edge(row, 0, s - 1).start()

        @pl.when(s < n_seq - 1)
        def _():
            self.edge(row, 1, s + 1).start()

        for k, other in enumerate(self.at.seq_others):
            self.far(row, k, other).start()
        self.far_out[row, s] = self.far_rows(row, s)[...]

    def arrive(self, row):
        s, n_seq = self.at.s, self.at.n_seq
        blank = jnp.zeros(self.edge_out.shape[2:], BF)

        @pl.when(s > 0)
        def _():
            self.edge(row, 1, s - 1).wait_recv()

        @pl.when(s == 0)
        def _():
            self.edge_out[row, 0] = blank

        @pl.when(s < n_seq - 1)
        def _():
            self.edge(row, 0, s + 1).wait_recv()

        @pl.when(s == n_seq - 1)
        def _():
            self.edge_out[row, 1] = blank

        base = row * (2 + n_seq) + 2
        for other in self.at.seq_others:
            here = self.far_out.at[row, other]
            pltpu.make_async_remote_copy(
                src_ref=here,
                dst_ref=here,
                send_sem=self.send.at[base],
                recv_sem=self.recv.at[base + other],
                device_id=(self.at.d, other),
                device_id_type=MESH,
            ).wait_recv()

    def finish(self, row):
        s, n_seq = self.at.s, self.at.n_seq

        @pl.when(s > 0)
        def _():
            self.edge(row, 0, s - 1).wait_send()

        @pl.when(s < n_seq - 1)
        def _():
            self.edge(row, 1, s + 1).wait_send()

        for k, other in enumerate(self.at.seq_others):
            self.far(row, k, other).wait_send()


class SmallSum:
    sems = 2

    def __init__(self, place, copies, own, seq_in, dp_in, base):
        self.at, self.copies, self.own = place, copies, own
        self.seq_in, self.dp_in, self.base = seq_in, dp_in, base

    def start(self):
        me = self.at
        self.seq_in[me.s] = self.own[...]
        for o in me.seq_others:
            here = self.seq_in.at[me.s]
            self.copies.push(self.own, here, self.base, self.base, (me.d, o), alone=False)

    def turn(self):
        me = self.at
        rest = self.seq_in.at[0 : me.n_seq - 1]
        self.copies.arrived(rest, self.base, (me.d, me.mate))
        total = self.seq_in[0]
        for o in range(1, me.n_seq):
            total += self.seq_in[o]
        self.dp_in[me.d] = total
        for o in me.dp_others:
            here = self.dp_in.at[me.d]
            self.copies.push(here, here, self.base + 1, self.base + 1, (o, me.s), alone=False)

    def finish(self):
        me = self.at
        rest = self.dp_in.at[0 : me.n_dp - 1]
        self.copies.arrived(rest, self.base + 1, (me.flip, me.s))
        total = self.dp_in[0]
        for o in range(1, me.n_dp):
            total += self.dp_in[o]
        self.copies.left(self.seq_in.at[0 : me.n_seq - 1], self.base, (me.d, me.mate))
        self.copies.left(rest, self.base + 1, (me.flip, me.s))
        return total


def grad_parts(n_dp, n_seq):
    if D // n_seq % 128:
        return [
            (0, 0, FF, True, True, "up"),
            (1, 0, FF, False, False, "down"),
            (2, 0, 4 * D, True, True, "kv"),
        ]
    return [
        (0, 0, FF // 2, True, True, "first"),
        (0, FF // 2, FF, True, True, "up"),
        (1, 0, FF, False, False, "down"),
        (2, 3 * D, 4 * D, True, True, "out"),
        (2, 0, D, True, False, "q"),
        (2, D, 2 * D, True, True, "kv"),
        (2, 2 * D, 3 * D, True, False, "kv"),
    ]


def block_shape(part, n_dp, n_seq):
    _, lo, hi, by_rows, _, _ = part
    if by_rows:
        return (D // n_dp, (hi - lo) // n_seq)
    return (D // n_seq, (hi - lo) // n_dp)


class Reduce:
    def __init__(self, place, sources, finals, buffers, copies, base):
        self.at, self.sources, self.finals = place, sources, finals
        self.parts = grad_parts(place.n_dp, place.n_seq)
        n = len(self.parts)
        groups = [buffers[i * n : i * n + n] for i in range(5)]
        self.core_in, self.held, self.high_in, self.y_in, self.z_in = groups
        self.copies, self.base = copies, base
        self.stride = self.sems(place.n_dp, place.n_seq)

    @staticmethod
    def sems(n_dp, n_seq):
        return 2 + (n_seq // 2 - 1) + (n_dp // 2 - 1) + 1

    @staticmethod
    def scratch(n_dp, n_seq):
        high, depth = n_seq // 2, n_dp // 2
        groups = [[], [], [], [], []]
        for part in grad_parts(n_dp, n_seq):
            _, lo, up, by_rows, first, _ = part
            a, b = block_shape(part, n_dp, n_seq)
            shapes = [
                (D, (up - lo) // 2) if by_rows else (FF // CHUNK, D // 2, CHUNK),
                (high, depth, 2, a, b),
                (high - 1, depth, 2, a, b) if first else (high - 1, depth, a, b),
                (depth, a, b) if first else (high, depth, a, b),
                (depth - 1, a, b),
            ]
            for group, shape in zip(groups, shapes):
                group.append(pltpu.VMEM(shape, BF))
        return [item for group in groups for item in group]

    def of(self, *stages):
        return [p for p, part in enumerate(self.parts) if part[5] in stages]

    def sem(self, p, stage, index=0):
        sizes = (1, 1, self.at.high - 1, self.at.depth - 1)
        return self.base + p * self.stride + sum(sizes[:stage]) + index

    def start(self, p):
        me = self.at
        src, lo, up, by_rows, _, _ = self.parts[p]
        ref = self.sources[src]
        which = 1 - me.core
        if by_rows:
            w = (up - lo) // 2
            half = ref.at[:, pl.ds(pl.multiple_of(lo + which * w, 128), w)]
        else:
            w = D // 2
            half = ref.at[:, pl.ds(pl.multiple_of(which * w, w), w), :]
        self.copies.push(half, self.core_in[p], self.sem(p, 0), self.sem(p, 0), (me.d, me.mate))

    def push_y(self, p, held):
        me = self.at
        self.copies.push(held, self.y_in[p], self.sem(p, 1), self.sem(p, 1), (me.flip, me.s))

    def take_y(self, p):
        me = self.at
        self.copies.arrived(self.y_in[p], self.sem(p, 1), (me.flip, me.s))


    def push_high(self, p, y):
        me = self.at
        for k in range(1, me.high):
            h = lax.rem(me.hi + k, me.high)
            src = self.held[p].at[h] if y is None else self.held[p].at[h, :, y]
            self.copies.push(
                src,
                self.high_in[p].at[me.high - k - 1],
                self.sem(p, 2, k - 1),
                self.sem(p, 2, me.high - k - 1),
                (me.d, h * 2 + me.core),
            )

    def take_high(self, p):
        me = self.at
        for k in range(1, me.high):
            h = lax.rem(me.hi + k, me.high)
            self.copies.arrived(
                self.high_in[p].at[k - 1], self.sem(p, 2, k - 1), (me.d, h * 2 + me.core)
            )

    def combine(self, p):
        me = self.at
        part = self.parts[p]
        src, lo, up, by_rows, first, _ = part
        a, b = block_shape(part, me.n_dp, me.n_seq)
        self.copies.arrived(self.core_in[p], self.sem(p, 0), (me.d, me.mate))
        theirs, held, source = self.core_in[p], self.held[p], self.sources[src]
        for h in range(me.high):
            for shard in range(me.n_dp):
                which = me.core * me.high + h
                if by_rows:
                    r = slice(shard * a, shard * a + a)
                    left = source[r, pl.ds(pl.multiple_of(lo + which * b, 128), b)]
                    right = theirs[r, h * b : h * b + b]
                else:
                    block, lane = shard * b // CHUNK, shard * b % CHUNK
                    lanes = slice(lane, lane + b)
                    left = source[block, pl.ds(pl.multiple_of(which * a, a), a), lanes]
                    right = theirs[block, h * a : h * a + a, lanes]
                total = left.astype(F32) + right.astype(F32)
                held[h, shard // 2, shard % 2] = total.astype(BF)
        if first:
            self.push_high(p, None)
        else:
            self.push_y(p, held.at[:, :, 1 - me.y])

    def add_high(self, p):
        me = self.at
        held = self.held[p]
        self.take_high(p)
        first = self.parts[p][4]
        for zz in range(me.depth):
            for yy in (0, 1) if first else (me.y,):
                value = held[me.hi, zz, yy].astype(F32)
                for k in range(me.high - 1):
                    more = self.high_in[p][k, zz, yy] if first else self.high_in[p][k, zz]
                    value += more.astype(F32)
                held[me.hi, zz, yy] = value.astype(BF)

    def second(self, p):
        me = self.at
        held = self.held[p]
        if self.parts[p][4]:
            self.add_high(p)
            self.push_y(p, held.at[me.hi, :, 1 - me.y])
        else:
            self.take_y(p)
            for h in range(me.high):
                for zz in range(me.depth):
                    value = held[h, zz, me.y].astype(F32) + self.y_in[p][h, zz].astype(F32)
                    held[h, zz, me.y] = value.astype(BF)
            self.push_high(p, me.y)

    def third(self, p):
        me = self.at
        held = self.held[p]
        if self.parts[p][4]:
            self.take_y(p)
            for zz in range(me.depth):
                value = held[me.hi, zz, me.y].astype(F32) + self.y_in[p][zz].astype(F32)
                held[me.hi, zz, me.y] = value.astype(BF)
        else:
            self.add_high(p)
        for k in range(1, me.depth):
            zz = lax.rem(me.z + k, me.depth)
            self.copies.push(
                held.at[me.hi, zz, me.y],
                self.z_in[p].at[me.depth - k - 1],
                self.sem(p, 3, k - 1),
                self.sem(p, 3, me.depth - k - 1),
                (zz * 2 + me.y, me.s),
            )

    def place_of(self, p, owner):
        part = self.parts[p]
        src, lo, up, by_rows, _, _ = part
        a, b = block_shape(part, self.at.n_dp, self.at.n_seq)
        which = lax.rem(owner, 2) * self.at.high + lax.div(owner, 2)
        if by_rows:
            return self.finals[src].at[:, pl.ds(pl.multiple_of(lo + which * b, 128), b)]
        return self.finals[src].at[pl.ds(pl.multiple_of(which * a, a), a), :]

    def final(self, p):
        me = self.at
        value = self.held[p][me.hi, me.z, me.y].astype(F32)
        for k in range(1, me.depth):
            zz = lax.rem(me.z + k, me.depth)
            self.copies.arrived(self.z_in[p].at[k - 1], self.sem(p, 3, k - 1), (zz * 2 + me.y, me.s))
            value += self.z_in[p][k - 1].astype(F32)
        low = value.astype(BF)
        here = self.place_of(p, me.s)
        here[...] = low
        value = low.astype(F32)
        return jnp.sum(jnp.sum(value * value, axis=0, keepdims=True), axis=1, keepdims=True)

    def publish(self, p):
        me = self.at
        here = self.place_of(p, me.s)
        for o in me.seq_others:
            self.copies.push(here, here, self.sem(p, 4), self.sem(p, 4), (me.d, o), alone=False)

    def share(self, p):
        part = self.parts[p]
        a, b = block_shape(part, self.at.n_dp, self.at.n_seq)
        n = self.at.n_seq - 1
        if part[3]:
            return self.finals[part[0]].at[:, 0 : n * b]
        return self.finals[part[0]].at[0 : n * a, :]

    def settle(self, p):
        me = self.at
        self.copies.arrived(self.share(p), self.sem(p, 4), (me.d, me.mate))
        self.copies.left(self.share(p), self.sem(p, 4), (me.d, me.mate))


class Named:
    def __init__(self, names, refs):
        for name, ref in zip(names, refs):
            setattr(self, name, ref)


INPUTS = ["x_far", "seg", "og_far", "wqkv_far", "wout_far", "wup_far", "wdown_far", "norm_own"]
OUTPUTS = ["out_far", "ginput_far", "sup_far", "smix_far", "sdown_far", "small"]
FETCHES = 8 + FF // D
PARTS = 7


def layer_scratch(z):
    tokens = (z.tokens, D)
    tall = (max(z.tokens, 2 * NKEY), D)
    return {
        "slots": pltpu.VMEM((z.n_dp, 8, 128), F32),
        "norm": pltpu.VMEM((8, D), F32),
        "fqkv": pltpu.VMEM((3, D, D), BF),
        "fout": pltpu.VMEM((D, D), BF),
        "fup": pltpu.VMEM((D, FF), BF),
        "fdown": pltpu.VMEM((FF // CHUNK, CHUNK, D), BF),
        "normed": pltpu.VMEM(tokens, BF),
        "q": pltpu.VMEM(tokens, BF),
        "kv": pltpu.VMEM(z.pairs, BF),
        "coarse": pltpu.VMEM(z.pairs, BF),
        "edge_own": pltpu.VMEM(z.edge, BF),
        "edge_near": pltpu.VMEM(z.edge, BF),
        "edge_back": pltpu.VMEM(z.edge, BF),
        "far_all": pltpu.VMEM(z.far, BF),
        "gfar": pltpu.VMEM(z.far, BF),
        "far_back": pltpu.VMEM(z.far, BF),
        "keys": pltpu.VMEM((NKEY, 2 * D), BF),
        "bias": pltpu.VMEM((NKEY, QB), F32),
        "mixed": pltpu.VMEM(tokens, BF),
        "totals": pltpu.VMEM((z.rows, z.blocks, PAIRS, 2 * QB), F32),
        "second_t": pltpu.VMEM((D, z.tokens), BF),
        "og_t": pltpu.VMEM((D, z.tokens), BF),
        "acc": pltpu.VMEM(tall, F32),
        "gsec": pltpu.VMEM(tall, F32),
        "hid": pltpu.VMEM(tall, BF),
        "gpre": pltpu.VMEM(tall, BF),
        "gmix": pltpu.VMEM((D, 4 * D), BF),
        "grow": pltpu.VMEM((8, D), F32),
        "small_seq": pltpu.VMEM((z.n_seq, 8, D), F32),
        "small_dp": pltpu.VMEM((z.n_dp, 8, D), F32),
        "square": pltpu.VMEM((8, 128), F32),
        "square_seq": pltpu.VMEM((z.n_seq, 8, 128), F32),
        "square_dp": pltpu.VMEM((z.n_dp, 8, 128), F32),
        "send": DMA((z.sems + PARTS,)),
        "recv": DMA((z.sems + PARTS * Gather.sems(z.n_dp, z.n_seq),)),
        "edge_send": DMA((z.edge_sems,)),
        "edge_recv": DMA((z.edge_sems,)),
        "back_send": DMA((z.edge_sems,)),
        "back_recv": DMA((z.edge_sems,)),
        "local_sem": DMA((FETCHES + 4 + z.tokens // min(z.local, 512),)),
        "sup": pltpu.VMEM((D // z.n_dp, FF), BF),
        "smix": pltpu.VMEM((D // z.n_dp, 4 * D), BF),
        "sdown": pltpu.VMEM((D, FF // z.n_dp), BF),
        "x": pltpu.VMEM(tokens, BF),
        "og": pltpu.VMEM(tokens, BF),
        "ginput": pltpu.VMEM(tokens, F32),
    }


def layer_kernel(z, names, *refs):
    count = len(INPUTS) + len(OUTPUTS) + len(names)
    r = Named(INPUTS + OUTPUTS + names, refs[:count])
    ext = refs[count : count + LEVELS]
    gext = refs[count + LEVELS : count + 2 * LEVELS]
    buffers = refs[count + 2 * LEVELS :]
    rows, local, tokens, seq_len = z.rows, z.local, z.tokens, z.seq_len
    n_dp, n_seq = z.n_dp, z.n_seq
    shard = D // n_dp
    down = FF // n_dp
    own_down = r.gsec.at[0:down, :]
    own_out = r.gsec.at[down : down + shard, :]
    own_up = [
        r.gsec.at[down + shard * (c + 1) : down + shard * (c + 2), :] for c in range(FF // D)
    ]
    moves = [(r.x_far, r.x), (r.og_far, r.og), (r.wdown_far, own_down), (r.wout_far, own_out)]
    moves += [(r.wup_far.at[:, c * D : c * D + D], to) for c, to in enumerate(own_up)]
    own_qkv = [r.acc.at[c * shard : c * shard + shard, :] for c in range(3)]
    moves += [(r.wqkv_far.at[c], to) for c, to in enumerate(own_qkv)]
    fetch = [
        pltpu.make_async_copy(here, there, r.local_sem.at[at])
        for at, (here, there) in enumerate(moves)
    ]
    for copy in fetch[-3:] + fetch[:-3]:
        copy.start()
    me = Place(n_dp, n_seq)
    me.greet()
    copies = Copies(r.send, r.recv)
    reduce_base = n_dp + 2 * SmallSum.sems
    gather_base = reduce_base + z.parts * Reduce.sems(n_dp, n_seq)
    gather = Gather(
        me,
        [
            (own_qkv, r.fqkv, (1, 2), shard, True),
            (own_qkv, r.fqkv, (2, 3), shard, True),
            (own_qkv, r.fqkv, (0, 1), shard, True),
            (own_up[: FF // D // 2], r.fup.at[:, 0 : FF // 2], None, shard, True),
            (own_up[FF // D // 2 :], r.fup.at[:, FF // 2 : FF], None, shard, False),
            (own_down, r.fdown, "blocks", down, True),
            (own_out, r.fout, None, shard, False),
        ],
        copies,
        gather_base,
        gather_base,
        r.fup,
    )
    K, V, Q, UPA, UPB, DOWN, OUT = range(PARTS)
    reduce = Reduce(
        me,
        (r.fup, r.fdown, r.gmix),
        (r.sup, r.sdown, r.smix),
        buffers,
        copies,
        reduce_base,
    )
    exchange = Exchange(
        me, False, r.edge_own, r.coarse, r.edge_near, r.far_all, r.edge_send, r.edge_recv
    )
    exchange_back = Exchange(
        me, True, r.edge_own, r.gfar, r.edge_back, r.far_back, r.back_send, r.back_recv
    )
    tile = min(local, 512)
    tiles = tokens // tile
    row_tiles = local // tile

    def tile_of(i):
        return pl.ds(pl.multiple_of(i * tile, tile), tile)


    r.slots[me.d] = jnp.zeros((8, 128), F32)
    r.slots[me.d, 0:4, 0:shard] = r.norm_own[...].astype(BF).astype(F32)
    for k, o in enumerate(me.dp_others):
        copies.push(r.slots.at[me.d], r.slots.at[me.d], 1 + k, me.d, (o, me.s))
    for copy in fetch[-3:]:
        copy.wait()
    gather.start(K)
    gather.start(V)
    gather.start(Q)
    mean_of = averaging(local)
    for o in me.dp_others:
        copies.arrived(r.slots.at[o], o, (o, me.s))
    total = jnp.zeros((8, D), F32)
    for at in range(n_dp):
        i = lax.broadcasted_iota(jnp.int32, (128, D), 0)
        j = lax.broadcasted_iota(jnp.int32, (128, D), 1)
        pick = jnp.where((j == i + at * shard) & (i < shard), 1.0, 0.0).astype(BF)
        total += mm(r.slots[at].astype(BF), pick, NN)
    r.norm[...] = total
    fetch[0].wait()
    fetch[1].wait()

    def normalize(i, carry):
        part = tile_of(i)
        hat, _ = norm_parts(r.x[part, :].astype(F32))
        r.normed[part, :] = (hat * r.norm[0:1, :] + r.norm[1:2, :]).astype(BF)
        r.og_t[:, part] = r.og[part, :].T
        return carry

    lax.fori_loop(0, tiles, normalize, 0)
    gather.relay_z(K)
    gather.relay_z(V)
    gather.relay_y(K)
    gather.relay_z(Q)
    for copy in fetch[4:-3]:
        copy.wait()
    gather.start(UPA)
    gather.relay_y(V)
    gather.relay_x(K)
    gather.start(UPB)
    gather.relay_y(Q)
    gather.relay_x(V)
    gather.settle(K)
    gather.settle(V)
    fetch[2].wait()
    gather.start(DOWN)
    for row in range(rows):

        def project_kv(i, carry):
            part = tile_of(i)
            normed = r.normed[tile_of(row * row_tiles + i), :]
            r.kv[row, part, 0:D] = mm(normed, r.fqkv[1], NN).astype(BF)
            r.kv[row, part, D : 2 * D] = mm(normed, r.fqkv[2], NN).astype(BF)
            return carry

        lax.fori_loop(0, row_tiles, project_kv, 0)
        r.coarse[row] = mm(mean_of, r.kv[row], NN).astype(BF)
        for lv in edge_levels(local):
            n = local >> lv
            to = slice(16 * lv, 16 * lv + 16)
            if lv == 0:
                r.edge_own[row, 0, to, :] = r.kv[row, 0:16, :]
                r.edge_own[row, 1, to, :] = r.kv[row, n - 16 : n, :]
            else:
                at = level_offset(local, lv)
                r.edge_own[row, 0, to, :] = r.coarse[row, at : at + 16, :]
                r.edge_own[row, 1, to, :] = r.coarse[row, at + n - 16 : at + n, :]
        exchange.start(row)
        if row == 0:
            gather.relay_x(Q)
            gather.relay_z(UPA)
            fetch[3].wait()
            gather.start(OUT)
    gather.settle(Q)

    def project_q(i, carry):
        part = tile_of(i)
        r.q[part, :] = mm(r.normed[part, :], r.fqkv[0], NN).astype(BF)
        return carry

    lax.fori_loop(0, tiles, project_q, 0)
    gather.relay_y(UPA)
    gather.relay_z(UPB)


    offset = me.s * local
    blocks = local // QB
    half = blocks // 2

    score_at = [
        (slice(p // 2 * NKEY, p // 2 * NKEY + NKEY), slice(p % 2 * 2 * QB, p % 2 * 2 * QB + 2 * QB))
        for p in range(PAIRS)
    ]
    lanes_of = [slice(128 * p, 128 * p + 128) for p in range(PAIRS)]
    vlanes_of = [slice(D + 128 * p, D + 128 * p + 128) for p in range(PAIRS)]

    def queries(part, pair):
        return lane_halves(r.q[part, lanes_of[pair]] * BF(DH**-0.5))

    def part_of(row, block):
        return pl.ds(pl.multiple_of(row * local + block * QB, QB), QB)

    for row in range(rows):
        exchange.arrive(row)
        build_ext(row, local, r.kv, r.coarse, r.edge_near, r.far_all, ext)
        starts = document_bounds(r.seg[row : row + 1, :], seq_len)

        def attend(block, carry):
            gather_keys(ext, block, offset, local, r.keys)
            fill_bias(starts, offset + block * QB, seq_len, r.bias)
            part = part_of(row, block)
            both = jnp.concatenate([r.bias[...], r.bias[...]], axis=1)
            for pair in range(PAIRS):
                r.acc[score_at[pair]] = mm(r.keys[:, lanes_of[pair]], queries(part, pair), NT) + both
            sums = []
            for pair in range(PAIRS):
                scores = r.acc[score_at[pair]]
                peak = jnp.max(scores, axis=0, keepdims=True)
                weights = jnp.exp(scores - peak)
                sums.append(jnp.sum(weights, axis=0, keepdims=True))
                r.totals[row, block, pair : pair + 1, :] = peak + jnp.log(sums[pair])
                r.hid[score_at[pair]] = weights.astype(BF)
            for pair in range(PAIRS):
                mixed_t = mm(r.keys[:, vlanes_of[pair]], r.hid[score_at[pair]], TN) / sums[pair]
                r.mixed[part, lanes_of[pair]] = own_halves(mixed_t).T.astype(BF)
            return carry

        lax.fori_loop(0, min(1, blocks), attend, 0)
        if row == 0:
            gather.relay_z(DOWN)
        lax.fori_loop(min(1, blocks), half, attend, 0)
        if row == 0:
            gather.relay_y(UPB)
        if row == rows - 1:
            gather.relay_y(OUT)
        lax.fori_loop(max(half, min(1, blocks)), blocks, attend, 0)
        if row == 0:
            gather.relay_y(DOWN)
            gather.relay_z(OUT)
            gather.relay_x(UPA)
    gather.settle(OUT)
    for row in range(rows):
        exchange.finish(row)


    def feed_first(i, carry):
        part = tile_of(i)
        resid = r.x[part, :].astype(F32) + mm(r.mixed[part, :], r.fout[...], NN)
        r.ginput[part, :] = resid
        r.acc[part, :] = resid
        hat, _ = norm_parts(resid)
        second = (hat * r.norm[2:3, :] + r.norm[3:4, :]).astype(BF)
        r.x[part, :] = second
        r.second_t[:, part] = second.T
        r.gsec[part, :] = jnp.zeros((tile, D), F32)
        return carry

    gather.relay_x(DOWN)
    lax.fori_loop(0, tiles, feed_first, 0)
    for p in (UPA, UPB, DOWN):
        gather.settle(p)
    gather.finish()
    copies.finish()

    def feed_chunk(f, carry):
        cols = pl.ds(pl.multiple_of(f * CHUNK, CHUNK), CHUNK)

        everything = slice(0, tokens)
        pre = mm(r.x[...], r.fup[:, cols], NN)
        square = pre * pre
        tangent = jnp.tanh(pre * (0.7978845608 + (0.7978845608 * 0.044715) * square))
        upper = 0.5 + 0.5 * tangent
        hidden = pre * upper
        slope = upper + (hidden * (1.0 - tangent)) * (
            0.7978845608 + (0.7978845608 * 3.0 * 0.044715) * square
        )
        hidden = hidden.astype(BF)
        grad_pre = (mm(r.og[...], r.fdown[f], NT) * slope).astype(BF)
        r.hid[everything, :] = hidden
        r.gpre[everything, :] = grad_pre
        r.acc[everything, :] += mm(hidden, r.fdown[f], NN)
        r.gsec[everything, :] += mm(grad_pre, r.fup[:, cols], NT)
        r.fdown[f] = mm(r.og_t[...], r.hid[everything, :], NN).astype(BF)
        r.fup[:, cols] = mm(r.second_t[...], r.gpre[everything, :], NN).astype(BF)
        return carry

    chunks = FF // CHUNK
    lax.fori_loop(0, chunks // 2, feed_chunk, 0)
    for p in reduce.of("first"):
        reduce.start(p)
    lax.fori_loop(chunks // 2, chunks - 1, feed_chunk, 0)
    for p in reduce.of("first"):
        reduce.combine(p)
    lax.fori_loop(chunks - 1, chunks, feed_chunk, 0)
    for p in reduce.of("up", "down"):
        reduce.start(p)
    again = pltpu.make_async_copy(r.x_far, r.x, r.local_sem.at[FETCHES - 1])
    again.start()
    r.grow[...] = jnp.zeros_like(r.grow)

    def feed_last(i, carry):
        part = tile_of(i)
        r.gpre[part, :] = r.acc[part, :].astype(BF)
        hat, inverse = norm_parts(r.ginput[part, :])
        grad = r.gsec[part, :]
        gres = r.og[part, :].astype(F32) + norm_back(grad, hat, inverse, r.norm[2:3, :])
        r.ginput[part, :] = gres
        r.og[part, :] = gres.astype(BF)
        r.grow[2:3, :] += jnp.sum(grad * hat, axis=0, keepdims=True)
        r.grow[3:4, :] += jnp.sum(grad, axis=0, keepdims=True)
        return carry

    lax.fori_loop(0, tiles, feed_last, 0)
    store_out = pltpu.make_async_copy(
        r.gpre.at[0:tokens, :], r.out_far, r.local_sem.at[FETCHES]
    )
    store_out.start()
    for p in reduce.of("first"):
        reduce.second(p)
    for p in reduce.of("up", "down"):
        reduce.combine(p)
    r.gmix[:, 3 * D : 4 * D] = mm(r.mixed[...], r.og[...], TN).astype(BF)
    for p in reduce.of("out"):
        reduce.start(p)

    def mixed_back(i, carry):
        part = tile_of(i)
        r.mixed[part, :] = mm(r.og[part, :], r.fout[...], NT).astype(BF)
        r.og_t[:, part] = r.normed[part, :].T
        return carry

    lax.fori_loop(0, tiles, mixed_back, 0)


    store_out.wait()

    square = jnp.zeros((1, 1), F32)
    backwards = list(range(rows))[::-1]
    for turn, row in enumerate(backwards):
        if turn > 0:
            build_ext(row, local, r.kv, r.coarse, r.edge_near, r.far_all, ext)
        starts = document_bounds(r.seg[row : row + 1, :], seq_len)
        for item in gext:
            item[...] = jnp.zeros_like(item)

        def attend_back(block, carry):
            gather_keys(ext, block, offset, local, r.keys)
            fill_bias(starts, offset + block * QB, seq_len, r.bias)
            part = part_of(row, block)
            both = jnp.concatenate([r.bias[...], r.bias[...]], axis=1)
            def grads(pair):
                return lane_halves(r.mixed[part, lanes_of[pair]])

            for pair in range(PAIRS):
                at = score_at[pair]
                r.acc[at] = mm(r.keys[:, lanes_of[pair]], queries(part, pair), NT) + both
                r.gsec[at] = mm(r.keys[:, vlanes_of[pair]], grads(pair), NT)
            for pair in range(PAIRS):
                at = score_at[pair]
                soft = jnp.exp(r.acc[at] - r.totals[row, block, pair : pair + 1, :])
                gsoft = r.gsec[at]
                row_total = jnp.sum(soft * gsoft, axis=0, keepdims=True)
                r.hid[at] = soft.astype(BF)
                r.gpre[at] = (soft * (gsoft - row_total)).astype(BF)
            for pair in range(PAIRS):
                at = score_at[pair]
                gkeys = mm(r.gpre[at], queries(part, pair), NN)
                gvalues = mm(r.hid[at], grads(pair), NN)
                for lv in range(LEVELS):
                    n, at_key = key_rows(lv), key_start(lv)
                    to = pl.ds(pl.multiple_of(window_start(lv, block, offset, local), 16), n)
                    gext[lv][to, lanes_of[pair]] += gkeys[at_key : at_key + n, :]
                    gext[lv][to, vlanes_of[pair]] += gvalues[at_key : at_key + n, :]
                gq_t = own_halves(mm(r.keys[:, lanes_of[pair]], r.gpre[at], TN)) * DH**-0.5
                r.og[part, lanes_of[pair]] = gq_t.T.astype(BF)
            return carry

        lax.fori_loop(0, half, attend_back, 0)
        if turn == 0:
            for p in reduce.of("out"):
                reduce.combine(p)
            for p in reduce.of("first"):
                reduce.third(p)
            for p in reduce.of("up"):
                reduce.second(p)
        if turn == rows - 1:
            for p in reduce.of("down", "out"):
                reduce.second(p)
            for p in reduce.of("up"):
                reduce.third(p)
        lax.fori_loop(half, blocks, attend_back, 0)
        if turn == 0:
            for p in reduce.of("first"):
                square += reduce.final(p)
                reduce.publish(p)
        r.kv[row] = gext[0][16 : 16 + local, :].astype(BF)
        for lv in edge_levels(local):
            n = local >> lv
            to = slice(16 * lv, 16 * lv + 16)
            if lv > 0:
                at = level_offset(local, lv)
                r.coarse[row, at : at + n, :] = gext[lv][16 : 16 + n, :].astype(BF)
            r.edge_own[row, 0, to, :] = gext[lv][0:16, :].astype(BF)
            r.edge_own[row, 1, to, :] = gext[lv][16 + n : 32 + n, :].astype(BF)
        for owner in range(n_seq):
            pieces = []
            used = 0
            for lv in far_levels(local):
                n = local >> lv
                pieces.append(gext[lv][16 + owner * n : 16 + owner * n + n, :])
                used += n
            pieces.append(jnp.zeros((16 - used, 2 * D), F32))
            r.gfar[row, owner] = jnp.concatenate(pieces, axis=0).astype(BF)
        exchange_back.start(row)


    for p in reduce.of("out"):
        reduce.third(p)
    r.gmix[:, 0:D] = mm(r.og_t[...], r.og[...], NN).astype(BF)
    for p in reduce.of("q"):
        reduce.start(p)
    for p in reduce.of("down"):
        reduce.third(p)
    for p in reduce.of("q"):
        reduce.combine(p)

    def settle_inputs(i):
        part = tile_of(i)
        gnormed = (
            mm(r.og[part, :], r.fqkv[0], NT)
            + mm(r.hid[part, :], r.fqkv[1], NT)
            + mm(r.gpre[part, :], r.fqkv[2], NT)
        )
        hat, inverse = norm_parts(r.x[part, :].astype(F32))
        r.ginput[part, :] += norm_back(gnormed, hat, inverse, r.norm[0:1, :])
        r.grow[0:1, :] += jnp.sum(gnormed * hat, axis=0, keepdims=True)
        r.grow[1:2, :] += jnp.sum(gnormed, axis=0, keepdims=True)
        store = pltpu.make_async_copy(
            r.ginput.at[part, :], r.ginput_far.at[part, :], r.local_sem.at[FETCHES + 4 + i]
        )
        store.start()
        return store

    stores = []
    again.wait()
    spread_of = averaging(local)
    for turn, row in enumerate(backwards):
        exchange_back.arrive(row)
        base = row * local
        for lv in edge_levels(local):
            n = local >> lv
            for way in range(2):
                more = r.edge_back[row, way, 16 * lv : 16 * lv + 16, :].astype(F32)
                low_row = 0 if way == 0 else n - 16
                if lv == 0:
                    sums = r.kv[row, low_row : low_row + 16, :].astype(F32) + more
                    r.kv[row, low_row : low_row + 16, :] = sums.astype(BF)
                else:
                    at = level_offset(local, lv) + low_row
                    sums = r.coarse[row, at : at + 16, :].astype(F32) + more
                    r.coarse[row, at : at + 16, :] = sums.astype(BF)
        total = r.far_back[row, 0].astype(F32)
        for owner in range(1, n_seq):
            total += r.far_back[row, owner].astype(F32)
        r.coarse[row, local - 16 : local, :] = total.astype(BF)
        for at in range(0, local, tile):
            span, where = slice(at, at + tile), slice(base + at, base + at + tile)
            spread = mm(spread_of[:, span], r.coarse[row], TN)
            pair = (r.kv[row, span, :].astype(F32) + spread).astype(BF)
            r.hid[where, :] = pair[:, 0:D]
            r.gpre[where, :] = pair[:, D : 2 * D]
        if turn < rows - 1:
            stores += [settle_inputs(row * row_tiles + i) for i in range(row_tiles)]
    for p in reduce.of("q"):
        reduce.second(p)
    late = reduce.of("kv")
    r.gmix[:, D : 2 * D] = mm(r.og_t[...], r.hid[0:tokens, :], NN).astype(BF)
    if len(late) > 1:
        reduce.start(late[0])
    r.gmix[:, 2 * D : 3 * D] = mm(r.og_t[...], r.gpre[0:tokens, :], NN).astype(BF)
    reduce.start(late[-1])

    stores += [settle_inputs(backwards[-1] * row_tiles + i) for i in range(row_tiles)]
    rows_total = SmallSum(me, copies, r.grow, r.small_seq, r.small_dp, n_dp)
    square_total = SmallSum(me, copies, r.square, r.square_seq, r.square_dp, n_dp + 2)
    for p in late:
        reduce.combine(p)
    rows_total.start()
    for p in reduce.of("q"):
        reduce.third(p)
    for p in late:
        reduce.second(p)
    for p in reduce.of("up"):
        square += reduce.final(p)
        reduce.publish(p)
    for p in late:
        reduce.third(p)
    for p in reduce.of("out", "down"):
        square += reduce.final(p)
        reduce.publish(p)
    rows_total.turn()
    for p in reduce.of("q"):
        square += reduce.final(p)
        reduce.publish(p)
    for p in late:
        square += reduce.final(p)
    r.square[...] = jnp.broadcast_to(square, (8, 128))
    square_total.start()
    for p in late:
        reduce.publish(p)
    square_total.turn()
    r.small[...] = rows_total.finish()
    for p in range(len(reduce.parts)):
        reduce.settle(p)
    for at, name in enumerate(("sup", "smix", "sdown")):
        store = pltpu.make_async_copy(
            getattr(r, name), getattr(r, name + "_far"), r.local_sem.at[FETCHES + 1 + at]
        )
        store.start()
        stores.append(store)
    total = square_total.finish()
    r.small[4:5, 0:128] = total[0:1, :]
    for row in range(rows):
        exchange_back.finish(row)
    for store in stores:
        store.wait()
    copies.finish()


DMA = pltpu.SemaphoreType.DMA


class Shapes:
    def __init__(self, inputs, segment_ids):
        self.n_dp, self.n_seq = lax.axis_size("dp"), lax.axis_size("seq")
        self.rows, self.local = inputs.shape[0], inputs.shape[1]
        self.seq_len = segment_ids.shape[1]
        self.tokens = self.rows * self.local
        self.blocks = self.local // QB
        edge = 16 * len(edge_levels(self.local))
        self.edge = (self.rows, 2, edge, 2 * D)
        self.far = (self.rows, self.n_seq, 16, 2 * D)
        ext = [(ext_rows(self.local, self.seq_len, lv), 2 * D) for lv in range(LEVELS)]
        self.ext_low = [pltpu.VMEM(shape, BF) for shape in ext]
        self.ext_wide = [pltpu.VMEM(shape, F32) for shape in ext]
        self.edge_sems = Exchange.sems(self.rows, self.n_seq)
        self.heads = (self.rows, self.local, D)
        self.parts = len(grad_parts(self.n_dp, self.n_seq))
        self.sems = self.n_dp + 2 * SmallSum.sems
        self.sems += self.parts * Reduce.sems(self.n_dp, self.n_seq)
        self.pairs = (self.rows, self.local, 2 * D)


def run_layer(z, inputs, segment_ids, out_grad, w_qkv, w_out, w_up, w_down, norm_params):
    flat = (z.tokens, D)
    named = layer_scratch(z)
    return pl.pallas_call(
        functools.partial(layer_kernel, z, list(named)),
        out_shape=[
            sds(flat, BF),
            sds(flat, F32),
            sds((D // z.n_dp, FF), BF),
            sds((D // z.n_dp, 4 * D), BF),
            sds((D, FF // z.n_dp), BF),
            sds((8, D), F32),
        ],
        in_specs=[ANY if name.endswith("_far") else VM for name in INPUTS],
        out_specs=[ANY if name.endswith("_far") else VM for name in OUTPUTS],
        scratch_shapes=[
            *named.values(),
            *z.ext_low,
            *z.ext_wide,
            *Reduce.scratch(z.n_dp, z.n_seq),
        ],
        compiler_params=params(0),
        name="layer",
    )(
        inputs.reshape(flat),
        segment_ids,
        out_grad.reshape(flat),
        w_qkv,
        w_out,
        w_up,
        w_down,
        norm_params,
    )


def run_adam(z, sums, masters, firsts, seconds, passed):
    shapes = [sds(w.shape, F32) for w in masters]
    norm_shape = sds(firsts[4].shape, F32)
    steps = 2 if D // z.n_dp % 32 == 0 else 1
    coarse = max(1, steps // (FF // z.n_dp // 128))
    down = max(128, FF // z.n_dp // steps)

    def rows_of(shape):
        if len(shape) == 3:
            return pl.BlockSpec((shape[0], shape[1] // steps, shape[2]), lambda i: (0, i, 0))
        return pl.BlockSpec((shape[0] // steps, shape[1]), lambda i: (i, 0))

    def whole(shape):
        return pl.BlockSpec(shape, lambda i: (0, 0))

    big = [rows_of(w.shape) for w in masters]
    big[3] = pl.BlockSpec((down, D), lambda i: (i // coarse, 0))
    norm_spec = whole(firsts[4].shape)
    down_spec = pl.BlockSpec((D, down), lambda i: (0, i // coarse))
    through = [rows_of(item.shape) for item in passed]
    sums_spec = [rows_of(sums[0].shape), rows_of(sums[1].shape), down_spec, whole((8, D))]
    return pl.pallas_call(
        functools.partial(adam_kernel, z.n_dp),
        grid=(steps,),
        out_shape=shapes
        + [norm_shape]
        + shapes
        + [norm_shape]
        + shapes
        + [norm_shape, sds((1, 1), F32)]
        + [sds(item.shape, item.dtype) for item in passed],
        in_specs=sums_spec + big + big + [norm_spec] + big + [norm_spec] + through,
        out_specs=(big + [norm_spec]) * 3 + [whole((1, 1))] + through,
        compiler_params=params(),
        name="adam",
    )(*sums, *masters, *firsts, *seconds, *passed)


def on_device(
    inputs,
    segment_ids,
    out_grad,
    w_qkv,
    w_out,
    w_up,
    w_down,
    norm_params,
    qkv_first,
    qkv_second,
    out_first,
    out_second,
    up_first,
    up_second,
    down_first,
    down_second,
    norm_first,
    norm_second,
):
    z = Shapes(inputs, segment_ids)
    masters = [w_qkv, w_out, w_up, w_down]
    firsts = [qkv_first, out_first, up_first, down_first, norm_first]
    seconds = [qkv_second, out_second, up_second, down_second, norm_second]
    outputs, input_grad, *sums = run_layer(
        z, inputs, segment_ids, out_grad, *masters, norm_params
    )
    updated = run_adam(z, sums, masters, firsts, seconds, (outputs, input_grad))
    return (
        updated[16].reshape(z.heads),
        updated[17].reshape(z.heads),
        updated[15].reshape(()),
        *updated[0:15],
    )


def solution(mesh):
    tokens = P("dp", "seq", None)
    rows, stack, lanes = P("dp", None), P(None, "dp", None), P(None, "dp")
    moments = (stack, stack, rows, rows, rows, rows, rows, rows, lanes, lanes)
    weights = (stack, rows, rows, rows)
    return jax.shard_map(
        on_device,
        mesh=mesh,
        in_specs=(tokens, rows, tokens, *weights, lanes, *moments),
        out_specs=(tokens, tokens, P(), *weights, lanes, *weights, lanes, *weights, lanes),
        check_vma=False,
    )
```
